32 devices in a mesh: row: 4 (over x, core), th: 2 (over y), ph: 4 (over z).
Axes of the slice: x: 2, y: 2, z: 4, core: 2. Of those that a mesh axis runs over, the one named last changes fastest.
Arguments:
- right_side: float32 [8, 16, 8, 256], P(None, 'ph', 'th', 'row'), may hold values from -14 to 14
- conduct: float32 [8, 16, 8, 256], P(None, 'ph', 'th', 'row'), may hold values from 0.05 to 0.3
- coupling: float32 [8, 8], replicated, may hold values from -0.6 to 0.6
- inverse: bfloat16 [16, 8, 16, 128, 128], P('ph', 'th', 'row'), may hold values from -0.45 to 1.45
- face_codes: int32 [2, 16, 8], P(None, 'ph', 'th'), may hold values from 0 to 2
Outputs:
- correction: float32 [8, 16, 8, 256], P(None, 'ph', 'th', 'row')
- residual: float32 [8, 16, 8, 256], P(None, 'ph', 'th', 'row')
The draws below stay inside these ranges and needn't reach their ends.
Inputs may be any that keep to these rules, and one draw needn't show every extreme that they name: `face_codes`: 0 marks a fixed radial face, 1 an outflow face, 2 a reflecting face.
All inputs are finite; a program needn't handle non-finite values.
Results may differ from the reference program's by a relative error of at most 0.0095.
The reference program's roundings to bfloat16 on the way count: a program that leaves them out, or rounds other values in their place, can miss the bound.
Values sent between devices are 32-bit elements; how exact they have to be, the bound alone decides.
No kernel may reach another device: no remote copies, remote signals or barrier semaphores. Data moves between devices by JAX's collectives and lax.ppermute only.
A program may use at most 64 MiB of HBM per device.

```python
import math
import jax
import jax.numpy as jnp
from jax import lax

VARS = 8
BLK = 16
S = 4
CYCLES = 1
NPH = 16
NTH = 8
NR = 256


def draw_right_side(key, part):
    shape = (VARS, NPH, NTH, NR)
    base = jnp.clip(jax.random.normal(key, shape, jnp.float32), -5.0, 5.0)
    radial = 0.6 + 1.2 * lax.broadcasted_iota(jnp.float32, (1, 1, 1, NR), 3) / NR
    return (base * radial).astype(jnp.float32)


def draw_inverse(key, part):
    order = VARS * BLK
    shape = (NPH, NTH, NR // BLK, order, order)
    key_off = jax.random.fold_in(key, 11)
    key_diag = jax.random.fold_in(key, 12)
    spread = 0.6 / math.sqrt(order)
    offdiag = jnp.clip(jax.random.normal(key_off, shape, jnp.float32) * spread, -4.0 * spread, 4.0 * spread)
    diagonal = jax.random.uniform(key_diag, shape[:-1], jnp.float32, 0.6, 1.4)
    identity = jnp.eye(order, dtype=jnp.float32)
    return (offdiag * (1.0 - identity) + identity * diagonal[..., None]).astype(jnp.bfloat16)


def plant(drawn, rng, least, high):
    dims = drawn.shape
    spot = [jax.random.randint(jax.random.fold_in(rng, axis), (), 0, dims[axis]) for axis in range(len(dims))]
    drawn = drawn.at[tuple(spot)].set(least)
    longest = dims.index(max(dims))
    spot[longest] = (spot[longest] + 1) % dims[longest]
    return drawn.at[tuple(spot)].set(high)


def level_of(rng, extent, cuts, low, largest):
    loudness = 1.0
    for dim, blocks in cuts:
        draws = jax.random.uniform(jax.random.fold_in(jax.random.fold_in(rng, 6), dim), (blocks,), jnp.float32, low / len(cuts), largest / len(cuts))
        loudness = loudness * jnp.repeat(jnp.exp(draws), extent[dim] // blocks).reshape((-1,) + (1,) * (len(extent) - 1 - dim))
    return loudness


def bell_draw(rng, dims, scale, bound, kind=jnp.bfloat16):
    array = scale * jax.random.normal(rng, dims, jnp.float32)
    return jnp.clip(array, min=-bound, max=bound).astype(kind)


def setup_inputs(seed: int = 0) -> dict:
    key_list = jax.random.split(jax.random.key(seed), 6)
    right_side = draw_right_side(jax.random.fold_in(key_list[5], 71), 0)
    conduct = jnp.clip(jnp.exp(math.log(0.3) - 1.7917595 * jax.random.uniform(key_list[1], (VARS, NPH, NTH, NR), jnp.float32) ** level_of(key_list[1], (VARS, NPH, NTH, NR), ((1, 4), (2, 2), (3, 4)), -0.2, 0.2)), 0.05, 0.3)
    coupling = bell_draw(key_list[2], (VARS, VARS), 0.15, 0.6, jnp.float32)
    inverse = draw_inverse(jax.random.fold_in(key_list[5], 71), 0)
    face_codes = plant(jax.random.randint(key_list[4], (2, NPH, NTH), 0, 3), jax.random.fold_in(key_list[4], 1), 0, 2).astype(jnp.int32)
    return {"right_side": right_side, "conduct": conduct, "coupling": coupling, "inverse": inverse, "face_codes": face_codes}


def face_factor(codes):
    return (codes == 1).astype(jnp.float32) - (codes == 2).astype(jnp.float32)

def operate(field, conduct, coupling, face_codes):
    inner_ghost = face_factor(face_codes[0])[None] * field[..., 0]
    outer_ghost = face_factor(face_codes[1])[None] * field[..., -1]
    radial_sum = jnp.concatenate([inner_ghost[..., None], field[..., :-1]], 3) + jnp.concatenate([field[..., 1:], outer_ghost[..., None]], 3)
    zero_rim = jnp.zeros_like(field[:, :, :1])
    polar_sum = jnp.concatenate([zero_rim, field[:, :, :-1]], 2) + jnp.concatenate([field[:, :, 1:], zero_rim], 2)
    azimuth_sum = jnp.roll(field, 1, 1) + jnp.roll(field, -1, 1)
    mixed = jnp.einsum('kj,jpqr->kpqr', coupling, field, precision=lax.Precision.HIGHEST)
    return field + mixed + conduct * (6.0 * field - radial_sum - polar_sum - azimuth_sum)

def precondition(field, inverse):
    nblocks = NR // BLK
    rounded = field.astype(jnp.bfloat16)
    blocked = rounded.reshape(VARS, NPH, NTH, nblocks, BLK).transpose(1, 2, 3, 0, 4).reshape(NPH, NTH, nblocks, VARS * BLK)

    def one_slice(pair):
        matrices, vectors = pair
        return jnp.einsum('qbij,qbj->qbi', matrices.astype(jnp.float32), vectors.astype(jnp.float32), precision=lax.Precision.HIGHEST)
    result = lax.map(one_slice, (inverse, blocked))
    return result.reshape(NPH, NTH, nblocks, VARS, BLK).transpose(3, 0, 1, 2, 4).reshape(VARS, NPH, NTH, NR)

def solve_small(upper_factor):
    matrix = upper_factor[:, :S] + upper_factor[:, 1:]
    target = upper_factor[:, 0]
    normal = jnp.dot(matrix.T, matrix, precision=lax.Precision.HIGHEST)
    moment = jnp.dot(matrix.T, target, precision=lax.Precision.HIGHEST)
    lower = jnp.linalg.cholesky(normal)
    forward = []
    for target_row in range(S):
        summed = moment[target_row]
        for source_row in range(target_row):
            summed = summed - lower[target_row, source_row] * forward[source_row]
        forward.append(summed / lower[target_row, target_row])
    backward = [None] * S
    for target_row in reversed(range(S)):
        summed = forward[target_row]
        for source_row in range(target_row + 1, S):
            summed = summed - lower[source_row, target_row] * backward[source_row]
        backward[target_row] = summed / lower[target_row, target_row]
    return backward

def reference(right_side, conduct, coupling, inverse, face_codes):
    correction = jnp.zeros_like(right_side)
    residual = right_side
    for restart in range(CYCLES):
        krylov = [residual]
        directions = []
        for column in range(S):
            smoothed = precondition(krylov[column], inverse)
            directions.append(smoothed)
            krylov.append(operate(smoothed, conduct, coupling, face_codes) - krylov[column])
        flat = jnp.stack(krylov).reshape(S + 1, -1)
        products = jnp.dot(flat, flat.T, precision=lax.Precision.HIGHEST)
        upper_factor = jnp.linalg.cholesky(products).T
        weights = solve_small(upper_factor)
        residual = krylov[0]
        for column in range(S):
            correction = correction + weights[column] * directions[column]
            residual = residual - weights[column] * (krylov[column + 1] + krylov[column])
    return (correction, residual)
```

```python
import functools

import jax
import jax.numpy as jnp
from jax import lax
from jax.experimental import pallas as pl
from jax.experimental.pallas import tpu as pltpu
from jax.sharding import PartitionSpec as P

VARS = 8
BLK = 16
S = 4
LANES = VARS * BLK
GROUP = 8
VMEM_LIMIT = 24 * 1024 * 1024


def pairs_low(count):
    return [(i, i ^ 1) for i in range(count)]


def pairs_high(count):
    return [(i, (i + 1) % count if i % 2 else (i - 1) % count) for i in range(count)]


def to_rows(field):
    var, ph, th, radial = field.shape
    split = field.reshape(var, ph, th, radial // BLK, BLK).transpose(3, 1, 2, 0, 4)
    return split.reshape(-1, var * BLK)


def from_rows(rows, shape):
    var, ph, th, radial = shape
    split = rows.reshape(radial // BLK, ph, th, var, BLK).transpose(3, 1, 2, 0, 4)
    return split.reshape(shape)


def apply_blocks(field, inverse_ref, ph, th):
    rounded = field.astype(jnp.bfloat16)
    across = 2 * GROUP
    row = lax.broadcasted_iota(jnp.int32, (across, LANES), 0) % GROUP
    parts = []
    for first in range(0, field.shape[0], across):
        vectors = rounded[first : first + across]
        spread = jnp.concatenate(
            [jnp.where(row == m, vectors, jnp.zeros_like(vectors)) for m in range(GROUP)], axis=1
        )
        halves = []
        for half in range(2):
            blocks = []
            for m in range(GROUP):
                index = first + half * GROUP + m
                b, place = divmod(index, ph * th)
                p, t = divmod(place, th)
                blocks.append(inverse_ref[p, t, b])
            halves.append(jnp.concatenate(blocks, axis=1))
        matrix = jnp.concatenate(halves, axis=0)
        out = lax.dot_general(
            spread, matrix, (((1,), (1,)), ((), ())), preferred_element_type=jnp.float32
        )
        parts += [out[:GROUP, :LANES], out[GROUP:, LANES:]]
    return jnp.concatenate(parts, axis=0)


def pack_faces(field, d_ref, out_refs, flags_ref, ph, th):
    ph_a, ph_b, row_a, row_b, th_a, th_b = out_refs
    rows = field.shape[0]
    per = ph * th
    nb = rows // per
    cell = lax.broadcasted_iota(jnp.int32, (per, LANES), 1) % BLK
    odd_ph, odd_row, odd_th = flags_ref[0] == 1, flags_ref[1] == 1, flags_ref[2] == 1
    low = jnp.concatenate([field[b * per : b * per + th] for b in range(nb)], axis=0)
    high = jnp.concatenate([field[(b + 1) * per - th : (b + 1) * per] for b in range(nb)], axis=0)
    ph_a[...] = jnp.where(odd_ph, low, high)
    ph_b[...] = jnp.where(odd_ph, high, low)
    low = jnp.where(cell == BLK - 1, pltpu.roll(field[:per], BLK - 1, 1), 0.0)
    high = jnp.where(cell == 0, pltpu.roll(field[rows - per :], LANES - BLK + 1, 1), 0.0)
    row_a[...] = jnp.where(odd_row, low, high)
    if row_b is not None:
        row_b[...] = jnp.where(odd_row, high, low)
    low = d_ref[pl.ds(0, rows // th, stride=th), :]
    high = d_ref[pl.ds(th - 1, rows // th, stride=th), :]
    th_a[...] = jnp.where(odd_th, low, high)
    if th_b is not None:
        th_b[...] = jnp.where(odd_th, high, low)


def local_part(field, d_ref, krylov, conduct, diagonal, mixing_ref, ph, th):
    rows = field.shape[0]
    per = ph * th
    lane = lax.broadcasted_iota(jnp.int32, (rows, LANES), 1)
    row = lax.broadcasted_iota(jnp.int32, (rows, LANES), 0)
    cell = lane % BLK
    polar = row % th
    azimuth = (row // th) % ph
    mixed = field * mixing_ref[0:1, :]
    for m in range(1, VARS):
        mixed += pltpu.roll(field, LANES - BLK * m, 1) * mixing_ref[m : m + 1, :]
    zero = jnp.zeros((per, LANES), jnp.float32)
    from_low = pltpu.roll(field, LANES - BLK + 1, 1)
    from_low = jnp.concatenate([zero, from_low[: rows - per]], axis=0)
    from_high = pltpu.roll(field, BLK - 1, 1)
    from_high = jnp.concatenate([from_high[per:], zero], axis=0)
    total = jnp.where(cell == 0, from_low, pltpu.roll(field, 1, 1))
    total += jnp.where(cell == BLK - 1, from_high, pltpu.roll(field, LANES - 1, 1))
    total += jnp.where(polar == 0, 0.0, pltpu.roll(field, 1, 0))
    total += jnp.where(polar == th - 1, 0.0, pltpu.roll(field, rows - 1, 0))
    total += jnp.where(azimuth == 0, 0.0, pltpu.roll(field, th, 0))
    total += jnp.where(azimuth == ph - 1, 0.0, pltpu.roll(field, rows - th, 0))
    return field + mixed + conduct * (diagonal * field - total) - krylov


def add_faces(halo_ref, in_refs, flags_ref, ph, th):
    ph_a, ph_b, row_a, row_b, th_a, th_b = in_refs
    rows = halo_ref.shape[0]
    per = ph * th
    nb = rows // per
    odd_ph, odd_row, odd_th = flags_ref[0] == 1, flags_ref[1] == 1, flags_ref[2] == 1
    halo_ref[...] = jnp.zeros_like(halo_ref)

    def sides(odd, a, b, has_low, has_high):
        first = a[...]
        second = jnp.zeros_like(first) if b is None else b[...]
        low = jnp.where(odd, first, second)
        high = jnp.where(odd, second, first)
        if has_low is not None:
            low = jnp.where(has_low, low, 0.0)
            high = jnp.where(has_high, high, 0.0)
        return low, high

    low, high = sides(odd_ph, ph_a, ph_b, None, None)
    for b in range(nb):
        halo_ref[b * per : b * per + th, :] += low[b * th : (b + 1) * th]
        halo_ref[(b + 1) * per - th : (b + 1) * per, :] += high[b * th : (b + 1) * th]
    low, high = sides(odd_row, row_a, row_b, flags_ref[3] == 1, flags_ref[4] == 1)
    halo_ref[:per, :] += low
    halo_ref[rows - per :, :] += high
    low, high = sides(odd_th, th_a, th_b, flags_ref[5] == 1, flags_ref[6] == 1)
    halo_ref[pl.ds(0, rows // th, stride=th), :] += low
    halo_ref[pl.ds(th - 1, rows // th, stride=th), :] += high
    return halo_ref[...]


def fill(refs, present):
    refs = iter(refs)
    return [next(refs) if there else None for there in present]


def first_kernel(ph, th, present, flags_ref, krylov_ref, inverse_ref, d_ref, *faces):
    direction = apply_blocks(krylov_ref[...], inverse_ref, ph, th)
    d_ref[...] = direction
    pack_faces(direction, d_ref, fill(faces, present), flags_ref, ph, th)


def step_kernel(ph, th, present, flags_ref, krylov_ref, last_ref, conduct_ref, diagonal_ref, mixing_ref, inverse_ref, *rest):
    n = sum(present)
    in_faces, (next_ref, d_ref), out_faces, (halo_ref,) = rest[:n], rest[n : n + 2], rest[n + 2 : 2 * n + 2], rest[2 * n + 2 :]
    conduct = conduct_ref[...]
    local = local_part(last_ref[...], last_ref, krylov_ref[...], conduct, diagonal_ref[...], mixing_ref, ph, th)
    halo = add_faces(halo_ref, fill(in_faces, present), flags_ref, ph, th)
    krylov = local - conduct * halo
    next_ref[...] = krylov
    direction = apply_blocks(krylov, inverse_ref, ph, th)
    d_ref[...] = direction
    pack_faces(direction, d_ref, fill(out_faces, present), flags_ref, ph, th)


def last_kernel(ph, th, present, flags_ref, krylov_ref, last_ref, conduct_ref, diagonal_ref, mixing_ref, *rest):
    n = sum(present)
    older, in_faces, (next_ref, gram_ref), (halo_ref,) = rest[: S - 1], rest[S - 1 : S - 1 + n], rest[S - 1 + n : S + 1 + n], rest[S + 1 + n :]
    conduct = conduct_ref[...]
    newest = krylov_ref[...]
    local = local_part(last_ref[...], last_ref, newest, conduct, diagonal_ref[...], mixing_ref, ph, th)
    halo = add_faces(halo_ref, fill(in_faces, present), flags_ref, ph, th)
    final = local - conduct * halo
    next_ref[...] = final
    basis = [ref[...] for ref in older] + [newest, final]
    sums = []
    for i in range(S + 1):
        for j in range(i + 1):
            product = basis[i] * basis[j]
            sums.append(jnp.sum(product, axis=0, keepdims=True))
    sums += [jnp.zeros_like(sums[0])] * (-len(sums) % 8)
    stacked = jnp.concatenate(sums, axis=0)
    each = jnp.sum(stacked, axis=1, keepdims=True)
    lane = lax.broadcasted_iota(jnp.int32, stacked.shape, 1)
    row = lax.broadcasted_iota(jnp.int32, stacked.shape, 0)
    line = jnp.sum(jnp.where(lane == row, each, 0.0), axis=0, keepdims=True)
    gram_ref[...] = jnp.broadcast_to(line, gram_ref.shape)


def cholesky(matrix, order):
    lower = [[None] * order for _ in range(order)]
    for j in range(order):
        summed = matrix[j][j]
        for k in range(j):
            summed = summed - lower[j][k] * lower[j][k]
        lower[j][j] = jnp.sqrt(summed)
        for i in range(j + 1, order):
            summed = matrix[i][j]
            for k in range(j):
                summed = summed - lower[i][k] * lower[j][k]
            lower[i][j] = summed / lower[j][j]
    return lower


def small_solve(products):
    factor = cholesky(products, S + 1)
    upper = [[factor[j][i] if i <= j else None for j in range(S + 1)] for i in range(S + 1)]

    def plus(a, b):
        return b if a is None else a if b is None else a + b

    hess = [[plus(upper[i][j], upper[i][j + 1]) for j in range(S)] for i in range(S + 1)]

    def dot(j, k):
        total = None
        for i in range(S + 1):
            if hess[i][j] is not None and hess[i][k] is not None:
                total = plus(total, hess[i][j] * hess[i][k])
        return total

    normal = [[dot(j, k) for k in range(j + 1)] for j in range(S)]
    moment = [hess[0][j] * upper[0][0] for j in range(S)]
    lower = cholesky(normal, S)
    forward = []
    for i in range(S):
        summed = moment[i]
        for k in range(i):
            summed = summed - lower[i][k] * forward[k]
        forward.append(summed / lower[i][i])
    weights = [None] * S
    for i in reversed(range(S)):
        summed = forward[i]
        for k in range(i + 1, S):
            summed = summed - lower[k][i] * weights[k]
        weights[i] = summed / lower[i][i]
    return weights


def combine_kernel(gram_ref, *refs):
    krylov, directions, (correction_ref, residual_ref) = refs[: S + 1], refs[S + 1 : 2 * S + 1], refs[2 * S + 1 :]
    line = jnp.sum(gram_ref[...], axis=0, keepdims=True)
    products, place = [], 0
    for i in range(S + 1):
        products.append([])
        for j in range(i + 1):
            products[i].append(line[:, place : place + 1])
            place += 1
    weights = small_solve(products)
    basis = [ref[...] for ref in krylov]
    correction = jnp.zeros_like(basis[0])
    residual = basis[0]
    for j in range(S):
        correction = correction + weights[j] * directions[j][...]
        residual = residual - weights[j] * (basis[j + 1] + basis[j])
    correction_ref[...] = correction
    residual_ref[...] = residual


def call(kernel, outs, scratch, *args):
    specs = [
        pl.BlockSpec(memory_space=pltpu.SMEM if a.dtype == jnp.int32 else pltpu.VMEM) for a in args
    ]
    return pl.pallas_call(
        kernel,
        out_shape=outs,
        in_specs=specs,
        out_specs=[pl.BlockSpec(memory_space=pltpu.VMEM)] * len(outs),
        scratch_shapes=scratch,
        compiler_params=pltpu.CompilerParams(vmem_limit_bytes=VMEM_LIMIT),
    )(*args)


def local(right_side, conduct, coupling, inverse, face_codes):
    _, ph, th, radial = right_side.shape
    nb = radial // BLK
    per = ph * th
    rows = per * nb
    at = {axis: (lax.axis_index(axis), lax.axis_size(axis)) for axis in ("row", "th", "ph")}
    (row_at, row_n), (th_at, th_n), (ph_at, ph_n) = at["row"], at["th"], at["ph"]
    present = (True, True, True, row_n > 2, True, th_n > 2)
    flags = jnp.stack(
        [ph_at % 2, row_at % 2, th_at % 2, row_at > 0, row_at < row_n - 1, th_at > 0, th_at < th_n - 1]
    ).astype(jnp.int32)

    factor = (face_codes == 1).astype(jnp.float32) - (face_codes == 2).astype(jnp.float32)
    factor = factor.reshape(2, 1, per, 1)
    block = lax.broadcasted_iota(jnp.int32, (nb, per, LANES), 0)
    cell = lax.broadcasted_iota(jnp.int32, (nb, per, LANES), 2) % BLK
    ghost = jnp.where((block == 0) & (cell == 0) & (row_at == 0), factor[0], 0.0)
    ghost += jnp.where((block == nb - 1) & (cell == BLK - 1) & (row_at == row_n - 1), factor[1], 0.0)
    diagonal = (6.0 - ghost).reshape(rows, LANES)
    mixing = jnp.stack([jnp.diagonal(jnp.roll(coupling, -m, 1)) for m in range(VARS)])
    mixing = jnp.repeat(mixing, BLK, axis=1)
    conducts = to_rows(conduct)

    def shape(n):
        return jax.ShapeDtypeStruct((n, LANES), jnp.float32)

    face_rows = (nb * th, nb * th, per, per, rows // th, rows // th)
    faces = [shape(n) for n, there in zip(face_rows, present) if there]
    whole = shape(rows)

    def exchange(sent):
        plan = (("ph", pairs_low), ("ph", pairs_high), ("row", pairs_low), ("row", pairs_high), ("th", pairs_low), ("th", pairs_high))
        plan = [p for p, there in zip(plan, present) if there]
        taken = [None] * len(plan)
        order = sorted(range(len(plan)), key=lambda i: (plan[i][0] != "ph", plan[i][0] != "th", plan[i][1] is pairs_low))
        for i in order:
            axis, pairs = plan[i]
            taken[i] = lax.ppermute(sent[i], axis, pairs(lax.axis_size(axis)))
        return taken

    krylov = [to_rows(right_side)]
    direction, *sent = call(
        functools.partial(first_kernel, ph, th, present), [whole] + faces, [], flags, krylov[0], inverse
    )
    directions = [direction]
    halo = [pltpu.VMEM((rows, LANES), jnp.float32)]
    for _ in range(S - 1):
        taken = exchange(sent)
        following, direction, *sent = call(
            functools.partial(step_kernel, ph, th, present),
            [whole, whole] + faces,
            halo,
            flags, krylov[-1], directions[-1], conducts, diagonal, mixing, inverse, *taken,
        )
        krylov.append(following)
        directions.append(direction)
    taken = exchange(sent)
    devices = row_n * th_n * ph_n
    following, gram = call(
        functools.partial(last_kernel, ph, th, present),
        [whole, shape(devices)],
        halo,
        flags, krylov[-1], directions[-1], conducts, diagonal, mixing, *krylov[:-1], *taken,
    )
    krylov.append(following)
    gram = lax.all_to_all(gram, ("row", "th", "ph"), 0, 0, tiled=True)
    correction, residual = call(combine_kernel, [whole, whole], [], gram, *krylov, *directions)
    return from_rows(correction, right_side.shape), from_rows(residual, right_side.shape)


def solution(mesh):
    placed = (
        P(None, "ph", "th", "row"),
        P(None, "ph", "th", "row"),
        P(),
        P("ph", "th", "row", None, None),
        P(None, "ph", "th"),
    )
    return jax.shard_map(
        local,
        mesh=mesh,
        in_specs=placed,
        out_specs=(P(None, "ph", "th", "row"), P(None, "ph", "th", "row")),
        check_vma=False,
    )
```

```python
import functools

import jax
import jax.numpy as jnp
from jax import lax
from jax.experimental import pallas as pl
from jax.experimental.pallas import tpu as pltpu
from jax.sharding import PartitionSpec as P

VARS = 8
BLK = 16
S = 4
LANES = VARS * BLK
GROUP = 8
VMEM_LIMIT = 24 * 1024 * 1024


def pairs_low(count):
    return [(i, i ^ 1) for i in range(count)]


def pairs_high(count):
    return [(i, (i + 1) % count if i % 2 else (i - 1) % count) for i in range(count)]


def to_rows(native_ref):
    var, ph, th, radial = native_ref.shape
    planes = [
        jnp.concatenate([native_ref[v, p] for p in range(ph)], axis=0) for v in range(var)
    ]
    return jnp.concatenate(
        [
            jnp.concatenate([plane[:, r : r + BLK] for plane in planes], axis=1)
            for r in range(0, radial, BLK)
        ],
        axis=0,
    )


def from_rows(rows, native_ref):
    var, ph, th, radial = native_ref.shape
    per = ph * th
    for v in range(var):
        plane = jnp.concatenate(
            [rows[b * per : (b + 1) * per, v * BLK : (v + 1) * BLK] for b in range(radial // BLK)], axis=1
        )
        for p in range(ph):
            native_ref[v, p] = plane[p * th : (p + 1) * th]


def apply_blocks(vectors, turned_ref, first):
    rounded = vectors.astype(jnp.bfloat16)
    row = lax.broadcasted_iota(jnp.int32, rounded.shape, 0) % GROUP
    spread = jnp.concatenate(
        [jnp.where(row == m, rounded, jnp.zeros_like(rounded)) for m in range(GROUP)], axis=1
    )
    halves = [
        jnp.concatenate([turned_ref[first + half * GROUP + m] for m in range(GROUP)], axis=0) for half in range(2)
    ]
    out = jnp.dot(spread, jnp.concatenate(halves, axis=1), preferred_element_type=jnp.float32)
    return jnp.concatenate([out[:GROUP, :LANES], out[GROUP:, LANES:]], axis=0)


def apply_all(field, turned_ref):
    return jnp.concatenate(
        [apply_blocks(field[i : i + 2 * GROUP], turned_ref, i) for i in range(0, field.shape[0], 2 * GROUP)], axis=0
    )


def pack_faces(field, d_ref, out_refs, flags_ref, ph, th):
    ph_a, ph_b, row_a, row_b, th_a, th_b = out_refs
    rows = field.shape[0]
    per = ph * th
    nb = rows // per
    cell = lax.broadcasted_iota(jnp.int32, (per, LANES), 1) % BLK
    odd_ph, odd_row, odd_th = flags_ref[0] == 1, flags_ref[1] == 1, flags_ref[2] == 1
    low = jnp.concatenate([field[b * per : b * per + th] for b in range(nb)], axis=0)
    high = jnp.concatenate([field[(b + 1) * per - th : (b + 1) * per] for b in range(nb)], axis=0)
    ph_a[...] = jnp.where(odd_ph, low, high)
    ph_b[...] = jnp.where(odd_ph, high, low)
    low = jnp.where(cell == BLK - 1, pltpu.roll(field[:per], BLK - 1, 1), 0.0)
    high = jnp.where(cell == 0, pltpu.roll(field[rows - per :], LANES - BLK + 1, 1), 0.0)
    row_a[...] = jnp.where(odd_row, low, high)
    if row_b is not None:
        row_b[...] = jnp.where(odd_row, high, low)
    low = d_ref[pl.ds(0, rows // th, stride=th), :]
    high = d_ref[pl.ds(th - 1, rows // th, stride=th), :]
    th_a[...] = jnp.where(odd_th, low, high)
    if th_b is not None:
        th_b[...] = jnp.where(odd_th, high, low)


def local_part(field, d_ref, krylov, conduct, diagonal, mixing_ref, ph, th):
    rows = field.shape[0]
    per = ph * th
    lane = lax.broadcasted_iota(jnp.int32, (rows, LANES), 1)
    row = lax.broadcasted_iota(jnp.int32, (rows, LANES), 0)
    cell = lane % BLK
    polar = row % th
    azimuth = (row // th) % ph
    mixed = field * mixing_ref[0:1, :]
    for m in range(1, VARS):
        mixed += pltpu.roll(field, LANES - BLK * m, 1) * mixing_ref[m : m + 1, :]
    zero = jnp.zeros((per, LANES), jnp.float32)
    from_low = pltpu.roll(field, LANES - BLK + 1, 1)
    from_low = jnp.concatenate([zero, from_low[: rows - per]], axis=0)
    from_high = pltpu.roll(field, BLK - 1, 1)
    from_high = jnp.concatenate([from_high[per:], zero], axis=0)
    total = jnp.where(cell == 0, from_low, pltpu.roll(field, 1, 1))
    total += jnp.where(cell == BLK - 1, from_high, pltpu.roll(field, LANES - 1, 1))
    total += jnp.where(polar == 0, 0.0, pltpu.roll(field, 1, 0))
    total += jnp.where(polar == th - 1, 0.0, pltpu.roll(field, rows - 1, 0))
    total += jnp.where(azimuth == 0, 0.0, pltpu.roll(field, th, 0))
    total += jnp.where(azimuth == ph - 1, 0.0, pltpu.roll(field, rows - th, 0))
    return field + mixed + conduct * (diagonal * field - total) - krylov


def add_faces(halo_ref, in_refs, flags_ref, ph, th):
    ph_a, ph_b, row_a, row_b, th_a, th_b = in_refs
    rows = halo_ref.shape[0]
    per = ph * th
    nb = rows // per
    odd_ph, odd_row, odd_th = flags_ref[0] == 1, flags_ref[1] == 1, flags_ref[2] == 1
    halo_ref[...] = jnp.zeros_like(halo_ref)

    def sides(odd, a, b, has_low, has_high):
        first = a[...]
        second = jnp.zeros_like(first) if b is None else b[...]
        low = jnp.where(odd, first, second)
        high = jnp.where(odd, second, first)
        if has_low is not None:
            low = jnp.where(has_low, low, 0.0)
            high = jnp.where(has_high, high, 0.0)
        return low, high

    low, high = sides(odd_ph, ph_a, ph_b, None, None)
    for b in range(nb):
        halo_ref[b * per : b * per + th, :] += low[b * th : (b + 1) * th]
        halo_ref[(b + 1) * per - th : (b + 1) * per, :] += high[b * th : (b + 1) * th]
    low, high = sides(odd_row, row_a, row_b, flags_ref[3] == 1, flags_ref[4] == 1)
    halo_ref[:per, :] += low
    halo_ref[rows - per :, :] += high
    low, high = sides(odd_th, th_a, th_b, flags_ref[5] == 1, flags_ref[6] == 1)
    halo_ref[pl.ds(0, rows // th, stride=th), :] += low
    halo_ref[pl.ds(th - 1, rows // th, stride=th), :] += high
    return halo_ref[...]


def fill(refs, present):
    refs = iter(refs)
    return [next(refs) if there else None for there in present]


def first_kernel(ph, th, present, flags_ref, right_ref, conduct_ref, coupling_ref, codes_ref, inverse_ref, *rest):
    n = sum(present)
    krylov_ref, conducts_ref, diagonal_ref, mixing_ref, turned_ref, d_ref = rest[:6]
    faces = fill(rest[6 : 6 + n], present)
    right, conduct, coupling, codes, blocks, sems = rest[6 + n :]
    per = ph * th
    rows = d_ref.shape[0]
    nb = rows // per
    pairs = [(right_ref, right), (coupling_ref, coupling), (codes_ref, codes)]
    pairs += [(inverse_ref.at[:, :, b], blocks.at[b]) for b in range(nb)] + [(conduct_ref, conduct)]
    copies = [pltpu.make_async_copy(a, b, sems.at[i]) for i, (a, b) in enumerate(pairs)]
    for copy in copies:
        copy.start()

    copies[0].wait()
    krylov = to_rows(right)
    krylov_ref[...] = krylov
    copies[1].wait()
    lane = lax.broadcasted_iota(jnp.int32, (1, LANES), 1)
    for m in range(VARS):
        line = jnp.zeros((1, LANES), jnp.float32)
        for k in range(VARS):
            line = jnp.where(lane // BLK == k, coupling[k, (k + m) % VARS], line)
        mixing_ref[m : m + 1, :] = line
    copies[2].wait()
    cell = lax.broadcasted_iota(jnp.int32, (per, LANES), 1) % BLK
    row = lax.broadcasted_iota(jnp.int32, (per, LANES), 0)
    diagonal_ref[...] = jnp.full_like(diagonal_ref, 6.0)
    for side, (edge, first, has) in enumerate(((0, 0, flags_ref[3]), (BLK - 1, rows - per, flags_ref[4]))):
        factor = jnp.zeros((per, LANES), jnp.float32)
        for i in range(per):
            code = codes[side, i // th, i % th]
            value = jnp.where(code == 1, 1.0, jnp.where(code == 2, -1.0, 0.0))
            factor = jnp.where(row == i, value, factor)
        factor = jnp.where((cell == edge) & (has == 0), factor, 0.0)
        diagonal_ref[first : first + per, :] -= factor
    for b in range(nb):
        copies[3 + b].wait()
        for i in range(per):
            turned_ref[b * per + i] = blocks[b, i // th, i % th].T
        for i in range(b * per, (b + 1) * per, 2 * GROUP):
            d_ref[i : i + 2 * GROUP, :] = apply_blocks(krylov[i : i + 2 * GROUP], turned_ref, i)
    pack_faces(d_ref[...], d_ref, faces, flags_ref, ph, th)
    copies[3 + nb].wait()
    conducts_ref[...] = to_rows(conduct)


def local_kernel(ph, th, krylov_ref, last_ref, conduct_ref, diagonal_ref, mixing_ref, out_ref):
    out_ref[...] = local_part(
        last_ref[...], last_ref, krylov_ref[...], conduct_ref[...], diagonal_ref[...], mixing_ref, ph, th
    )


def gram_rows(left, right):
    lines = [jnp.sum(a * b, axis=0, keepdims=True) for a, b in zip(left, right)]
    return lines + [jnp.zeros_like(lines[0])] * (-len(lines) % 8)


def gram_kernel(*refs):
    basis = [ref[...] for ref in refs[:-1]]
    left = [basis[i] for i in range(S) for _ in range(i + 1)]
    right = [basis[j] for i in range(S) for j in range(i + 1)]
    refs[-1][...] = jnp.concatenate(gram_rows(left, right), axis=0)


def step_kernel(ph, th, present, flags_ref, local_ref, conduct_ref, turned_ref, *rest):
    n = sum(present)
    in_faces, (next_ref, d_ref), out_faces, (halo_ref,) = rest[:n], rest[n : n + 2], rest[n + 2 : 2 * n + 2], rest[2 * n + 2 :]
    halo = add_faces(halo_ref, fill(in_faces, present), flags_ref, ph, th)
    krylov = local_ref[...] - conduct_ref[...] * halo
    next_ref[...] = krylov
    direction = apply_all(krylov, turned_ref)
    d_ref[...] = direction
    pack_faces(direction, d_ref, fill(out_faces, present), flags_ref, ph, th)


def last_kernel(ph, th, present, flags_ref, local_ref, conduct_ref, partial_ref, *rest):
    n = sum(present)
    older, in_faces, (next_ref, gram_ref), (halo_ref,) = rest[:S], rest[S : S + n], rest[S + n : S + 2 + n], rest[S + 2 + n :]
    halo = add_faces(halo_ref, fill(in_faces, present), flags_ref, ph, th)
    final = local_ref[...] - conduct_ref[...] * halo
    next_ref[...] = final
    basis = [ref[...] for ref in older] + [final]
    stacked = jnp.concatenate([partial_ref[...]] + gram_rows([final] * (S + 1), basis), axis=0)
    each = jnp.sum(stacked, axis=1, keepdims=True)
    lane = lax.broadcasted_iota(jnp.int32, stacked.shape, 1)
    row = lax.broadcasted_iota(jnp.int32, stacked.shape, 0)
    line = jnp.sum(jnp.where(lane == row, each, 0.0), axis=0, keepdims=True)
    gram_ref[...] = jnp.broadcast_to(line, gram_ref.shape)


def cholesky(matrix, order):
    lower = [[None] * order for _ in range(order)]
    for j in range(order):
        summed = matrix[j][j]
        for k in range(j):
            summed = summed - lower[j][k] * lower[j][k]
        lower[j][j] = jnp.sqrt(summed)
        for i in range(j + 1, order):
            summed = matrix[i][j]
            for k in range(j):
                summed = summed - lower[i][k] * lower[j][k]
            lower[i][j] = summed / lower[j][j]
    return lower


def small_solve(products):
    factor = cholesky(products, S + 1)
    upper = [[factor[j][i] if i <= j else None for j in range(S + 1)] for i in range(S + 1)]

    def plus(a, b):
        return b if a is None else a if b is None else a + b

    hess = [[plus(upper[i][j], upper[i][j + 1]) for j in range(S)] for i in range(S + 1)]

    def dot(j, k):
        total = None
        for i in range(S + 1):
            if hess[i][j] is not None and hess[i][k] is not None:
                total = plus(total, hess[i][j] * hess[i][k])
        return total

    normal = [[dot(j, k) for k in range(j + 1)] for j in range(S)]
    moment = [hess[0][j] * upper[0][0] for j in range(S)]
    lower = cholesky(normal, S)
    forward = []
    for i in range(S):
        summed = moment[i]
        for k in range(i):
            summed = summed - lower[i][k] * forward[k]
        forward.append(summed / lower[i][i])
    weights = [None] * S
    for i in reversed(range(S)):
        summed = forward[i]
        for k in range(i + 1, S):
            summed = summed - lower[k][i] * weights[k]
        weights[i] = summed / lower[i][i]
    return weights


def combine_kernel(partial_rows, gram_ref, *refs):
    krylov, directions, rest = refs[: S + 1], refs[S + 1 : 2 * S + 1], refs[2 * S + 1 :]
    correction_ref, residual_ref, correction, residual, sems = rest
    line = jnp.sum(gram_ref[...], axis=0, keepdims=True)
    products, place = [], 0
    for i in range(S + 1):
        products.append([])
        place = partial_rows if i == S else place
        for j in range(i + 1):
            products[i].append(line[:, place : place + 1])
            place += 1
    weights = small_solve(products)
    total = weights[0] * directions[0][...]
    for j in range(1, S):
        total = total + weights[j] * directions[j][...]
    from_rows(total, correction)
    first = pltpu.make_async_copy(correction, correction_ref, sems.at[0])
    first.start()
    basis = [ref[...] for ref in krylov]
    total = basis[0]
    for j in range(S):
        total = total - weights[j] * (basis[j + 1] + basis[j])
    from_rows(total, residual)
    second = pltpu.make_async_copy(residual, residual_ref, sems.at[1])
    second.start()
    first.wait()
    second.wait()


def call(kernel, outs, scratch, *args, stay=False):
    def space(a):
        if a.dtype == jnp.int32 and a.ndim == 1:
            return pltpu.SMEM
        return pltpu.HBM if stay and (a.ndim > 3 or a.shape[-1] != LANES) else pltpu.VMEM

    placed = [pltpu.with_memory_space_constraint(a, pltpu.HBM) if space(a) == pltpu.HBM else a for a in args]
    return pl.pallas_call(
        kernel,
        out_shape=outs,
        in_specs=[pl.BlockSpec(memory_space=space(a)) for a in args],
        out_specs=[pl.BlockSpec(memory_space=space(a)) for a in outs],
        scratch_shapes=scratch,
        compiler_params=pltpu.CompilerParams(vmem_limit_bytes=VMEM_LIMIT),
    )(*placed)


def local(right_side, conduct, coupling, inverse, face_codes):
    _, ph, th, radial = right_side.shape
    nb = radial // BLK
    per = ph * th
    rows = per * nb
    at = {axis: (lax.axis_index(axis), lax.axis_size(axis)) for axis in ("row", "th", "ph")}
    (row_at, row_n), (th_at, th_n), (ph_at, ph_n) = at["row"], at["th"], at["ph"]
    present = (True, True, True, row_n > 2, True, th_n > 2)
    flags = jnp.stack(
        [ph_at % 2, row_at % 2, th_at % 2, row_at > 0, row_at < row_n - 1, th_at > 0, th_at < th_n - 1]
    ).astype(jnp.int32)

    def shape(n):
        return jax.ShapeDtypeStruct((n, LANES), jnp.float32)

    face_rows = (nb * th, nb * th, per, per, rows // th, rows // th)
    faces = [shape(n) for n, there in zip(face_rows, present) if there]
    whole = shape(rows)

    def exchange(sent):
        plan = (("ph", pairs_low), ("ph", pairs_high), ("row", pairs_low), ("row", pairs_high), ("th", pairs_low), ("th", pairs_high))
        plan = [p for p, there in zip(plan, present) if there]
        taken = [None] * len(plan)
        order = sorted(range(len(plan)), key=lambda i: (plan[i][0] != "ph", plan[i][0] != "th", plan[i][1] is pairs_low))
        for i in order:
            axis, pairs = plan[i]
            taken[i] = lax.ppermute(sent[i], axis, pairs(lax.axis_size(axis)))
        return taken

    field = pltpu.VMEM(right_side.shape, jnp.float32)
    start, conducts, diagonal, mixing, turned, direction, *sent = call(
        functools.partial(first_kernel, ph, th, present),
        [whole, whole, whole, shape(VARS), jax.ShapeDtypeStruct((rows, LANES, LANES), jnp.bfloat16), whole] + faces,
        [
            field,
            field,
            pltpu.SMEM(coupling.shape, jnp.float32),
            pltpu.SMEM(face_codes.shape, jnp.int32),
            pltpu.VMEM((nb, ph, th, LANES, LANES), jnp.bfloat16),
            pltpu.SemaphoreType.DMA((nb + 4,)),
        ],
        flags, right_side, conduct, coupling, face_codes, inverse,
        stay=True,
    )
    krylov, directions = [start], [direction]
    halo = [pltpu.VMEM((rows, LANES), jnp.float32)]
    for step in range(S):
        taken = exchange(sent)
        (beside,) = call(
            functools.partial(local_kernel, ph, th), [whole], [], krylov[-1], directions[-1], conducts, diagonal, mixing
        )
        if step < S - 1:
            following, direction, *sent = call(
                functools.partial(step_kernel, ph, th, present),
                [whole, whole] + faces,
                halo,
                flags, beside, conducts, turned, *taken,
            )
            krylov.append(following)
            directions.append(direction)
    partial_rows = S * (S + 1) // 2
    partial_rows += -partial_rows % 8
    (partial,) = call(gram_kernel, [shape(partial_rows)], [], *krylov)
    following, gram = call(
        functools.partial(last_kernel, ph, th, present),
        [whole, shape(row_n * th_n * ph_n)],
        halo,
        flags, beside, conducts, partial, *krylov, *taken,
    )
    krylov.append(following)
    gram = lax.all_to_all(gram, ("row", "th", "ph"), 0, 0, tiled=True)
    native = jax.ShapeDtypeStruct(right_side.shape, jnp.float32)
    return tuple(
        call(
            functools.partial(combine_kernel, partial_rows),
            [native, native],
            [field, field, pltpu.SemaphoreType.DMA((2,))],
            gram, *krylov, *directions,
            stay=True,
        )
    )


def solution(mesh):
    placed = (
        P(None, "ph", "th", "row"),
        P(None, "ph", "th", "row"),
        P(),
        P("ph", "th", "row", None, None),
        P(None, "ph", "th"),
    )
    return jax.shard_map(
        local,
        mesh=mesh,
        in_specs=placed,
        out_specs=(P(None, "ph", "th", "row"), P(None, "ph", "th", "row")),
        check_vma=False,
    )
```

```python
import functools

import jax
import jax.numpy as jnp
from jax import lax
from jax.experimental import pallas as pl
from jax.experimental.pallas import tpu as pltpu
from jax.sharding import PartitionSpec as P

VARS = 8
BLK = 16
S = 4
LANES = VARS * BLK
GROUP = 8
VMEM_LIMIT = 24 * 1024 * 1024


def pairs_low(count):
    return [(i, i ^ 1) for i in range(count)]


def pairs_high(count):
    return [(i, (i + 1) % count if i % 2 else (i - 1) % count) for i in range(count)]


def to_rows(native_ref):
    var, ph, th, radial = native_ref.shape
    planes = [
        jnp.concatenate([native_ref[v, p] for p in range(ph)], axis=0) for v in range(var)
    ]
    return jnp.concatenate(
        [
            jnp.concatenate([plane[:, r : r + BLK] for plane in planes], axis=1)
            for r in range(0, radial, BLK)
        ],
        axis=0,
    )


def from_rows(rows, native_ref):
    var, ph, th, radial = native_ref.shape
    per = ph * th
    for v in range(var):
        plane = jnp.concatenate(
            [rows[b * per : (b + 1) * per, v * BLK : (v + 1) * BLK] for b in range(radial // BLK)], axis=1
        )
        for p in range(ph):
            native_ref[v, p] = plane[p * th : (p + 1) * th]


def apply_blocks(vectors, turned_ref, first):
    rounded = vectors.astype(jnp.bfloat16)
    row = lax.broadcasted_iota(jnp.int32, rounded.shape, 0) % GROUP
    spread = jnp.concatenate(
        [jnp.where(row == m, rounded, jnp.zeros_like(rounded)) for m in range(GROUP)], axis=1
    )
    halves = [
        jnp.concatenate([turned_ref[first + half * GROUP + m] for m in range(GROUP)], axis=0) for half in range(2)
    ]
    out = jnp.dot(spread, jnp.concatenate(halves, axis=1), preferred_element_type=jnp.float32)
    return jnp.concatenate([out[:GROUP, :LANES], out[GROUP:, LANES:]], axis=0)


def apply_all(field, turned_ref):
    return jnp.concatenate(
        [apply_blocks(field[i : i + 2 * GROUP], turned_ref, i) for i in range(0, field.shape[0], 2 * GROUP)], axis=0
    )


def pack_faces(field, d_ref, outs, flags_ref, ph, th):
    rows = field.shape[0]
    per = ph * th
    nb = rows // per
    cell = lax.broadcasted_iota(jnp.int32, (per, LANES), 1) % BLK
    odd_ph, odd_row, odd_th = flags_ref[0:1, :] > 0.5, flags_ref[1:2, :] > 0.5, flags_ref[2:3, :] > 0.5
    low = jnp.concatenate([field[b * per : b * per + th] for b in range(nb)], axis=0)
    high = jnp.concatenate([field[(b + 1) * per - th : (b + 1) * per] for b in range(nb)], axis=0)
    outs["ph_high"][...] = jnp.where(odd_ph, high, low)
    outs["ph_low"][...] = jnp.where(odd_ph, low, high)
    low = jnp.where(cell == BLK - 1, pltpu.roll(field[:per], BLK - 1, 1), 0.0)
    high = jnp.where(cell == 0, pltpu.roll(field[rows - per :], LANES - BLK + 1, 1), 0.0)
    outs["row_low"][...] = jnp.where(odd_row, low, high)
    if "row_high" in outs:
        outs["row_high"][...] = jnp.where(odd_row, high, low)
    low = d_ref[pl.ds(0, rows // th, stride=th), :]
    high = d_ref[pl.ds(th - 1, rows // th, stride=th), :]
    outs["th_low"][...] = jnp.where(odd_th, low, high)
    if "th_high" in outs:
        outs["th_high"][...] = jnp.where(odd_th, high, low)


def local_part(field, d_ref, krylov, conduct, diagonal, mixing_ref, ph, th):
    rows = field.shape[0]
    per = ph * th
    lane = lax.broadcasted_iota(jnp.int32, (rows, LANES), 1)
    row = lax.broadcasted_iota(jnp.int32, (rows, LANES), 0)
    cell = lane % BLK
    polar = row % th
    azimuth = (row // th) % ph
    mixed = field * mixing_ref[0:1, :]
    for m in range(1, VARS):
        mixed += pltpu.roll(field, LANES - BLK * m, 1) * mixing_ref[m : m + 1, :]
    zero = jnp.zeros((per, LANES), jnp.float32)
    from_low = pltpu.roll(field, LANES - BLK + 1, 1)
    from_low = jnp.concatenate([zero, from_low[: rows - per]], axis=0)
    from_high = pltpu.roll(field, BLK - 1, 1)
    from_high = jnp.concatenate([from_high[per:], zero], axis=0)
    total = jnp.where(cell == 0, from_low, pltpu.roll(field, 1, 1))
    total += jnp.where(cell == BLK - 1, from_high, pltpu.roll(field, LANES - 1, 1))
    total += jnp.where(polar == 0, 0.0, pltpu.roll(field, 1, 0))
    total += jnp.where(polar == th - 1, 0.0, pltpu.roll(field, rows - 1, 0))
    total += jnp.where(azimuth == 0, 0.0, pltpu.roll(field, th, 0))
    total += jnp.where(azimuth == ph - 1, 0.0, pltpu.roll(field, rows - th, 0))
    return field + mixed + conduct * (diagonal * field - total) - krylov


def add_faces(halo_ref, taken, flags_ref, ph, th):
    rows = halo_ref.shape[0]
    per = ph * th
    nb = rows // per
    flag = [flags_ref[i : i + 1, :] > 0.5 for i in range(7)]
    halo_ref[...] = jnp.zeros_like(halo_ref)

    def sides(axis, odd, has_low=None, has_high=None):
        first = taken[axis + "_low"][...]
        second = taken[axis + "_high"][...] if axis + "_high" in taken else jnp.zeros_like(first)
        low, high = jnp.where(odd, first, second), jnp.where(odd, second, first)
        if has_low is None:
            return low, high
        return jnp.where(has_low, low, 0.0), jnp.where(has_high, high, 0.0)

    low, high = sides("ph", flag[0])
    for b in range(nb):
        halo_ref[b * per : b * per + th, :] += low[b * th : (b + 1) * th]
        halo_ref[(b + 1) * per - th : (b + 1) * per, :] += high[b * th : (b + 1) * th]
    low, high = sides("row", flag[1], flag[3], flag[4])
    halo_ref[:per, :] += low
    halo_ref[rows - per :, :] += high
    low, high = sides("th", flag[2], flag[5], flag[6])
    halo_ref[pl.ds(0, rows // th, stride=th), :] += low
    halo_ref[pl.ds(th - 1, rows // th, stride=th), :] += high
    return halo_ref[...]


def first_kernel(ph, th, names, flags_ref, right_ref, conduct_ref, coupling_ref, codes_ref, inverse_ref, *rest):
    n = len(names)
    krylov_ref, conducts_ref, diagonal_ref, mixing_ref, turned_ref, d_ref = rest[:6]
    faces = dict(zip(names, rest[6 : 6 + n]))
    right, conduct, coupling, codes, blocks, sems = rest[6 + n :]
    per = ph * th
    rows = d_ref.shape[0]
    nb = rows // per
    pairs = [(right_ref, right), (coupling_ref, coupling), (codes_ref, codes)]
    pairs += [(inverse_ref.at[:, :, b], blocks.at[b]) for b in range(nb)] + [(conduct_ref, conduct)]
    copies = [pltpu.make_async_copy(a, b, sems.at[i]) for i, (a, b) in enumerate(pairs)]
    for copy in copies:
        copy.start()

    copies[0].wait()
    krylov = to_rows(right)
    krylov_ref[...] = krylov
    copies[1].wait()
    lane = lax.broadcasted_iota(jnp.int32, (1, LANES), 1)
    for m in range(VARS):
        line = jnp.zeros((1, LANES), jnp.float32)
        for k in range(VARS):
            line = jnp.where(lane // BLK == k, coupling[k, (k + m) % VARS], line)
        mixing_ref[m : m + 1, :] = line
    copies[2].wait()
    cell = lax.broadcasted_iota(jnp.int32, (per, LANES), 1) % BLK
    row = lax.broadcasted_iota(jnp.int32, (per, LANES), 0)
    diagonal_ref[...] = jnp.full_like(diagonal_ref, 6.0)
    for side, (edge, first, has) in enumerate(((0, 0, 3), (BLK - 1, rows - per, 4))):
        factor = jnp.zeros((per, LANES), jnp.float32)
        for i in range(per):
            code = codes[side, i // th, i % th]
            value = jnp.where(code == 1, 1.0, jnp.where(code == 2, -1.0, 0.0))
            factor = jnp.where(row == i, value, factor)
        factor = jnp.where((cell == edge) & (flags_ref[has : has + 1, :] < 0.5), factor, 0.0)
        diagonal_ref[first : first + per, :] -= factor
    for b in range(nb):
        copies[3 + b].wait()
        for i in range(per):
            turned_ref[b * per + i] = blocks[b, i // th, i % th].T
        for i in range(b * per, (b + 1) * per, 2 * GROUP):
            d_ref[i : i + 2 * GROUP, :] = apply_blocks(krylov[i : i + 2 * GROUP], turned_ref, i)
    pack_faces(d_ref[...], d_ref, faces, flags_ref, ph, th)
    copies[3 + nb].wait()
    conducts_ref[...] = to_rows(conduct)


def local_kernel(ph, th, krylov_ref, last_ref, conduct_ref, diagonal_ref, mixing_ref, out_ref):
    out_ref[...] = local_part(
        last_ref[...], last_ref, krylov_ref[...], conduct_ref[...], diagonal_ref[...], mixing_ref, ph, th
    )


def gram_rows(left, right):
    lines = [jnp.sum(a * b, axis=0, keepdims=True) for a, b in zip(left, right)]
    return lines + [jnp.zeros_like(lines[0])] * (-len(lines) % 8)


def gram_kernel(*refs):
    basis = [ref[...] for ref in refs[:-1]]
    left = [basis[i] for i in range(S) for _ in range(i + 1)]
    right = [basis[j] for i in range(S) for j in range(i + 1)]
    refs[-1][...] = jnp.concatenate(gram_rows(left, right), axis=0)


def step_kernel(ph, th, names, flags_ref, local_ref, conduct_ref, turned_ref, *rest):
    n = len(names)
    next_ref, d_ref, *sent, halo_ref = rest[n:]
    halo = add_faces(halo_ref, dict(zip(names, rest)), flags_ref, ph, th)
    krylov = local_ref[...] - conduct_ref[...] * halo
    next_ref[...] = krylov
    direction = apply_all(krylov, turned_ref)
    d_ref[...] = direction
    pack_faces(direction, d_ref, dict(zip(names, sent)), flags_ref, ph, th)


def last_kernel(ph, th, names, flags_ref, local_ref, conduct_ref, partial_ref, *rest):
    older, taken, (next_ref, gram_ref, halo_ref) = rest[:S], rest[S : S + len(names)], rest[S + len(names) :]
    halo = add_faces(halo_ref, dict(zip(names, taken)), flags_ref, ph, th)
    final = local_ref[...] - conduct_ref[...] * halo
    next_ref[...] = final
    basis = [ref[...] for ref in older] + [final]
    stacked = jnp.concatenate([partial_ref[...]] + gram_rows([final] * (S + 1), basis), axis=0)
    each = jnp.sum(stacked, axis=1, keepdims=True)
    lane = lax.broadcasted_iota(jnp.int32, stacked.shape, 1)
    row = lax.broadcasted_iota(jnp.int32, stacked.shape, 0)
    line = jnp.sum(jnp.where(lane == row, each, 0.0), axis=0, keepdims=True)
    gram_ref[...] = jnp.broadcast_to(line, gram_ref.shape)


def cholesky(matrix, order):
    lower = [[None] * order for _ in range(order)]
    for j in range(order):
        summed = matrix[j][j]
        for k in range(j):
            summed = summed - lower[j][k] * lower[j][k]
        lower[j][j] = jnp.sqrt(summed)
        for i in range(j + 1, order):
            summed = matrix[i][j]
            for k in range(j):
                summed = summed - lower[i][k] * lower[j][k]
            lower[i][j] = summed / lower[j][j]
    return lower


def small_solve(products):
    factor = cholesky(products, S + 1)
    upper = [[factor[j][i] if i <= j else None for j in range(S + 1)] for i in range(S + 1)]

    def plus(a, b):
        return b if a is None else a if b is None else a + b

    hess = [[plus(upper[i][j], upper[i][j + 1]) for j in range(S)] for i in range(S + 1)]

    def dot(j, k):
        total = None
        for i in range(S + 1):
            if hess[i][j] is not None and hess[i][k] is not None:
                total = plus(total, hess[i][j] * hess[i][k])
        return total

    normal = [[dot(j, k) for k in range(j + 1)] for j in range(S)]
    moment = [hess[0][j] * upper[0][0] for j in range(S)]
    lower = cholesky(normal, S)
    forward = []
    for i in range(S):
        summed = moment[i]
        for k in range(i):
            summed = summed - lower[i][k] * forward[k]
        forward.append(summed / lower[i][i])
    weights = [None] * S
    for i in reversed(range(S)):
        summed = forward[i]
        for k in range(i + 1, S):
            summed = summed - lower[k][i] * weights[k]
        weights[i] = summed / lower[i][i]
    return weights


def combine_kernel(partial_rows, gram_ref, *refs):
    krylov, directions, rest = refs[: S + 1], refs[S + 1 : 2 * S + 1], refs[2 * S + 1 :]
    correction_ref, residual_ref, correction, residual, sems = rest
    line = jnp.sum(gram_ref[...], axis=0, keepdims=True)
    products, place = [], 0
    for i in range(S + 1):
        products.append([])
        place = partial_rows if i == S else place
        for j in range(i + 1):
            products[i].append(line[:, place : place + 1])
            place += 1
    weights = small_solve(products)
    total = weights[0] * directions[0][...]
    for j in range(1, S):
        total = total + weights[j] * directions[j][...]
    from_rows(total, correction)
    first = pltpu.make_async_copy(correction, correction_ref, sems.at[0])
    first.start()
    basis = [ref[...] for ref in krylov]
    total = basis[0]
    for j in range(S):
        total = total - weights[j] * (basis[j + 1] + basis[j])
    from_rows(total, residual)
    second = pltpu.make_async_copy(residual, residual_ref, sems.at[1])
    second.start()
    first.wait()
    second.wait()


def call(kernel, outs, scratch, *args, stay=False):
    def space(a):
        return pltpu.HBM if stay and (a.ndim > 3 or a.shape[-1] != LANES) else pltpu.VMEM

    placed = [pltpu.with_memory_space_constraint(a, pltpu.HBM) if space(a) == pltpu.HBM else a for a in args]
    return pl.pallas_call(
        kernel,
        out_shape=outs,
        in_specs=[pl.BlockSpec(memory_space=space(a)) for a in args],
        out_specs=[pl.BlockSpec(memory_space=space(a)) for a in outs],
        scratch_shapes=scratch,
        compiler_params=pltpu.CompilerParams(vmem_limit_bytes=VMEM_LIMIT),
    )(*placed)


def local(right_side, conduct, coupling, inverse, face_codes):
    _, ph, th, radial = right_side.shape
    nb = radial // BLK
    per = ph * th
    rows = per * nb
    at = {axis: (lax.axis_index(axis), lax.axis_size(axis)) for axis in ("row", "th", "ph")}
    (row_at, row_n), (th_at, th_n), (ph_at, ph_n) = at["row"], at["th"], at["ph"]
    face_rows = {"ph_high": nb * th, "row_high": per, "ph_low": nb * th, "th_high": rows // th, "th_low": rows // th, "row_low": per}
    if row_n == 2:
        face_rows.pop("row_high")
    if th_n == 2:
        face_rows.pop("th_high")
    names = tuple(face_rows)
    flags = jnp.stack(
        [ph_at % 2, row_at % 2, th_at % 2, row_at > 0, row_at < row_n - 1, th_at > 0, th_at < th_n - 1, 0]
    ).astype(jnp.float32)
    flags = jnp.broadcast_to(flags[:, None], (flags.shape[0], LANES))

    def shape(n):
        return jax.ShapeDtypeStruct((n, LANES), jnp.float32)

    faces = [shape(n) for n in face_rows.values()]
    whole = shape(rows)

    plans = {"low": pairs_low, "high": pairs_high}

    def exchange(sent):
        taken = []
        for name, array in zip(names, sent):
            axis, side = name.split("_")
            taken.append(lax.ppermute(array, axis, plans[side](lax.axis_size(axis))))
        return taken

    field = pltpu.VMEM(right_side.shape, jnp.float32)
    start, conducts, diagonal, mixing, turned, direction, *sent = call(
        functools.partial(first_kernel, ph, th, names),
        [whole, whole, whole, shape(VARS), jax.ShapeDtypeStruct((rows, LANES, LANES), jnp.bfloat16), whole] + faces,
        [
            field,
            field,
            pltpu.SMEM(coupling.shape, jnp.float32),
            pltpu.SMEM(face_codes.shape, jnp.int32),
            pltpu.VMEM((nb, ph, th, LANES, LANES), jnp.bfloat16),
            pltpu.SemaphoreType.DMA((nb + 4,)),
        ],
        flags, right_side, conduct, coupling, face_codes, inverse,
        stay=True,
    )
    krylov, directions = [start], [direction]
    halo = [pltpu.VMEM((rows, LANES), jnp.float32)]
    for step in range(S):
        taken = exchange(sent)
        (beside,) = call(
            functools.partial(local_kernel, ph, th), [whole], [], krylov[-1], directions[-1], conducts, diagonal, mixing
        )
        if step < S - 1:
            following, direction, *sent = call(
                functools.partial(step_kernel, ph, th, names),
                [whole, whole] + faces,
                halo,
                flags, beside, conducts, turned, *taken,
            )
            krylov.append(following)
            directions.append(direction)
    partial_rows = S * (S + 1) // 2
    partial_rows += -partial_rows % 8
    (partial,) = call(gram_kernel, [shape(partial_rows)], [], *krylov)
    following, gram = call(
        functools.partial(last_kernel, ph, th, names),
        [whole, shape(row_n * th_n * ph_n)],
        halo,
        flags, beside, conducts, partial, *krylov, *taken,
    )
    krylov.append(following)
    gram = lax.all_to_all(gram, ("row", "th", "ph"), 0, 0, tiled=True)
    native = jax.ShapeDtypeStruct(right_side.shape, jnp.float32)
    return tuple(
        call(
            functools.partial(combine_kernel, partial_rows),
            [native, native],
            [field, field, pltpu.SemaphoreType.DMA((2,))],
            gram, *krylov, *directions,
            stay=True,
        )
    )


def solution(mesh):
    placed = (
        P(None, "ph", "th", "row"),
        P(None, "ph", "th", "row"),
        P(),
        P("ph", "th", "row", None, None),
        P(None, "ph", "th"),
    )
    return jax.shard_map(
        local,
        mesh=mesh,
        in_specs=placed,
        out_specs=(P(None, "ph", "th", "row"), P(None, "ph", "th", "row")),
        check_vma=False,
    )
```

```python
import functools

import jax
import jax.numpy as jnp
from jax import lax
from jax.experimental import pallas as pl
from jax.experimental.pallas import tpu as pltpu
from jax.sharding import PartitionSpec as P

VARS = 8
BLK = 16
S = 4
LANES = VARS * BLK
GROUP = 8
VMEM_LIMIT = 24 * 1024 * 1024


def pairs_low(count):
    return [(i, i ^ 1) for i in range(count)]


def pairs_high(count):
    return [(i, (i + 1) % count if i % 2 else (i - 1) % count) for i in range(count)]


def to_rows(native_ref):
    var, ph, th, radial = native_ref.shape
    planes = [
        jnp.concatenate([native_ref[v, p] for p in range(ph)], axis=0) for v in range(var)
    ]
    return jnp.concatenate(
        [
            jnp.concatenate([plane[:, r : r + BLK] for plane in planes], axis=1)
            for r in range(0, radial, BLK)
        ],
        axis=0,
    )


def from_rows(rows, native_ref):
    var, ph, th, radial = native_ref.shape
    per = ph * th
    for v in range(var):
        plane = jnp.concatenate(
            [rows[b * per : (b + 1) * per, v * BLK : (v + 1) * BLK] for b in range(radial // BLK)], axis=1
        )
        for p in range(ph):
            native_ref[v, p] = plane[p * th : (p + 1) * th]


def spread_rows(vectors):
    rounded = vectors.astype(jnp.bfloat16)
    row = lax.broadcasted_iota(jnp.int32, rounded.shape, 0) % GROUP
    return jnp.concatenate(
        [jnp.where(row == m, rounded, jnp.zeros_like(rounded)) for m in range(GROUP)], axis=1
    )


def own_halves(out):
    return jnp.concatenate([out[:GROUP, :LANES], out[GROUP:, LANES:]], axis=0)


def apply_stored(vectors, blocks):
    halves = [jnp.concatenate(blocks[half * GROUP : (half + 1) * GROUP], axis=1) for half in range(2)]
    out = lax.dot_general(
        spread_rows(vectors),
        jnp.concatenate(halves, axis=0),
        (((1,), (1,)), ((), ())),
        preferred_element_type=jnp.float32,
    )
    return own_halves(out)


def apply_turned(field, turned_ref):
    parts = []
    for first in range(0, field.shape[0], 2 * GROUP):
        halves = [
            jnp.concatenate([turned_ref[first + half * GROUP + m] for m in range(GROUP)], axis=0) for half in range(2)
        ]
        out = jnp.dot(
            spread_rows(field[first : first + 2 * GROUP]),
            jnp.concatenate(halves, axis=1),
            preferred_element_type=jnp.float32,
        )
        parts.append(own_halves(out))
    return jnp.concatenate(parts, axis=0)


def pack_faces(field, d_ref, outs, flags_ref, ph, th):
    rows = field.shape[0]
    per = ph * th
    nb = rows // per
    cell = lax.broadcasted_iota(jnp.int32, (per, LANES), 1) % BLK
    odd_ph, odd_row, odd_th = flags_ref[0:1, :] > 0.5, flags_ref[1:2, :] > 0.5, flags_ref[2:3, :] > 0.5
    low = jnp.concatenate([field[b * per : b * per + th] for b in range(nb)], axis=0)
    high = jnp.concatenate([field[(b + 1) * per - th : (b + 1) * per] for b in range(nb)], axis=0)
    outs["ph_high"][...] = jnp.where(odd_ph, high, low)
    outs["ph_low"][...] = jnp.where(odd_ph, low, high)
    low = jnp.where(cell == BLK - 1, pltpu.roll(field[:per], BLK - 1, 1), 0.0)
    high = jnp.where(cell == 0, pltpu.roll(field[rows - per :], LANES - BLK + 1, 1), 0.0)
    outs["row_low"][...] = jnp.where(odd_row, low, high)
    if "row_high" in outs:
        outs["row_high"][...] = jnp.where(odd_row, high, low)
    low = d_ref[pl.ds(0, rows // th, stride=th), :]
    high = d_ref[pl.ds(th - 1, rows // th, stride=th), :]
    outs["th_low"][...] = jnp.where(odd_th, low, high)
    if "th_high" in outs:
        outs["th_high"][...] = jnp.where(odd_th, high, low)


def local_part(field, d_ref, krylov, conduct, diagonal, mixing_ref, ph, th):
    rows = field.shape[0]
    per = ph * th
    lane = lax.broadcasted_iota(jnp.int32, (rows, LANES), 1)
    row = lax.broadcasted_iota(jnp.int32, (rows, LANES), 0)
    cell = lane % BLK
    polar = row % th
    azimuth = (row // th) % ph
    mixed = field * mixing_ref[0:1, :]
    for m in range(1, VARS):
        mixed += pltpu.roll(field, LANES - BLK * m, 1) * mixing_ref[m : m + 1, :]
    zero = jnp.zeros((per, LANES), jnp.float32)
    from_low = pltpu.roll(field, LANES - BLK + 1, 1)
    from_low = jnp.concatenate([zero, from_low[: rows - per]], axis=0)
    from_high = pltpu.roll(field, BLK - 1, 1)
    from_high = jnp.concatenate([from_high[per:], zero], axis=0)
    total = jnp.where(cell == 0, from_low, pltpu.roll(field, 1, 1))
    total += jnp.where(cell == BLK - 1, from_high, pltpu.roll(field, LANES - 1, 1))
    total += jnp.where(polar == 0, 0.0, pltpu.roll(field, 1, 0))
    total += jnp.where(polar == th - 1, 0.0, pltpu.roll(field, rows - 1, 0))
    total += jnp.where(azimuth == 0, 0.0, pltpu.roll(field, th, 0))
    total += jnp.where(azimuth == ph - 1, 0.0, pltpu.roll(field, rows - th, 0))
    return field + mixed + conduct * (diagonal * field - total) - krylov


def add_faces(halo_ref, taken, flags_ref, ph, th):
    rows = halo_ref.shape[0]
    per = ph * th
    nb = rows // per
    flag = [flags_ref[i : i + 1, :] > 0.5 for i in range(7)]
    halo_ref[...] = jnp.zeros_like(halo_ref)

    def sides(axis, odd, has_low=None, has_high=None):
        first = taken[axis + "_low"][...]
        second = taken[axis + "_high"][...] if axis + "_high" in taken else jnp.zeros_like(first)
        low, high = jnp.where(odd, first, second), jnp.where(odd, second, first)
        if has_low is None:
            return low, high
        return jnp.where(has_low, low, 0.0), jnp.where(has_high, high, 0.0)

    low, high = sides("ph", flag[0])
    for b in range(nb):
        halo_ref[b * per : b * per + th, :] += low[b * th : (b + 1) * th]
        halo_ref[(b + 1) * per - th : (b + 1) * per, :] += high[b * th : (b + 1) * th]
    low, high = sides("row", flag[1], flag[3], flag[4])
    halo_ref[:per, :] += low
    halo_ref[rows - per :, :] += high
    low, high = sides("th", flag[2], flag[5], flag[6])
    halo_ref[pl.ds(0, rows // th, stride=th), :] += low
    halo_ref[pl.ds(th - 1, rows // th, stride=th), :] += high
    return halo_ref[...]


def first_kernel(ph, th, names, sizes, right_ref, conduct_ref, coupling_ref, codes_ref, inverse_ref, *rest):
    flags_ref, krylov_ref, conducts_ref, diagonal_ref, mixing_ref, held_ref, d_ref, *sent = rest[: 7 + len(names)]
    right, conduct, coupling, codes, sems = rest[7 + len(names) :]
    per = ph * th
    rows = d_ref.shape[0]
    pairs = [(right_ref, right), (coupling_ref, coupling), (codes_ref, codes), (conduct_ref, conduct)]
    pairs += [(inverse_ref, held_ref)]
    copies = [pltpu.make_async_copy(a, b, sems.at[i]) for i, (a, b) in enumerate(pairs)]
    for copy in copies:
        copy.start()

    def mix():
        copies[1].wait()
        lane = lax.broadcasted_iota(jnp.int32, (1, LANES), 1)
        for m in range(VARS):
            line = jnp.zeros((1, LANES), jnp.float32)
            for k in range(VARS):
                line = jnp.where(lane // BLK == k, coupling[k, (k + m) % VARS], line)
            mixing_ref[m : m + 1, :] = line

    def ghosts():
        copies[2].wait()
        cell = lax.broadcasted_iota(jnp.int32, (per, LANES), 1) % BLK
        row = lax.broadcasted_iota(jnp.int32, (per, LANES), 0)
        diagonal_ref[...] = jnp.full_like(diagonal_ref, 6.0)
        for side, (edge, first, has) in enumerate(((0, 0, 3), (BLK - 1, rows - per, 4))):
            factor = jnp.zeros((per, LANES), jnp.float32)
            for i in range(per):
                code = codes[side, i // th, i % th]
                value = jnp.where(code == 1, 1.0, jnp.where(code == 2, -1.0, 0.0))
                factor = jnp.where(row == i, value, factor)
            factor = jnp.where((cell == edge) & (flags_ref[has : has + 1, :] < 0.5), factor, 0.0)
            diagonal_ref[first : first + per, :] -= factor

    def lay_out():
        copies[3].wait()
        conducts_ref[...] = to_rows(conduct)

    (row_at, row_n), (th_at, th_n), (ph_at, ph_n) = [(lax.axis_index(axis), n) for axis, n in sizes]
    values = [ph_at % 2, row_at % 2, th_at % 2, row_at > 0, row_at < row_n - 1, th_at > 0, th_at < th_n - 1]
    for i, value in enumerate(values):
        flags_ref[i : i + 1, :] = jnp.full((1, LANES), value.astype(jnp.float32))
    copies[0].wait()
    krylov_ref[...] = to_rows(right)
    mix()
    ghosts()
    lay_out()
    copies[4].wait()
    for first in range(0, rows, 2 * GROUP):
        blocks = [held_ref[i % per // th, i % th, i // per] for i in range(first, first + 2 * GROUP)]
        d_ref[first : first + 2 * GROUP, :] = apply_stored(krylov_ref[first : first + 2 * GROUP, :], blocks)
    pack_faces(d_ref[...], d_ref, dict(zip(names, sent)), flags_ref, ph, th)


def turn_kernel(held_ref, turned_ref):
    ph, th = held_ref.shape[:2]
    for i in range(turned_ref.shape[0]):
        b, place = divmod(i, ph * th)
        turned_ref[i] = held_ref[place // th, place % th, b].T


def local_kernel(ph, th, krylov_ref, last_ref, conduct_ref, diagonal_ref, mixing_ref, out_ref):
    out_ref[...] = local_part(
        last_ref[...], last_ref, krylov_ref[...], conduct_ref[...], diagonal_ref[...], mixing_ref, ph, th
    )


def gram_rows(left, right):
    lines = [jnp.sum(a * b, axis=0, keepdims=True) for a, b in zip(left, right)]
    return lines + [jnp.zeros_like(lines[0])] * (-len(lines) % 8)


def gram_kernel(*refs):
    basis = [ref[...] for ref in refs[:-1]]
    left = [basis[i] for i in range(S) for _ in range(i + 1)]
    right = [basis[j] for i in range(S) for j in range(i + 1)]
    refs[-1][...] = jnp.concatenate(gram_rows(left, right), axis=0)


def step_kernel(ph, th, names, flags_ref, local_ref, conduct_ref, turned_ref, *rest):
    n = len(names)
    next_ref, d_ref, *sent, halo_ref = rest[n:]
    halo = add_faces(halo_ref, dict(zip(names, rest)), flags_ref, ph, th)
    krylov = local_ref[...] - conduct_ref[...] * halo
    next_ref[...] = krylov
    direction = apply_turned(krylov, turned_ref)
    d_ref[...] = direction
    pack_faces(direction, d_ref, dict(zip(names, sent)), flags_ref, ph, th)


def last_kernel(ph, th, names, flags_ref, local_ref, conduct_ref, partial_ref, *rest):
    older, taken, (next_ref, gram_ref, halo_ref) = rest[:S], rest[S : S + len(names)], rest[S + len(names) :]
    halo = add_faces(halo_ref, dict(zip(names, taken)), flags_ref, ph, th)
    final = local_ref[...] - conduct_ref[...] * halo
    next_ref[...] = final
    basis = [ref[...] for ref in older] + [final]
    stacked = jnp.concatenate([partial_ref[...]] + gram_rows([final] * (S + 1), basis), axis=0)
    each = jnp.sum(stacked, axis=1, keepdims=True)
    lane = lax.broadcasted_iota(jnp.int32, stacked.shape, 1)
    row = lax.broadcasted_iota(jnp.int32, stacked.shape, 0)
    line = jnp.sum(jnp.where(lane == row, each, 0.0), axis=0, keepdims=True)
    gram_ref[...] = jnp.broadcast_to(line, gram_ref.shape)


def small_solve(products):
    def entry(i, j):
        return products[max(i, j)][min(i, j)]

    def normal(j, k):
        return (entry(j, k) + entry(j + 1, k + 1)) + (entry(j + 1, k) + entry(j, k + 1))

    matrix = [[normal(j, k) for k in range(j + 1)] for j in range(S)]
    moment = [entry(j, 0) + entry(j + 1, 0) for j in range(S)]
    inverse = []
    for j in range(S):
        inverse.append(1.0 / matrix[j][j])
        scaled = {i: matrix[i][j] * inverse[j] for i in range(j + 1, S)}
        for i in range(j + 1, S):
            for k in range(j + 1, i + 1):
                matrix[i][k] = matrix[i][k] - scaled[i] * matrix[k][j]
            moment[i] = moment[i] - scaled[i] * moment[j]
    weights = [None] * S
    for i in reversed(range(S)):
        summed = moment[i]
        for k in range(i + 1, S):
            summed = summed - matrix[k][i] * weights[k]
        weights[i] = summed * inverse[i]
    return weights


def combine_kernel(partial_rows, gram_ref, *refs):
    krylov, directions, rest = refs[: S + 1], refs[S + 1 : 2 * S + 1], refs[2 * S + 1 :]
    correction_ref, residual_ref, correction, residual, sems = rest
    line = jnp.sum(gram_ref[...], axis=0, keepdims=True)
    products, place = [], 0
    for i in range(S + 1):
        products.append([])
        place = partial_rows if i == S else place
        for j in range(i + 1):
            products[i].append(jnp.broadcast_to(line[:, place : place + 1], line.shape))
            place += 1
    weights = small_solve(products)
    total = weights[0] * directions[0][...]
    for j in range(1, S):
        total = total + weights[j] * directions[j][...]
    from_rows(total, correction)
    first = pltpu.make_async_copy(correction, correction_ref, sems.at[0])
    first.start()
    total = krylov[0][...]
    for j in range(S):
        total = total - weights[j] * (krylov[j + 1][...] + krylov[j][...])
    from_rows(total, residual)
    second = pltpu.make_async_copy(residual, residual_ref, sems.at[1])
    second.start()
    first.wait()
    second.wait()


def call(kernel, outs, scratch, *args, stay=()):
    def spec(a):
        return pl.BlockSpec(memory_space=pltpu.HBM if any(a is b for b in stay) else pltpu.VMEM)

    placed = [pltpu.with_memory_space_constraint(a, pltpu.HBM) if any(a is b for b in stay) else a for a in args]
    return pl.pallas_call(
        kernel,
        out_shape=outs,
        in_specs=[spec(a) for a in args],
        out_specs=[spec(a) for a in outs],
        scratch_shapes=scratch,
        compiler_params=pltpu.CompilerParams(vmem_limit_bytes=VMEM_LIMIT),
    )(*placed)


def local(right_side, conduct, coupling, inverse, face_codes):
    _, ph, th, radial = right_side.shape
    nb = radial // BLK
    per = ph * th
    rows = per * nb
    at = {axis: (lax.axis_index(axis), lax.axis_size(axis)) for axis in ("row", "th", "ph")}
    (row_at, row_n), (th_at, th_n), (ph_at, ph_n) = at["row"], at["th"], at["ph"]
    face_rows = {"ph_high": nb * th, "row_high": per, "ph_low": nb * th, "th_high": rows // th, "th_low": rows // th, "row_low": per}
    if row_n == 2:
        face_rows.pop("row_high")
    if th_n == 2:
        face_rows.pop("th_high")
    names = tuple(face_rows)
    def shape(n):
        return jax.ShapeDtypeStruct((n, LANES), jnp.float32)

    faces = [shape(n) for n in face_rows.values()]
    whole = shape(rows)

    plans = {"low": pairs_low, "high": pairs_high}

    def exchange(sent):
        taken = []
        for name, array in zip(names, sent):
            axis, side = name.split("_")
            taken.append(lax.ppermute(array, axis, plans[side](lax.axis_size(axis))))
        return taken

    field = pltpu.VMEM(right_side.shape, jnp.float32)
    flags, start, conducts, diagonal, mixing, held, direction, *sent = call(
        functools.partial(first_kernel, ph, th, names, (("row", row_n), ("th", th_n), ("ph", ph_n))),
        [shape(VARS), whole, whole, whole, shape(VARS), jax.ShapeDtypeStruct(inverse.shape, jnp.bfloat16), whole] + faces,
        [
            field,
            field,
            pltpu.SMEM(coupling.shape, jnp.float32),
            pltpu.SMEM(face_codes.shape, jnp.int32),
            pltpu.SemaphoreType.DMA((5,)),
        ],
        right_side, conduct, coupling, face_codes, inverse,
        stay=(right_side, conduct, coupling, face_codes, inverse),
    )
    (turned,) = call(turn_kernel, [jax.ShapeDtypeStruct((rows, LANES, LANES), jnp.bfloat16)], [], held)
    krylov, directions = [start], [direction]
    halo = [pltpu.VMEM((rows, LANES), jnp.float32)]
    for step in range(S):
        taken = exchange(sent)
        (beside,) = call(
            functools.partial(local_kernel, ph, th), [whole], [], krylov[-1], directions[-1], conducts, diagonal, mixing
        )
        if step < S - 1:
            following, direction, *sent = call(
                functools.partial(step_kernel, ph, th, names),
                [whole, whole] + faces,
                halo,
                flags, beside, conducts, turned, *taken,
            )
            krylov.append(following)
            directions.append(direction)
    partial_rows = S * (S + 1) // 2
    partial_rows += -partial_rows % 8
    (partial,) = call(gram_kernel, [shape(partial_rows)], [], *krylov)
    following, gram = call(
        functools.partial(last_kernel, ph, th, names),
        [whole, shape(row_n * th_n * ph_n)],
        halo,
        flags, beside, conducts, partial, *krylov, *taken,
    )
    krylov.append(following)
    gram = lax.all_to_all(gram, ("row", "th", "ph"), 0, 0, tiled=True)
    native = [jax.ShapeDtypeStruct(right_side.shape, jnp.float32)] * 2
    return tuple(
        call(
            functools.partial(combine_kernel, partial_rows),
            native,
            [field, field, pltpu.SemaphoreType.DMA((2,))],
            gram, *krylov, *directions,
            stay=native,
        )
    )


def solution(mesh):
    placed = (
        P(None, "ph", "th", "row"),
        P(None, "ph", "th", "row"),
        P(),
        P("ph", "th", "row", None, None),
        P(None, "ph", "th"),
    )
    return jax.shard_map(
        local,
        mesh=mesh,
        in_specs=placed,
        out_specs=(P(None, "ph", "th", "row"), P(None, "ph", "th", "row")),
        check_vma=False,
    )
```

```python
import functools

import jax
import jax.numpy as jnp
from jax import lax
from jax.experimental import pallas as pl
from jax.experimental.pallas import tpu as pltpu
from jax.sharding import PartitionSpec as P

VARS = 8
BLK = 16
S = 4
LANES = VARS * BLK
GROUP = 8
VMEM_LIMIT = 24 * 1024 * 1024


def pairs_low(count):
    return [(i, i ^ 1) for i in range(count)]


def pairs_high(count):
    return [(i, (i + 1) % count if i % 2 else (i - 1) % count) for i in range(count)]


def to_rows(native_ref, turn_ref):
    var, ph, th, radial = native_ref.shape
    planes = [jnp.concatenate([native_ref[v, p] for p in range(ph)], axis=0) for v in range(var)]
    for b in range(radial // BLK):
        turn_ref[b * ph * th : (b + 1) * ph * th, :] = jnp.concatenate(
            [plane[:, b * BLK : (b + 1) * BLK] for plane in planes], axis=1
        )
    slab = turn_ref.shape[0] // th
    return jnp.concatenate([turn_ref[pl.ds(t, slab, stride=th), :] for t in range(th)], axis=0)


def from_rows(rows, native_ref, turn_ref):
    var, ph, th, radial = native_ref.shape
    slab = rows.shape[0] // th
    for t in range(th):
        turn_ref[pl.ds(t, slab, stride=th), :] = rows[t * slab : (t + 1) * slab]
    turned = turn_ref[...]
    per = ph * th
    for v in range(var):
        plane = jnp.concatenate(
            [turned[b * per : (b + 1) * per, v * BLK : (v + 1) * BLK] for b in range(radial // BLK)], axis=1
        )
        for p in range(ph):
            native_ref[v, p] = plane[p * th : (p + 1) * th]


def spread_rows(vectors):
    rounded = vectors.astype(jnp.bfloat16)
    row = lax.broadcasted_iota(jnp.int32, rounded.shape, 0) % GROUP
    return jnp.concatenate(
        [jnp.where(row == m, rounded, jnp.zeros_like(rounded)) for m in range(GROUP)], axis=1
    )


def own_halves(out):
    return jnp.concatenate([out[:GROUP, :LANES], out[GROUP:, LANES:]], axis=0)


def apply_stored(vectors, blocks):
    halves = [jnp.concatenate(blocks[half * GROUP : (half + 1) * GROUP], axis=1) for half in range(2)]
    out = lax.dot_general(
        spread_rows(vectors),
        jnp.concatenate(halves, axis=0),
        (((1,), (1,)), ((), ())),
        preferred_element_type=jnp.float32,
    )
    return own_halves(out)


def apply_turned(field_ref, turned_ref, out_ref, firsts):
    for first in firsts:
        halves = [
            jnp.concatenate([turned_ref[first + half * GROUP + m] for m in range(GROUP)], axis=0) for half in range(2)
        ]
        out = jnp.dot(
            spread_rows(field_ref[pl.ds(first, 2 * GROUP), :]),
            jnp.concatenate(halves, axis=1),
            preferred_element_type=jnp.float32,
        )
        out_ref[pl.ds(first, 2 * GROUP), :] = own_halves(out)


def pack_faces(d_ref, outs, flags_ref, ph, th):
    rows = d_ref.shape[0]
    slab = rows // th
    per = ph * th
    cell = lax.broadcasted_iota(jnp.int32, (per, LANES), 1) % BLK
    odd_ph, odd_row, odd_th = [flags_ref[i : i + 1, :] > 0.5 for i in range(3)]
    low = d_ref[pl.ds(0, rows // ph, stride=ph), :]
    high = d_ref[pl.ds(ph - 1, rows // ph, stride=ph), :]
    outs["ph_high"][...] = jnp.where(odd_ph, high, low)
    outs["ph_low"][...] = jnp.where(odd_ph, low, high)
    low = jnp.concatenate([d_ref[t * slab : t * slab + ph, :] for t in range(th)], axis=0)
    high = jnp.concatenate([d_ref[(t + 1) * slab - ph : (t + 1) * slab, :] for t in range(th)], axis=0)
    low = jnp.where(cell == BLK - 1, pltpu.roll(low, BLK - 1, 1), 0.0)
    high = jnp.where(cell == 0, pltpu.roll(high, LANES - BLK + 1, 1), 0.0)
    near = jnp.where(odd_row, low, high)
    outs["row_low"][...] = near[: per // 2] + pltpu.roll(near[per // 2 :], 1, 1)
    if "row_high" in outs:
        outs["row_high"][...] = jnp.where(odd_row, high, low)
    low, high = d_ref[:slab, :], d_ref[rows - slab :, :]
    outs["th_low"][...] = jnp.where(odd_th, low, high)
    if "th_high" in outs:
        outs["th_high"][...] = jnp.where(odd_th, high, low)


def local_part(field, krylov, conduct, diagonal, mixing_ref, ph, th):
    rows = field.shape[0]
    slab = rows // th
    nb = slab // ph
    lane = lax.broadcasted_iota(jnp.int32, (rows, LANES), 1)
    row = lax.broadcasted_iota(jnp.int32, (rows, LANES), 0)
    cell = lane % BLK
    azimuth = row % ph
    block = (row // ph) % nb
    mixed = field * mixing_ref[0:1, :]
    for m in range(1, VARS):
        mixed += pltpu.roll(field, LANES - BLK * m, 1) * mixing_ref[m : m + 1, :]
    from_low = pltpu.roll(pltpu.roll(field, LANES - BLK + 1, 1), ph, 0)
    from_high = pltpu.roll(pltpu.roll(field, BLK - 1, 1), rows - ph, 0)
    total = jnp.where(cell == 0, jnp.where(block == 0, 0.0, from_low), pltpu.roll(field, 1, 1))
    total += jnp.where(
        cell == BLK - 1, jnp.where(block == nb - 1, 0.0, from_high), pltpu.roll(field, LANES - 1, 1)
    )
    total += jnp.where(azimuth == 0, 0.0, pltpu.roll(field, 1, 0))
    total += jnp.where(azimuth == ph - 1, 0.0, pltpu.roll(field, rows - 1, 0))
    zero = jnp.zeros((slab, LANES), jnp.float32)
    total += jnp.concatenate([zero, field[: rows - slab]], axis=0)
    total += jnp.concatenate([field[slab:], zero], axis=0)
    return field + mixed + conduct * (diagonal * field - total) - krylov


def sides(axis, taken, flags_ref):
    parity, has_low, has_high = {"ph": (0, None, None), "row": (1, 3, 4), "th": (2, 5, 6)}[axis]
    odd = flags_ref[parity : parity + 1, :] > 0.5
    first = taken[axis + "_low"][...]
    if axis == "row":
        edge = jnp.where(odd, 0, BLK - 1)
        cell = lax.broadcasted_iota(jnp.int32, first.shape, 1) % BLK
        first = jnp.concatenate(
            [jnp.where(cell == edge, part, 0.0) for part in (first, pltpu.roll(first, LANES - 1, 1))], axis=0
        )
    second = taken[axis + "_high"][...] if axis + "_high" in taken else jnp.zeros_like(first)
    low, high = jnp.where(odd, first, second), jnp.where(odd, second, first)
    if has_low is None:
        return low, high
    low = jnp.where(flags_ref[has_low : has_low + 1, :] > 0.5, low, 0.0)
    return low, jnp.where(flags_ref[has_high : has_high + 1, :] > 0.5, high, 0.0)


def add_faces(halo_ref, taken, flags_ref, ph, th):
    rows = halo_ref.shape[0]
    slab = rows // th
    halo_ref[...] = jnp.zeros_like(halo_ref)
    low, high = sides("ph", taken, flags_ref)
    halo_ref[pl.ds(0, rows // ph, stride=ph), :] = low
    halo_ref[pl.ds(ph - 1, rows // ph, stride=ph), :] = high
    low, high = sides("row", taken, flags_ref)
    for t in range(th):
        halo_ref[t * slab : t * slab + ph, :] += low[t * ph : (t + 1) * ph]
        halo_ref[(t + 1) * slab - ph : (t + 1) * slab, :] += high[t * ph : (t + 1) * ph]


def split_slabs(th, th_n):
    if th_n > 2:
        return list(range(1, th - 1)), [0, th - 1]
    at = lax.axis_index("th")
    return [i + at for i in range(th - 1)], [(th - 1) * (1 - at)]


def groups_of(slabs, slab):
    return [
        pl.multiple_of(s * slab + i, 2 * GROUP) if not isinstance(s, int) else s * slab + i
        for s in slabs
        for i in range(0, slab, 2 * GROUP)
    ]


def first_kernel(ph, th, names, sizes, right_ref, conduct_ref, coupling_ref, codes_ref, inverse_ref, *rest):
    flags_ref, krylov_ref, conducts_ref, diagonal_ref, mixing_ref, held_ref, d_ref, *sent = rest[: 7 + len(names)]
    right, conduct, coupling, codes, turn, sems = rest[7 + len(names) :]
    rows = d_ref.shape[0]
    slab = rows // th
    pairs = [(right_ref, right), (coupling_ref, coupling), (codes_ref, codes), (conduct_ref, conduct)]
    parts = [pl.ds(t, th // 2) for t in range(0, th, th // 2)]
    pairs += [(inverse_ref.at[:, part], held_ref.at[:, part]) for part in parts]
    copies = [pltpu.make_async_copy(a, b, sems.at[i]) for i, (a, b) in enumerate(pairs)]
    for copy in copies:
        copy.start()

    def mix():
        copies[1].wait()
        lane = lax.broadcasted_iota(jnp.int32, (1, LANES), 1)
        for m in range(VARS):
            line = jnp.zeros((1, LANES), jnp.float32)
            for k in range(VARS):
                line = jnp.where(lane // BLK == k, coupling[k, (k + m) % VARS], line)
            mixing_ref[m : m + 1, :] = line

    def ghosts():
        copies[2].wait()
        cell = lax.broadcasted_iota(jnp.int32, (slab, LANES), 1) % BLK
        row = lax.broadcasted_iota(jnp.int32, (slab, LANES), 0)
        for t in range(th):
            diagonal = jnp.full((slab, LANES), 6.0, jnp.float32)
            for side, (edge, first, has) in enumerate(((0, 0, 3), (BLK - 1, slab - ph, 4))):
                factor = jnp.zeros((slab, LANES), jnp.float32)
                for p in range(ph):
                    code = codes[side, p, t]
                    value = jnp.where(code == 1, 1.0, jnp.where(code == 2, -1.0, 0.0))
                    factor = jnp.where(row == first + p, value, factor)
                diagonal -= jnp.where((cell == edge) & (flags_ref[has : has + 1, :] < 0.5), factor, 0.0)
            diagonal_ref[t * slab : (t + 1) * slab, :] = diagonal

    def lay_out():
        copies[3].wait()
        conducts_ref[...] = to_rows(conduct, turn)

    (row_at, row_n), (th_at, th_n), (ph_at, ph_n) = [(lax.axis_index(axis), n) for axis, n in sizes]
    values = [ph_at % 2, row_at % 2, th_at % 2, row_at > 0, row_at < row_n - 1, th_at > 0, th_at < th_n - 1]
    for i, value in enumerate(values):
        flags_ref[i : i + 1, :] = jnp.full((1, LANES), value.astype(jnp.float32))
    copies[0].wait()
    krylov_ref[...] = to_rows(right, turn)
    mix()
    ghosts()
    lay_out()
    for i, copy in enumerate(copies[4:]):
        copy.wait()
        for first in range(i * rows // 2, (i + 1) * rows // 2, 2 * GROUP):
            blocks = [held_ref[k % ph, k // slab, k % slab // ph] for k in range(first, first + 2 * GROUP)]
            d_ref[first : first + 2 * GROUP, :] = apply_stored(krylov_ref[first : first + 2 * GROUP, :], blocks)
    pack_faces(d_ref, dict(zip(names, sent)), flags_ref, ph, th)


def turn_kernel(held_ref, turned_ref):
    ph, th, nb = held_ref.shape[:3]
    for i in range(turned_ref.shape[0]):
        turned_ref[i] = held_ref[i % ph, i // (nb * ph), i % (nb * ph) // ph].T


def local_kernel(ph, th, krylov_ref, last_ref, conduct_ref, diagonal_ref, mixing_ref, out_ref):
    out_ref[...] = local_part(
        last_ref[...], krylov_ref[...], conduct_ref[...], diagonal_ref[...], mixing_ref, ph, th
    )


def gram_rows(left, right):
    lines = [jnp.sum(a * b, axis=0, keepdims=True) for a, b in zip(left, right)]
    return lines + [jnp.zeros_like(lines[0])] * (-len(lines) % 8)


def gram_kernel(*refs):
    basis = [ref[...] for ref in refs[:-1]]
    left = [basis[i] for i in range(S) for _ in range(i + 1)]
    right = [basis[j] for i in range(S) for j in range(i + 1)]
    refs[-1][...] = jnp.concatenate(gram_rows(left, right), axis=0)


def early_kernel(ph, th, th_n, names, flags_ref, local_ref, conduct_ref, turned_ref, *rest):
    next_ref, d_ref, halo_ref = rest[len(names) :]
    add_faces(halo_ref, dict(zip(names, rest)), flags_ref, ph, th)
    next_ref[...] = local_ref[...] - conduct_ref[...] * halo_ref[...]
    early, late = split_slabs(th, th_n)
    slab = d_ref.shape[0] // th
    apply_turned(next_ref, turned_ref, d_ref, groups_of(early, slab))
    for first in groups_of(late, slab):
        d_ref[pl.ds(first, 2 * GROUP), :] = jnp.zeros((2 * GROUP, LANES), jnp.float32)


def late_kernel(ph, th, th_n, names, late_names, flags_ref, early_ref, part_ref, conduct_ref, turned_ref, *rest):
    n = len(late_names)
    next_ref, d_ref, *sent = rest[n:]
    next_ref[...] = early_ref[...]
    d_ref[...] = part_ref[...]
    rows = d_ref.shape[0]
    slab = rows // th
    low, high = sides("th", dict(zip(late_names, rest)), flags_ref)
    _, late = split_slabs(th, th_n)
    faces = [low, high] if th_n > 2 else [low + high]
    for s, face in zip(late, faces):
        at = pl.ds(pl.multiple_of(s * slab, 2 * GROUP) if not isinstance(s, int) else s * slab, slab)
        next_ref[at, :] = early_ref[at, :] - conduct_ref[at, :] * face
    apply_turned(next_ref, turned_ref, d_ref, groups_of(late, slab))
    pack_faces(d_ref, dict(zip(names, sent)), flags_ref, ph, th)


def last_kernel(ph, th, names, flags_ref, local_ref, conduct_ref, partial_ref, *rest):
    older, taken, (next_ref, gram_ref, halo_ref) = rest[:S], rest[S : S + len(names)], rest[S + len(names) :]
    taken = dict(zip(names, taken))
    add_faces(halo_ref, taken, flags_ref, ph, th)
    low, high = sides("th", taken, flags_ref)
    rows = halo_ref.shape[0]
    slab = rows // th
    halo_ref[:slab, :] += low
    halo_ref[rows - slab :, :] += high
    final = local_ref[...] - conduct_ref[...] * halo_ref[...]
    next_ref[...] = final
    basis = [ref[...] for ref in older] + [final]
    stacked = jnp.concatenate([partial_ref[...]] + gram_rows([final] * (S + 1), basis), axis=0)
    each = jnp.sum(stacked, axis=1, keepdims=True)
    lane = lax.broadcasted_iota(jnp.int32, stacked.shape, 1)
    row = lax.broadcasted_iota(jnp.int32, stacked.shape, 0)
    line = jnp.sum(jnp.where(lane == row, each, 0.0), axis=0, keepdims=True)
    gram_ref[...] = jnp.broadcast_to(line, gram_ref.shape)


def small_solve(products):
    def entry(i, j):
        return products[max(i, j)][min(i, j)]

    def normal(j, k):
        return (entry(j, k) + entry(j + 1, k + 1)) + (entry(j + 1, k) + entry(j, k + 1))

    matrix = [[normal(j, k) for k in range(j + 1)] for j in range(S)]
    moment = [entry(j, 0) + entry(j + 1, 0) for j in range(S)]
    inverse = []
    for j in range(S):
        inverse.append(1.0 / matrix[j][j])
        scaled = {i: matrix[i][j] * inverse[j] for i in range(j + 1, S)}
        for i in range(j + 1, S):
            for k in range(j + 1, i + 1):
                matrix[i][k] = matrix[i][k] - scaled[i] * matrix[k][j]
            moment[i] = moment[i] - scaled[i] * moment[j]
    weights = [None] * S
    for i in reversed(range(S)):
        summed = moment[i]
        for k in range(i + 1, S):
            summed = summed - matrix[k][i] * weights[k]
        weights[i] = summed * inverse[i]
    return weights


def combine_kernel(partial_rows, gram_ref, *refs):
    krylov, directions, rest = refs[: S + 1], refs[S + 1 : 2 * S + 1], refs[2 * S + 1 :]
    correction_ref, residual_ref, correction, residual, turn, other_turn, sems = rest
    line = jnp.sum(gram_ref[...], axis=0, keepdims=True)
    products, place = [], 0
    for i in range(S + 1):
        products.append([])
        place = partial_rows if i == S else place
        for j in range(i + 1):
            products[i].append(jnp.broadcast_to(line[:, place : place + 1], line.shape))
            place += 1
    weights = small_solve(products)
    total = weights[0] * directions[0][...]
    for j in range(1, S):
        total = total + weights[j] * directions[j][...]
    left = krylov[0][...]
    for j in range(S):
        left = left - weights[j] * (krylov[j + 1][...] + krylov[j][...])
    from_rows(total, correction, turn)
    from_rows(left, residual, other_turn)
    copies = [
        pltpu.make_async_copy(correction, correction_ref, sems.at[0]),
        pltpu.make_async_copy(residual, residual_ref, sems.at[1]),
    ]
    for copy in copies:
        copy.start()
    for copy in copies:
        copy.wait()


def call(kernel, outs, scratch, *args, stay=()):
    def spec(a):
        return pl.BlockSpec(memory_space=pltpu.HBM if any(a is b for b in stay) else pltpu.VMEM)

    placed = [pltpu.with_memory_space_constraint(a, pltpu.HBM) if any(a is b for b in stay) else a for a in args]
    return pl.pallas_call(
        kernel,
        out_shape=outs,
        in_specs=[spec(a) for a in args],
        out_specs=[spec(a) for a in outs],
        scratch_shapes=scratch,
        compiler_params=pltpu.CompilerParams(vmem_limit_bytes=VMEM_LIMIT),
    )(*placed)


def local(right_side, conduct, coupling, inverse, face_codes):
    _, ph, th, radial = right_side.shape
    nb = radial // BLK
    per = ph * th
    rows = per * nb
    at = {axis: (lax.axis_index(axis), lax.axis_size(axis)) for axis in ("row", "th", "ph")}
    (row_at, row_n), (th_at, th_n), (ph_at, ph_n) = at["row"], at["th"], at["ph"]
    face_rows = {"ph_high": nb * th, "row_high": per, "ph_low": nb * th, "row_low": per // 2, "th_high": rows // th, "th_low": rows // th}
    if row_n == 2:
        face_rows.pop("row_high")
    if th_n == 2:
        face_rows.pop("th_high")
    names = tuple(face_rows)
    late_names = tuple(name for name in names if name[:2] == "th")
    def shape(n):
        return jax.ShapeDtypeStruct((n, LANES), jnp.float32)

    faces = [shape(n) for n in face_rows.values()]
    whole = shape(rows)

    plans = {"low": pairs_low, "high": pairs_high}

    def exchange(sent):
        taken = []
        for name, array in zip(names, sent):
            axis, side = name.split("_")
            taken.append(lax.ppermute(array, axis, plans[side](lax.axis_size(axis))))
        return taken

    field = pltpu.VMEM(right_side.shape, jnp.float32)
    turn = pltpu.VMEM((rows, LANES), jnp.float32)
    flags, start, conducts, diagonal, mixing, held, direction, *sent = call(
        functools.partial(first_kernel, ph, th, names, (("row", row_n), ("th", th_n), ("ph", ph_n))),
        [shape(VARS), whole, whole, whole, shape(VARS), jax.ShapeDtypeStruct(inverse.shape, jnp.bfloat16), whole] + faces,
        [
            field,
            field,
            pltpu.SMEM(coupling.shape, jnp.float32),
            pltpu.SMEM(face_codes.shape, jnp.int32),
            turn,
            pltpu.SemaphoreType.DMA((6,)),
        ],
        right_side, conduct, coupling, face_codes, inverse,
        stay=(right_side, conduct, coupling, face_codes, inverse),
    )
    (turned,) = call(turn_kernel, [jax.ShapeDtypeStruct((rows, LANES, LANES), jnp.bfloat16)], [], held)
    krylov, directions = [start], [direction]
    for step in range(S):
        taken = exchange(sent)
        (beside,) = call(
            functools.partial(local_kernel, ph, th), [whole], [], krylov[-1], directions[-1], conducts, diagonal, mixing
        )
        if step < S - 1:
            early_names, early_taken = zip(*[(n, t) for n, t in zip(names, taken) if n not in late_names])
            early, part = call(
                functools.partial(early_kernel, ph, th, th_n, early_names),
                [whole, whole],
                [turn],
                flags, beside, conducts, turned, *early_taken,
            )
            following, direction, *sent = call(
                functools.partial(late_kernel, ph, th, th_n, names, late_names),
                [whole, whole] + faces,
                [],
                flags, early, part, conducts, turned, *[t for n, t in zip(names, taken) if n in late_names],
            )
            krylov.append(following)
            directions.append(direction)
    partial_rows = S * (S + 1) // 2
    partial_rows += -partial_rows % 8
    (partial,) = call(gram_kernel, [shape(partial_rows)], [], *krylov)
    following, gram = call(
        functools.partial(last_kernel, ph, th, names),
        [whole, shape(row_n * th_n * ph_n)],
        [turn],
        flags, beside, conducts, partial, *krylov, *taken,
    )
    krylov.append(following)
    gram = lax.all_to_all(gram, ("row", "th", "ph"), 0, 0, tiled=True)
    native = [jax.ShapeDtypeStruct(right_side.shape, jnp.float32)] * 2
    return tuple(
        call(
            functools.partial(combine_kernel, partial_rows),
            native,
            [field, field, turn, turn, pltpu.SemaphoreType.DMA((2,))],
            gram, *krylov, *directions,
            stay=native,
        )
    )


def solution(mesh):
    placed = (
        P(None, "ph", "th", "row"),
        P(None, "ph", "th", "row"),
        P(),
        P("ph", "th", "row", None, None),
        P(None, "ph", "th"),
    )
    return jax.shard_map(
        local,
        mesh=mesh,
        in_specs=placed,
        out_specs=(P(None, "ph", "th", "row"), P(None, "ph", "th", "row")),
        check_vma=False,
    )
```

```python
import functools

import jax
import jax.numpy as jnp
from jax import lax
from jax.experimental import pallas as pl
from jax.experimental.pallas import tpu as pltpu
from jax.sharding import PartitionSpec as P

VARS = 8
BLK = 16
S = 4
LANES = VARS * BLK
GROUP = 8
VMEM_LIMIT = 24 * 1024 * 1024


def pairs_low(count):
    return [(i, i ^ 1) for i in range(count)]


def pairs_high(count):
    return [(i, (i + 1) % count if i % 2 else (i - 1) % count) for i in range(count)]


def to_rows(native_ref, turn_ref):
    var, ph, th, radial = native_ref.shape
    planes = [jnp.concatenate([native_ref[v, p] for p in range(ph)], axis=0) for v in range(var)]
    for b in range(radial // BLK):
        turn_ref[b * ph * th : (b + 1) * ph * th, :] = jnp.concatenate(
            [plane[:, b * BLK : (b + 1) * BLK] for plane in planes], axis=1
        )
    slab = turn_ref.shape[0] // th
    return jnp.concatenate([turn_ref[pl.ds(t, slab, stride=th), :] for t in range(th)], axis=0)


def from_rows(rows, native_ref, turn_ref):
    var, ph, th, radial = native_ref.shape
    slab = rows.shape[0] // th
    for t in range(th):
        turn_ref[pl.ds(t, slab, stride=th), :] = rows[t * slab : (t + 1) * slab]
    turned = turn_ref[...]
    per = ph * th
    for v in range(var):
        plane = jnp.concatenate(
            [turned[b * per : (b + 1) * per, v * BLK : (v + 1) * BLK] for b in range(radial // BLK)], axis=1
        )
        for p in range(ph):
            native_ref[v, p] = plane[p * th : (p + 1) * th]


def spread_rows(vectors):
    rounded = vectors.astype(jnp.bfloat16)
    row = lax.broadcasted_iota(jnp.int32, rounded.shape, 0) % GROUP
    return jnp.concatenate(
        [jnp.where(row == m, rounded, jnp.zeros_like(rounded)) for m in range(GROUP)], axis=1
    )


def own_halves(out):
    return jnp.concatenate([out[:GROUP, :LANES], out[GROUP:, LANES:]], axis=0)


def apply_stored(vectors, blocks):
    halves = [jnp.concatenate(blocks[half * GROUP : (half + 1) * GROUP], axis=1) for half in range(2)]
    out = lax.dot_general(
        spread_rows(vectors),
        jnp.concatenate(halves, axis=0),
        (((1,), (1,)), ((), ())),
        preferred_element_type=jnp.float32,
    )
    return own_halves(out)


def apply_turned(field_ref, turned_ref, out_ref, firsts):
    for first in firsts:
        halves = [
            jnp.concatenate([turned_ref[first + half * GROUP + m] for m in range(GROUP)], axis=0) for half in range(2)
        ]
        out = jnp.dot(
            spread_rows(field_ref[pl.ds(first, 2 * GROUP), :]),
            jnp.concatenate(halves, axis=1),
            preferred_element_type=jnp.float32,
        )
        out_ref[pl.ds(first, 2 * GROUP), :] = own_halves(out)


def pack_faces(d_ref, outs, flags_ref, ph, th):
    rows = d_ref.shape[0]
    slab = rows // th
    per = ph * th
    cell = lax.broadcasted_iota(jnp.int32, (per, LANES), 1) % BLK
    odd_ph, odd_row, odd_th = [flags_ref[i : i + 1, :] > 0.5 for i in range(3)]
    low = d_ref[pl.ds(0, rows // ph, stride=ph), :]
    high = d_ref[pl.ds(ph - 1, rows // ph, stride=ph), :]
    outs["ph_high"][...] = jnp.where(odd_ph, high, low)
    outs["ph_low"][...] = jnp.where(odd_ph, low, high)
    low = jnp.concatenate([d_ref[t * slab : t * slab + ph, :] for t in range(th)], axis=0)
    high = jnp.concatenate([d_ref[(t + 1) * slab - ph : (t + 1) * slab, :] for t in range(th)], axis=0)
    half = per // 2
    low_next = jnp.where(cell[half:] == 0, pltpu.roll(low[half:], BLK, 1), 0.0)
    high_next = jnp.where(cell[half:] == 1, pltpu.roll(high[half:], LANES - BLK + 2, 1), 0.0)
    low = jnp.where(cell == BLK - 1, pltpu.roll(low, BLK - 1, 1), 0.0)
    high = jnp.where(cell == 0, pltpu.roll(high, LANES - BLK + 1, 1), 0.0)
    outs["row_low"][...] = jnp.where(odd_row, low[:half] + low_next, high[:half] + high_next)
    if "row_high" in outs:
        outs["row_high"][...] = jnp.where(odd_row, high, low)
    low, high = d_ref[:slab, :], d_ref[rows - slab :, :]
    outs["th_low"][...] = jnp.where(odd_th, low, high)
    if "th_high" in outs:
        outs["th_high"][...] = jnp.where(odd_th, high, low)


def local_part(field, krylov, conduct, diagonal, mixing_ref, ph, th):
    rows = field.shape[0]
    slab = rows // th
    nb = slab // ph
    lane = lax.broadcasted_iota(jnp.int32, (rows, LANES), 1)
    row = lax.broadcasted_iota(jnp.int32, (rows, LANES), 0)
    cell = lane % BLK
    azimuth = row % ph
    block = (row // ph) % nb
    mixed = field * mixing_ref[0:1, :]
    for m in range(1, VARS):
        mixed += pltpu.roll(field, LANES - BLK * m, 1) * mixing_ref[m : m + 1, :]
    from_low = pltpu.roll(pltpu.roll(field, LANES - BLK + 1, 1), ph, 0)
    from_high = pltpu.roll(pltpu.roll(field, BLK - 1, 1), rows - ph, 0)
    total = jnp.where(cell == 0, jnp.where(block == 0, 0.0, from_low), pltpu.roll(field, 1, 1))
    total += jnp.where(
        cell == BLK - 1, jnp.where(block == nb - 1, 0.0, from_high), pltpu.roll(field, LANES - 1, 1)
    )
    total += jnp.where(azimuth == 0, 0.0, pltpu.roll(field, 1, 0))
    total += jnp.where(azimuth == ph - 1, 0.0, pltpu.roll(field, rows - 1, 0))
    zero = jnp.zeros((slab, LANES), jnp.float32)
    total += jnp.concatenate([zero, field[: rows - slab]], axis=0)
    total += jnp.concatenate([field[slab:], zero], axis=0)
    return field + mixed + conduct * (diagonal * field - total) - krylov


def sides(axis, taken, flags_ref):
    parity, has_low, has_high = {"ph": (0, None, None), "row": (1, 3, 4), "th": (2, 5, 6)}[axis]
    odd = flags_ref[parity : parity + 1, :] > 0.5
    first = taken[axis + "_low"][...]
    if axis == "row":
        edge = jnp.where(odd, 0, BLK - 1)
        cell = lax.broadcasted_iota(jnp.int32, first.shape, 1) % BLK
        first = jnp.concatenate(
            [jnp.where(cell == edge, part, 0.0) for part in (first, pltpu.roll(first, LANES - 1, 1))], axis=0
        )
    second = taken[axis + "_high"][...] if axis + "_high" in taken else jnp.zeros_like(first)
    low, high = jnp.where(odd, first, second), jnp.where(odd, second, first)
    if has_low is None:
        return low, high
    low = jnp.where(flags_ref[has_low : has_low + 1, :] > 0.5, low, 0.0)
    return low, jnp.where(flags_ref[has_high : has_high + 1, :] > 0.5, high, 0.0)


def add_faces(halo_ref, taken, flags_ref, ph, th):
    rows = halo_ref.shape[0]
    slab = rows // th
    halo_ref[...] = jnp.zeros_like(halo_ref)
    low, high = sides("ph", taken, flags_ref)
    halo_ref[pl.ds(0, rows // ph, stride=ph), :] = low
    halo_ref[pl.ds(ph - 1, rows // ph, stride=ph), :] = high
    low, high = sides("row", taken, flags_ref)
    for t in range(th):
        halo_ref[t * slab : t * slab + ph, :] += low[t * ph : (t + 1) * ph]
        halo_ref[(t + 1) * slab - ph : (t + 1) * slab, :] += high[t * ph : (t + 1) * ph]


def split_slabs(th, th_n):
    if th_n > 2:
        return list(range(1, th - 1)), [0, th - 1]
    at = lax.axis_index("th")
    return [i + at for i in range(th - 1)], [(th - 1) * (1 - at)]


def groups_of(slabs, slab):
    return [
        pl.multiple_of(s * slab + i, 2 * GROUP) if not isinstance(s, int) else s * slab + i
        for s in slabs
        for i in range(0, slab, 2 * GROUP)
    ]


def first_kernel(ph, th, names, sizes, right_ref, conduct_ref, coupling_ref, codes_ref, inverse_ref, *rest):
    flags_ref, krylov_ref, conducts_ref, diagonal_ref, mixing_ref, held_ref, d_ref, *sent = rest[: 7 + len(names)]
    right, conduct, coupling, codes, turn, sems = rest[7 + len(names) :]
    rows = d_ref.shape[0]
    slab = rows // th
    pairs = [(right_ref, right), (coupling_ref, coupling), (codes_ref, codes), (conduct_ref, conduct)]
    parts = [pl.ds(t, th // 2) for t in range(0, th, th // 2)]
    pairs += [(inverse_ref.at[:, part], held_ref.at[:, part]) for part in parts]
    copies = [pltpu.make_async_copy(a, b, sems.at[i]) for i, (a, b) in enumerate(pairs)]
    for copy in copies:
        copy.start()

    def mix():
        copies[1].wait()
        lane = lax.broadcasted_iota(jnp.int32, (1, LANES), 1)
        for m in range(VARS):
            line = jnp.zeros((1, LANES), jnp.float32)
            for k in range(VARS):
                line = jnp.where(lane // BLK == k, coupling[k, (k + m) % VARS], line)
            mixing_ref[m : m + 1, :] = line

    def ghosts():
        copies[2].wait()
        cell = lax.broadcasted_iota(jnp.int32, (slab, LANES), 1) % BLK
        row = lax.broadcasted_iota(jnp.int32, (slab, LANES), 0)
        for t in range(th):
            diagonal = jnp.full((slab, LANES), 6.0, jnp.float32)
            for side, (edge, first, has) in enumerate(((0, 0, 3), (BLK - 1, slab - ph, 4))):
                factor = jnp.zeros((slab, LANES), jnp.float32)
                for p in range(ph):
                    code = codes[side, p, t]
                    value = jnp.where(code == 1, 1.0, jnp.where(code == 2, -1.0, 0.0))
                    factor = jnp.where(row == first + p, value, factor)
                diagonal -= jnp.where((cell == edge) & (flags_ref[has : has + 1, :] < 0.5), factor, 0.0)
            diagonal_ref[t * slab : (t + 1) * slab, :] = diagonal

    def lay_out():
        copies[3].wait()
        conducts_ref[...] = to_rows(conduct, turn)

    (row_at, row_n), (th_at, th_n), (ph_at, ph_n) = [(lax.axis_index(axis), n) for axis, n in sizes]
    values = [ph_at % 2, row_at % 2, th_at % 2, row_at > 0, row_at < row_n - 1, th_at > 0, th_at < th_n - 1]
    for i, value in enumerate(values):
        flags_ref[i : i + 1, :] = jnp.full((1, LANES), value.astype(jnp.float32))
    copies[0].wait()
    krylov_ref[...] = to_rows(right, turn)
    mix()
    ghosts()
    lay_out()
    for i, copy in enumerate(copies[4:]):
        copy.wait()
        for first in range(i * rows // 2, (i + 1) * rows // 2, 2 * GROUP):
            blocks = [held_ref[k % ph, k // slab, k % slab // ph] for k in range(first, first + 2 * GROUP)]
            d_ref[first : first + 2 * GROUP, :] = apply_stored(krylov_ref[first : first + 2 * GROUP, :], blocks)
    pack_faces(d_ref, dict(zip(names, sent)), flags_ref, ph, th)


def turn_kernel(held_ref, turned_ref):
    ph, th, nb = held_ref.shape[:3]
    for i in range(turned_ref.shape[0]):
        turned_ref[i] = held_ref[i % ph, i // (nb * ph), i % (nb * ph) // ph].T


def local_kernel(ph, th, krylov_ref, last_ref, conduct_ref, diagonal_ref, mixing_ref, out_ref):
    out_ref[...] = local_part(
        last_ref[...], krylov_ref[...], conduct_ref[...], diagonal_ref[...], mixing_ref, ph, th
    )


def gram_rows(left, right):
    lines = [jnp.sum(a * b, axis=0, keepdims=True) for a, b in zip(left, right)]
    return lines + [jnp.zeros_like(lines[0])] * (-len(lines) % 8)


def gram_kernel(*refs):
    basis = [ref[...] for ref in refs[:-1]]
    left = [basis[i] for i in range(S) for _ in range(i + 1)]
    right = [basis[j] for i in range(S) for j in range(i + 1)]
    refs[-1][...] = jnp.concatenate(gram_rows(left, right), axis=0)


def early_kernel(ph, th, th_n, names, flags_ref, local_ref, conduct_ref, turned_ref, *rest):
    next_ref, d_ref, halo_ref = rest[len(names) :]
    add_faces(halo_ref, dict(zip(names, rest)), flags_ref, ph, th)
    next_ref[...] = local_ref[...] - conduct_ref[...] * halo_ref[...]
    early, late = split_slabs(th, th_n)
    slab = d_ref.shape[0] // th
    apply_turned(next_ref, turned_ref, d_ref, groups_of(early, slab))
    for first in groups_of(late, slab):
        d_ref[pl.ds(first, 2 * GROUP), :] = jnp.zeros((2 * GROUP, LANES), jnp.float32)


def late_kernel(ph, th, th_n, names, late_names, flags_ref, early_ref, part_ref, conduct_ref, turned_ref, *rest):
    n = len(late_names)
    next_ref, d_ref, *sent = rest[n:]
    next_ref[...] = early_ref[...]
    d_ref[...] = part_ref[...]
    rows = d_ref.shape[0]
    slab = rows // th
    low, high = sides("th", dict(zip(late_names, rest)), flags_ref)
    _, late = split_slabs(th, th_n)
    faces = [low, high] if th_n > 2 else [low + high]
    for s, face in zip(late, faces):
        at = pl.ds(pl.multiple_of(s * slab, 2 * GROUP) if not isinstance(s, int) else s * slab, slab)
        next_ref[at, :] = early_ref[at, :] - conduct_ref[at, :] * face
    apply_turned(next_ref, turned_ref, d_ref, groups_of(late, slab))
    pack_faces(d_ref, dict(zip(names, sent)), flags_ref, ph, th)


def last_kernel(ph, th, names, flags_ref, local_ref, conduct_ref, partial_ref, *rest):
    older, taken, (next_ref, gram_ref, halo_ref) = rest[:S], rest[S : S + len(names)], rest[S + len(names) :]
    taken = dict(zip(names, taken))
    add_faces(halo_ref, taken, flags_ref, ph, th)
    low, high = sides("th", taken, flags_ref)
    rows = halo_ref.shape[0]
    slab = rows // th
    halo_ref[:slab, :] += low
    halo_ref[rows - slab :, :] += high
    final = local_ref[...] - conduct_ref[...] * halo_ref[...]
    next_ref[...] = final
    basis = [ref[...] for ref in older] + [final]
    stacked = jnp.concatenate([partial_ref[...]] + gram_rows([final] * (S + 1), basis), axis=0)
    each = jnp.sum(stacked, axis=1, keepdims=True)
    lane = lax.broadcasted_iota(jnp.int32, stacked.shape, 1)
    row = lax.broadcasted_iota(jnp.int32, stacked.shape, 0)
    line = jnp.sum(jnp.where(lane == row, each, 0.0), axis=0, keepdims=True)
    gram_ref[...] = jnp.broadcast_to(line, gram_ref.shape)


def small_solve(products):
    def entry(i, j):
        return products[max(i, j)][min(i, j)]

    def normal(j, k):
        return (entry(j, k) + entry(j + 1, k + 1)) + (entry(j + 1, k) + entry(j, k + 1))

    matrix = [[normal(j, k) for k in range(j + 1)] for j in range(S)]
    moment = [entry(j, 0) + entry(j + 1, 0) for j in range(S)]
    inverse = []
    for j in range(S):
        inverse.append(1.0 / matrix[j][j])
        scaled = {i: matrix[i][j] * inverse[j] for i in range(j + 1, S)}
        for i in range(j + 1, S):
            for k in range(j + 1, i + 1):
                matrix[i][k] = matrix[i][k] - scaled[i] * matrix[k][j]
            moment[i] = moment[i] - scaled[i] * moment[j]
    weights = [None] * S
    for i in reversed(range(S)):
        summed = moment[i]
        for k in range(i + 1, S):
            summed = summed - matrix[k][i] * weights[k]
        weights[i] = summed * inverse[i]
    return weights


def combine_kernel(partial_rows, gram_ref, *refs):
    krylov, directions, rest = refs[: S + 1], refs[S + 1 : 2 * S + 1], refs[2 * S + 1 :]
    correction_ref, residual_ref, correction, residual, turn, other_turn, sems = rest
    line = jnp.sum(gram_ref[...], axis=0, keepdims=True)
    products, place = [], 0
    for i in range(S + 1):
        products.append([])
        place = partial_rows if i == S else place
        for j in range(i + 1):
            products[i].append(jnp.broadcast_to(line[:, place : place + 1], line.shape))
            place += 1
    weights = small_solve(products)
    total = weights[0] * directions[0][...]
    for j in range(1, S):
        total = total + weights[j] * directions[j][...]
    left = krylov[0][...]
    for j in range(S):
        left = left - weights[j] * (krylov[j + 1][...] + krylov[j][...])
    from_rows(total, correction, turn)
    from_rows(left, residual, other_turn)
    copies = [
        pltpu.make_async_copy(correction, correction_ref, sems.at[0]),
        pltpu.make_async_copy(residual, residual_ref, sems.at[1]),
    ]
    for copy in copies:
        copy.start()
    for copy in copies:
        copy.wait()


def call(kernel, outs, scratch, *args, stay=()):
    def spec(a):
        return pl.BlockSpec(memory_space=pltpu.HBM if any(a is b for b in stay) else pltpu.VMEM)

    placed = [pltpu.with_memory_space_constraint(a, pltpu.HBM) if any(a is b for b in stay) else a for a in args]
    return pl.pallas_call(
        kernel,
        out_shape=outs,
        in_specs=[spec(a) for a in args],
        out_specs=[spec(a) for a in outs],
        scratch_shapes=scratch,
        compiler_params=pltpu.CompilerParams(vmem_limit_bytes=VMEM_LIMIT),
    )(*placed)


def local(right_side, conduct, coupling, inverse, face_codes):
    _, ph, th, radial = right_side.shape
    nb = radial // BLK
    per = ph * th
    rows = per * nb
    at = {axis: (lax.axis_index(axis), lax.axis_size(axis)) for axis in ("row", "th", "ph")}
    (row_at, row_n), (th_at, th_n), (ph_at, ph_n) = at["row"], at["th"], at["ph"]
    face_rows = {"ph_high": nb * th, "row_high": per, "ph_low": nb * th, "row_low": per // 2, "th_high": rows // th, "th_low": rows // th}
    if row_n == 2:
        face_rows.pop("row_high")
    if th_n == 2:
        face_rows.pop("th_high")
    names = tuple(face_rows)
    late_names = tuple(name for name in names if name[:2] == "th")
    def shape(n):
        return jax.ShapeDtypeStruct((n, LANES), jnp.float32)

    faces = [shape(n) for n in face_rows.values()]
    whole = shape(rows)

    plans = {"low": pairs_low, "high": pairs_high}

    def exchange(sent):
        taken = []
        for name, array in zip(names, sent):
            axis, side = name.split("_")
            taken.append(lax.ppermute(array, axis, plans[side](lax.axis_size(axis))))
        return taken

    field = pltpu.VMEM(right_side.shape, jnp.float32)
    turn = pltpu.VMEM((rows, LANES), jnp.float32)
    flags, start, conducts, diagonal, mixing, held, direction, *sent = call(
        functools.partial(first_kernel, ph, th, names, (("row", row_n), ("th", th_n), ("ph", ph_n))),
        [shape(VARS), whole, whole, whole, shape(VARS), jax.ShapeDtypeStruct(inverse.shape, jnp.bfloat16), whole] + faces,
        [
            field,
            field,
            pltpu.SMEM(coupling.shape, jnp.float32),
            pltpu.SMEM(face_codes.shape, jnp.int32),
            turn,
            pltpu.SemaphoreType.DMA((6,)),
        ],
        right_side, conduct, coupling, face_codes, inverse,
        stay=(right_side, conduct, coupling, face_codes, inverse),
    )
    (turned,) = call(turn_kernel, [jax.ShapeDtypeStruct((rows, LANES, LANES), jnp.bfloat16)], [], held)
    krylov, directions = [start], [direction]
    for step in range(S):
        taken = exchange(sent)
        (beside,) = call(
            functools.partial(local_kernel, ph, th), [whole], [], krylov[-1], directions[-1], conducts, diagonal, mixing
        )
        if step < S - 1:
            early_names, early_taken = zip(*[(n, t) for n, t in zip(names, taken) if n not in late_names])
            early, part = call(
                functools.partial(early_kernel, ph, th, th_n, early_names),
                [whole, whole],
                [turn],
                flags, beside, conducts, turned, *early_taken,
            )
            following, direction, *sent = call(
                functools.partial(late_kernel, ph, th, th_n, names, late_names),
                [whole, whole] + faces,
                [],
                flags, early, part, conducts, turned, *[t for n, t in zip(names, taken) if n in late_names],
            )
            krylov.append(following)
            directions.append(direction)
    partial_rows = S * (S + 1) // 2
    partial_rows += -partial_rows % 8
    (partial,) = call(gram_kernel, [shape(partial_rows)], [], *krylov)
    following, gram = call(
        functools.partial(last_kernel, ph, th, names),
        [whole, shape(row_n * th_n * ph_n)],
        [turn],
        flags, beside, conducts, partial, *krylov, *taken,
    )
    krylov.append(following)
    gram = lax.all_to_all(gram, ("row", "th", "ph"), 0, 0, tiled=True)
    native = [jax.ShapeDtypeStruct(right_side.shape, jnp.float32)] * 2
    return tuple(
        call(
            functools.partial(combine_kernel, partial_rows),
            native,
            [field, field, turn, turn, pltpu.SemaphoreType.DMA((2,))],
            gram, *krylov, *directions,
            stay=native,
        )
    )


def solution(mesh):
    placed = (
        P(None, "ph", "th", "row"),
        P(None, "ph", "th", "row"),
        P(),
        P("ph", "th", "row", None, None),
        P(None, "ph", "th"),
    )
    return jax.shard_map(
        local,
        mesh=mesh,
        in_specs=placed,
        out_specs=(P(None, "ph", "th", "row"), P(None, "ph", "th", "row")),
        check_vma=False,
    )
```

```python
import functools

import jax
import jax.numpy as jnp
from jax import lax
from jax.experimental import pallas as pl
from jax.experimental.pallas import tpu as pltpu
from jax.sharding import PartitionSpec as P

VARS = 8
BLK = 16
S = 4
LANES = VARS * BLK
GROUP = 8
VMEM_LIMIT = 24 * 1024 * 1024


def pairs_low(count):
    return [(i, i ^ 1) for i in range(count)]


def pairs_high(count):
    return [(i, (i + 1) % count if i % 2 else (i - 1) % count) for i in range(count)]


def to_rows(native_ref, turn_ref):
    var, ph, th, radial = native_ref.shape
    planes = [jnp.concatenate([native_ref[v, p] for p in range(ph)], axis=0) for v in range(var)]
    for b in range(radial // BLK):
        turn_ref[b * ph * th : (b + 1) * ph * th, :] = jnp.concatenate(
            [plane[:, b * BLK : (b + 1) * BLK] for plane in planes], axis=1
        )
    slab = turn_ref.shape[0] // th
    return jnp.concatenate([turn_ref[pl.ds(t, slab, stride=th), :] for t in range(th)], axis=0)


def from_rows(rows, native_ref, turn_ref):
    var, ph, th, radial = native_ref.shape
    slab = rows.shape[0] // th
    for t in range(th):
        turn_ref[pl.ds(t, slab, stride=th), :] = rows[t * slab : (t + 1) * slab]
    turned = turn_ref[...]
    per = ph * th
    for v in range(var):
        plane = jnp.concatenate(
            [turned[b * per : (b + 1) * per, v * BLK : (v + 1) * BLK] for b in range(radial // BLK)], axis=1
        )
        for p in range(ph):
            native_ref[v, p] = plane[p * th : (p + 1) * th]


def spread_rows(vectors):
    rounded = vectors.astype(jnp.bfloat16)
    row = lax.broadcasted_iota(jnp.int32, rounded.shape, 0) % GROUP
    return jnp.concatenate(
        [jnp.where(row == m, rounded, jnp.zeros_like(rounded)) for m in range(GROUP)], axis=1
    )


def own_halves(out):
    return jnp.concatenate([out[:GROUP, :LANES], out[GROUP:, LANES:]], axis=0)


def apply_stored(vectors, blocks):
    halves = [jnp.concatenate(blocks[half * GROUP : (half + 1) * GROUP], axis=1) for half in range(2)]
    out = lax.dot_general(
        spread_rows(vectors),
        jnp.concatenate(halves, axis=0),
        (((1,), (1,)), ((), ())),
        preferred_element_type=jnp.float32,
    )
    return own_halves(out)


def apply_turned(field_ref, turned_ref, out_ref, firsts):
    for first in firsts:
        halves = [
            jnp.concatenate([turned_ref[first + half * GROUP + m] for m in range(GROUP)], axis=0) for half in range(2)
        ]
        out = jnp.dot(
            spread_rows(field_ref[pl.ds(first, 2 * GROUP), :]),
            jnp.concatenate(halves, axis=1),
            preferred_element_type=jnp.float32,
        )
        out_ref[pl.ds(first, 2 * GROUP), :] = own_halves(out)


def pack_faces(d_ref, outs, flags_ref, ph, th):
    rows = d_ref.shape[0]
    slab = rows // th
    odd_ph, odd_row, odd_th = [flags_ref[i : i + 1, :] > 0.5 for i in range(3)]
    low = d_ref[pl.ds(0, rows // ph, stride=ph), :]
    high = d_ref[pl.ds(ph - 1, rows // ph, stride=ph), :]
    outs["ph_high"][...] = jnp.where(odd_ph, high, low)
    outs["ph_low"][...] = jnp.where(odd_ph, low, high)
    if "row_high" in outs:
        for t in range(th):
            low, high = radial_edges(d_ref, t, slab, ph)
            outs["row_high"][t * ph : (t + 1) * ph, :] = jnp.where(odd_row, high, low)
    low, high = d_ref[:slab, :], d_ref[rows - slab :, :]
    outs["th_low"][...] = jnp.where(odd_th, low, high)
    if "th_high" in outs:
        outs["th_high"][...] = jnp.where(odd_th, high, low)


def radial_edges(d_ref, t, slab, ph):
    return d_ref[t * slab : t * slab + ph, :], d_ref[(t + 1) * slab - ph : (t + 1) * slab, :]


def near_kernel(ph, th, flags_ref, d_ref, out_ref):
    slab = d_ref.shape[0] // th
    half = out_ref.shape[0]
    low, high = [jnp.concatenate(side, axis=0) for side in zip(*[radial_edges(d_ref, t, slab, ph) for t in range(th)])]
    cell = lax.broadcasted_iota(jnp.int32, (half, LANES), 1) % BLK
    low = jnp.where(cell == BLK - 1, pltpu.roll(low[:half], BLK - 1, 1), 0.0) + jnp.where(
        cell == 0, pltpu.roll(low[half:], BLK, 1), 0.0
    )
    high = jnp.where(cell == 0, pltpu.roll(high[:half], LANES - BLK + 1, 1), 0.0) + jnp.where(
        cell == 1, pltpu.roll(high[half:], LANES - BLK + 2, 1), 0.0
    )
    out_ref[...] = jnp.where(flags_ref[1:2, :] > 0.5, low, high)


def across_kernel(flags_ref, face_ref, out_ref):
    face = face_ref[...]
    cell = lax.broadcasted_iota(jnp.int32, face.shape, 1) % BLK
    below = jnp.where(cell == 0, pltpu.roll(face, LANES - BLK + 1, 1), 0.0)
    above = jnp.where(cell == BLK - 1, pltpu.roll(face, BLK - 1, 1), 0.0)
    out_ref[...] = jnp.where(flags_ref[1:2, :] > 0.5, above, below)


def local_part(field, krylov, conduct, diagonal, mixing_ref, ph, th):
    rows = field.shape[0]
    slab = rows // th
    nb = slab // ph
    lane = lax.broadcasted_iota(jnp.int32, (rows, LANES), 1)
    row = lax.broadcasted_iota(jnp.int32, (rows, LANES), 0)
    cell = lane % BLK
    azimuth = row % ph
    block = (row // ph) % nb
    mixed = field * mixing_ref[0:1, :]
    for m in range(1, VARS):
        mixed += pltpu.roll(field, LANES - BLK * m, 1) * mixing_ref[m : m + 1, :]
    from_low = pltpu.roll(pltpu.roll(field, LANES - BLK + 1, 1), ph, 0)
    from_high = pltpu.roll(pltpu.roll(field, BLK - 1, 1), rows - ph, 0)
    total = jnp.where(cell == 0, jnp.where(block == 0, 0.0, from_low), pltpu.roll(field, 1, 1))
    total += jnp.where(
        cell == BLK - 1, jnp.where(block == nb - 1, 0.0, from_high), pltpu.roll(field, LANES - 1, 1)
    )
    total += jnp.where(azimuth == 0, 0.0, pltpu.roll(field, 1, 0))
    total += jnp.where(azimuth == ph - 1, 0.0, pltpu.roll(field, rows - 1, 0))
    zero = jnp.zeros((slab, LANES), jnp.float32)
    total += jnp.concatenate([zero, field[: rows - slab]], axis=0)
    total += jnp.concatenate([field[slab:], zero], axis=0)
    return field + mixed + conduct * (diagonal * field - total) - krylov


def sides(axis, taken, flags_ref):
    parity, has_low, has_high = {"ph": (0, None, None), "row": (1, 3, 4), "th": (2, 5, 6)}[axis]
    odd = flags_ref[parity : parity + 1, :] > 0.5
    first = taken[axis + "_low"][...]
    if axis == "row":
        edge = jnp.where(odd, 0, BLK - 1)
        cell = lax.broadcasted_iota(jnp.int32, first.shape, 1) % BLK
        first = jnp.concatenate(
            [jnp.where(cell == edge, part, 0.0) for part in (first, pltpu.roll(first, LANES - 1, 1))], axis=0
        )
    second = taken[axis + "_high"][...] if axis + "_high" in taken else jnp.zeros_like(first)
    low, high = jnp.where(odd, first, second), jnp.where(odd, second, first)
    if has_low is None:
        return low, high
    low = jnp.where(flags_ref[has_low : has_low + 1, :] > 0.5, low, 0.0)
    return low, jnp.where(flags_ref[has_high : has_high + 1, :] > 0.5, high, 0.0)


def add_faces(halo_ref, taken, flags_ref, ph, th):
    rows = halo_ref.shape[0]
    slab = rows // th
    halo_ref[...] = jnp.zeros_like(halo_ref)
    low, high = sides("ph", taken, flags_ref)
    halo_ref[pl.ds(0, rows // ph, stride=ph), :] = low
    halo_ref[pl.ds(ph - 1, rows // ph, stride=ph), :] = high
    low, high = sides("row", taken, flags_ref)
    for t in range(th):
        halo_ref[t * slab : t * slab + ph, :] += low[t * ph : (t + 1) * ph]
        halo_ref[(t + 1) * slab - ph : (t + 1) * slab, :] += high[t * ph : (t + 1) * ph]


def split_slabs(th, th_n):
    if th_n > 2:
        return list(range(1, th - 1)), [0, th - 1]
    at = lax.axis_index("th")
    return [i + at for i in range(th - 1)], [(th - 1) * (1 - at)]


def groups_of(slabs, slab):
    return [
        pl.multiple_of(s * slab + i, 2 * GROUP) if not isinstance(s, int) else s * slab + i
        for s in slabs
        for i in range(0, slab, 2 * GROUP)
    ]


def first_kernel(ph, th, names, sizes, right_ref, conduct_ref, coupling_ref, codes_ref, inverse_ref, *rest):
    flags_ref, krylov_ref, conducts_ref, diagonal_ref, mixing_ref, held_ref, d_ref, *sent = rest[: 7 + len(names)]
    right, conduct, coupling, codes, turn, sems = rest[7 + len(names) :]
    rows = d_ref.shape[0]
    slab = rows // th
    pairs = [(right_ref, right), (coupling_ref, coupling), (codes_ref, codes), (conduct_ref, conduct)]
    parts = [pl.ds(t, th // 2) for t in range(0, th, th // 2)]
    pairs += [(inverse_ref.at[:, part], held_ref.at[:, part]) for part in parts]
    copies = [pltpu.make_async_copy(a, b, sems.at[i]) for i, (a, b) in enumerate(pairs)]
    for copy in copies:
        copy.start()

    def mix():
        copies[1].wait()
        lane = lax.broadcasted_iota(jnp.int32, (1, LANES), 1)
        for m in range(VARS):
            line = jnp.zeros((1, LANES), jnp.float32)
            for k in range(VARS):
                line = jnp.where(lane // BLK == k, coupling[k, (k + m) % VARS], line)
            mixing_ref[m : m + 1, :] = line

    def ghosts():
        copies[2].wait()
        cell = lax.broadcasted_iota(jnp.int32, (slab, LANES), 1) % BLK
        row = lax.broadcasted_iota(jnp.int32, (slab, LANES), 0)
        for t in range(th):
            diagonal = jnp.full((slab, LANES), 6.0, jnp.float32)
            for side, (edge, first, has) in enumerate(((0, 0, 3), (BLK - 1, slab - ph, 4))):
                factor = jnp.zeros((slab, LANES), jnp.float32)
                for p in range(ph):
                    code = codes[side, p, t]
                    value = jnp.where(code == 1, 1.0, jnp.where(code == 2, -1.0, 0.0))
                    factor = jnp.where(row == first + p, value, factor)
                diagonal -= jnp.where((cell == edge) & (flags_ref[has : has + 1, :] < 0.5), factor, 0.0)
            diagonal_ref[t * slab : (t + 1) * slab, :] = diagonal

    def lay_out():
        copies[3].wait()
        conducts_ref[...] = to_rows(conduct, turn)

    (row_at, row_n), (th_at, th_n), (ph_at, ph_n) = [(lax.axis_index(axis), n) for axis, n in sizes]
    values = [ph_at % 2, row_at % 2, th_at % 2, row_at > 0, row_at < row_n - 1, th_at > 0, th_at < th_n - 1]
    for i, value in enumerate(values):
        flags_ref[i : i + 1, :] = jnp.full((1, LANES), value.astype(jnp.float32))
    copies[0].wait()
    krylov_ref[...] = to_rows(right, turn)
    mix()
    ghosts()
    lay_out()
    for i, copy in enumerate(copies[4:]):
        copy.wait()
        for first in range(i * rows // 2, (i + 1) * rows // 2, 2 * GROUP):
            blocks = [held_ref[k % ph, k // slab, k % slab // ph] for k in range(first, first + 2 * GROUP)]
            d_ref[first : first + 2 * GROUP, :] = apply_stored(krylov_ref[first : first + 2 * GROUP, :], blocks)
    pack_faces(d_ref, dict(zip(names, sent)), flags_ref, ph, th)


def turn_kernel(held_ref, turned_ref):
    ph, th, nb = held_ref.shape[:3]
    for i in range(turned_ref.shape[0]):
        turned_ref[i] = held_ref[i % ph, i // (nb * ph), i % (nb * ph) // ph].T


def local_kernel(ph, th, krylov_ref, last_ref, conduct_ref, diagonal_ref, mixing_ref, out_ref):
    out_ref[...] = local_part(
        last_ref[...], krylov_ref[...], conduct_ref[...], diagonal_ref[...], mixing_ref, ph, th
    )


def gram_rows(left, right):
    lines = [jnp.sum(a * b, axis=0, keepdims=True) for a, b in zip(left, right)]
    return lines + [jnp.zeros_like(lines[0])] * (-len(lines) % 8)


def gram_kernel(*refs):
    basis = [ref[...] for ref in refs[:-1]]
    left = [basis[i] for i in range(S) for _ in range(i + 1)]
    right = [basis[j] for i in range(S) for j in range(i + 1)]
    refs[-1][...] = jnp.concatenate(gram_rows(left, right), axis=0)


def early_kernel(ph, th, th_n, names, flags_ref, local_ref, conduct_ref, turned_ref, *rest):
    next_ref, d_ref, halo_ref = rest[len(names) :]
    add_faces(halo_ref, dict(zip(names, rest)), flags_ref, ph, th)
    next_ref[...] = local_ref[...] - conduct_ref[...] * halo_ref[...]
    early, late = split_slabs(th, th_n)
    slab = d_ref.shape[0] // th
    apply_turned(next_ref, turned_ref, d_ref, groups_of(early, slab))
    for first in groups_of(late, slab):
        d_ref[pl.ds(first, 2 * GROUP), :] = jnp.zeros((2 * GROUP, LANES), jnp.float32)


def late_kernel(ph, th, th_n, names, late_names, flags_ref, early_ref, part_ref, conduct_ref, turned_ref, *rest):
    n = len(late_names)
    next_ref, d_ref, *sent = rest[n:]
    next_ref[...] = early_ref[...]
    d_ref[...] = part_ref[...]
    rows = d_ref.shape[0]
    slab = rows // th
    low, high = sides("th", dict(zip(late_names, rest)), flags_ref)
    _, late = split_slabs(th, th_n)
    faces = [low, high] if th_n > 2 else [low + high]
    for s, face in zip(late, faces):
        at = pl.ds(pl.multiple_of(s * slab, 2 * GROUP) if not isinstance(s, int) else s * slab, slab)
        next_ref[at, :] = early_ref[at, :] - conduct_ref[at, :] * face
    apply_turned(next_ref, turned_ref, d_ref, groups_of(late, slab))
    pack_faces(d_ref, dict(zip(names, sent)), flags_ref, ph, th)


def last_kernel(ph, th, names, flags_ref, local_ref, conduct_ref, partial_ref, *rest):
    older, taken, (next_ref, gram_ref, halo_ref) = rest[:S], rest[S : S + len(names)], rest[S + len(names) :]
    taken = dict(zip(names, taken))
    add_faces(halo_ref, taken, flags_ref, ph, th)
    low, high = sides("th", taken, flags_ref)
    rows = halo_ref.shape[0]
    slab = rows // th
    halo_ref[:slab, :] += low
    halo_ref[rows - slab :, :] += high
    final = local_ref[...] - conduct_ref[...] * halo_ref[...]
    next_ref[...] = final
    basis = [ref[...] for ref in older] + [final]
    stacked = jnp.concatenate([partial_ref[...]] + gram_rows([final] * (S + 1), basis), axis=0)
    each = jnp.sum(stacked, axis=1, keepdims=True)
    lane = lax.broadcasted_iota(jnp.int32, stacked.shape, 1)
    row = lax.broadcasted_iota(jnp.int32, stacked.shape, 0)
    line = jnp.sum(jnp.where(lane == row, each, 0.0), axis=0, keepdims=True)
    gram_ref[...] = jnp.broadcast_to(line, gram_ref.shape)


def small_solve(products):
    def entry(i, j):
        return products[max(i, j)][min(i, j)]

    def normal(j, k):
        return (entry(j, k) + entry(j + 1, k + 1)) + (entry(j + 1, k) + entry(j, k + 1))

    matrix = [[normal(j, k) for k in range(j + 1)] for j in range(S)]
    moment = [entry(j, 0) + entry(j + 1, 0) for j in range(S)]
    inverse = []
    for j in range(S):
        inverse.append(1.0 / matrix[j][j])
        scaled = {i: matrix[i][j] * inverse[j] for i in range(j + 1, S)}
        for i in range(j + 1, S):
            for k in range(j + 1, i + 1):
                matrix[i][k] = matrix[i][k] - scaled[i] * matrix[k][j]
            moment[i] = moment[i] - scaled[i] * moment[j]
    weights = [None] * S
    for i in reversed(range(S)):
        summed = moment[i]
        for k in range(i + 1, S):
            summed = summed - matrix[k][i] * weights[k]
        weights[i] = summed * inverse[i]
    return weights


def combine_kernel(partial_rows, gram_ref, *refs):
    krylov, directions, rest = refs[: S + 1], refs[S + 1 : 2 * S + 1], refs[2 * S + 1 :]
    correction_ref, residual_ref, correction, residual, turn, other_turn, sems = rest
    line = jnp.sum(gram_ref[...], axis=0, keepdims=True)
    products, place = [], 0
    for i in range(S + 1):
        products.append([])
        place = partial_rows if i == S else place
        for j in range(i + 1):
            products[i].append(jnp.broadcast_to(line[:, place : place + 1], line.shape))
            place += 1
    weights = small_solve(products)
    total = weights[0] * directions[0][...]
    for j in range(1, S):
        total = total + weights[j] * directions[j][...]
    left = krylov[0][...]
    for j in range(S):
        left = left - weights[j] * (krylov[j + 1][...] + krylov[j][...])
    from_rows(total, correction, turn)
    from_rows(left, residual, other_turn)
    copies = [
        pltpu.make_async_copy(correction, correction_ref, sems.at[0]),
        pltpu.make_async_copy(residual, residual_ref, sems.at[1]),
    ]
    for copy in copies:
        copy.start()
    for copy in copies:
        copy.wait()


def call(kernel, outs, scratch, *args, stay=()):
    def spec(a):
        return pl.BlockSpec(memory_space=pltpu.HBM if any(a is b for b in stay) else pltpu.VMEM)

    placed = [pltpu.with_memory_space_constraint(a, pltpu.HBM) if any(a is b for b in stay) else a for a in args]
    return pl.pallas_call(
        kernel,
        out_shape=outs,
        in_specs=[spec(a) for a in args],
        out_specs=[spec(a) for a in outs],
        scratch_shapes=scratch,
        compiler_params=pltpu.CompilerParams(vmem_limit_bytes=VMEM_LIMIT),
    )(*placed)


def local(right_side, conduct, coupling, inverse, face_codes):
    _, ph, th, radial = right_side.shape
    nb = radial // BLK
    per = ph * th
    rows = per * nb
    at = {axis: (lax.axis_index(axis), lax.axis_size(axis)) for axis in ("row", "th", "ph")}
    (row_at, row_n), (th_at, th_n), (ph_at, ph_n) = at["row"], at["th"], at["ph"]
    face_rows = {"ph_high": nb * th, "row_high": per, "ph_low": nb * th, "row_low": per // 2, "th_high": rows // th, "th_low": rows // th}
    if row_n == 2:
        face_rows.pop("row_high")
    if th_n == 2:
        face_rows.pop("th_high")
    names = tuple(face_rows)
    late_names = tuple(name for name in names if name[:2] == "th")
    packed = tuple(name for name in names if name != "row_low")
    def shape(n):
        return jax.ShapeDtypeStruct((n, LANES), jnp.float32)

    faces = [shape(face_rows[name]) for name in packed]
    whole = shape(rows)

    plans = {"low": pairs_low, "high": pairs_high}

    def exchange(sent, direction):
        (near,) = call(functools.partial(near_kernel, ph, th), [shape(face_rows["row_low"])], [], flags, direction)
        sent = dict(zip(packed, sent), row_low=near)
        taken = []
        for name in names:
            axis, side = name.split("_")
            face = lax.ppermute(sent[name], axis, plans[side](lax.axis_size(axis)))
            if name == "row_high":
                (face,) = call(across_kernel, [shape(per)], [], flags, face)
            taken.append(face)
        return taken

    field = pltpu.VMEM(right_side.shape, jnp.float32)
    turn = pltpu.VMEM((rows, LANES), jnp.float32)
    flags, start, conducts, diagonal, mixing, held, direction, *sent = call(
        functools.partial(first_kernel, ph, th, packed, (("row", row_n), ("th", th_n), ("ph", ph_n))),
        [shape(VARS), whole, whole, whole, shape(VARS), jax.ShapeDtypeStruct(inverse.shape, jnp.bfloat16), whole] + faces,
        [
            field,
            field,
            pltpu.SMEM(coupling.shape, jnp.float32),
            pltpu.SMEM(face_codes.shape, jnp.int32),
            turn,
            pltpu.SemaphoreType.DMA((6,)),
        ],
        right_side, conduct, coupling, face_codes, inverse,
        stay=(right_side, conduct, coupling, face_codes, inverse),
    )
    (turned,) = call(turn_kernel, [jax.ShapeDtypeStruct((rows, LANES, LANES), jnp.bfloat16)], [], held)
    krylov, directions = [start], [direction]
    for step in range(S):
        taken = exchange(sent, directions[-1])
        (beside,) = call(
            functools.partial(local_kernel, ph, th), [whole], [], krylov[-1], directions[-1], conducts, diagonal, mixing
        )
        if step < S - 1:
            early_names, early_taken = zip(*[(n, t) for n, t in zip(names, taken) if n not in late_names])
            early, part = call(
                functools.partial(early_kernel, ph, th, th_n, early_names),
                [whole, whole],
                [turn],
                flags, beside, conducts, turned, *early_taken,
            )
            following, direction, *sent = call(
                functools.partial(late_kernel, ph, th, th_n, packed, late_names),
                [whole, whole] + faces,
                [],
                flags, early, part, conducts, turned, *[t for n, t in zip(names, taken) if n in late_names],
            )
            krylov.append(following)
            directions.append(direction)
    partial_rows = S * (S + 1) // 2
    partial_rows += -partial_rows % 8
    (partial,) = call(gram_kernel, [shape(partial_rows)], [], *krylov)
    following, gram = call(
        functools.partial(last_kernel, ph, th, names),
        [whole, shape(row_n * th_n * ph_n)],
        [turn],
        flags, beside, conducts, partial, *krylov, *taken,
    )
    krylov.append(following)
    gram = lax.all_to_all(gram, ("row", "th", "ph"), 0, 0, tiled=True)
    native = [jax.ShapeDtypeStruct(right_side.shape, jnp.float32)] * 2
    return tuple(
        call(
            functools.partial(combine_kernel, partial_rows),
            native,
            [field, field, turn, turn, pltpu.SemaphoreType.DMA((2,))],
            gram, *krylov, *directions,
            stay=native,
        )
    )


def solution(mesh):
    placed = (
        P(None, "ph", "th", "row"),
        P(None, "ph", "th", "row"),
        P(),
        P("ph", "th", "row", None, None),
        P(None, "ph", "th"),
    )
    return jax.shard_map(
        local,
        mesh=mesh,
        in_specs=placed,
        out_specs=(P(None, "ph", "th", "row"), P(None, "ph", "th", "row")),
        check_vma=False,
    )
```

```python
import functools

import jax
import jax.numpy as jnp
from jax import lax
from jax.experimental import pallas as pl
from jax.experimental.pallas import tpu as pltpu
from jax.sharding import PartitionSpec as P

VARS = 8
BLK = 16
S = 4
LANES = VARS * BLK
GROUP = 8
VMEM_LIMIT = 24 * 1024 * 1024


def pairs_low(count):
    return [(i, i ^ 1) for i in range(count)]


def pairs_high(count):
    return [(i, (i + 1) % count if i % 2 else (i - 1) % count) for i in range(count)]


def to_rows(native_ref, turn_ref):
    var, ph, th, radial = native_ref.shape
    planes = [jnp.concatenate([native_ref[v, p] for p in range(ph)], axis=0) for v in range(var)]
    for b in range(radial // BLK):
        turn_ref[b * ph * th : (b + 1) * ph * th, :] = jnp.concatenate(
            [plane[:, b * BLK : (b + 1) * BLK] for plane in planes], axis=1
        )
    slab = turn_ref.shape[0] // th
    return jnp.concatenate([turn_ref[pl.ds(t, slab, stride=th), :] for t in range(th)], axis=0)


def from_rows(rows, native_ref, turn_ref):
    var, ph, th, radial = native_ref.shape
    slab = rows.shape[0] // th
    for t in range(th):
        turn_ref[pl.ds(t, slab, stride=th), :] = rows[t * slab : (t + 1) * slab]
    turned = turn_ref[...]
    per = ph * th
    for v in range(var):
        plane = jnp.concatenate(
            [turned[b * per : (b + 1) * per, v * BLK : (v + 1) * BLK] for b in range(radial // BLK)], axis=1
        )
        for p in range(ph):
            native_ref[v, p] = plane[p * th : (p + 1) * th]


def spread_rows(vectors):
    rounded = vectors.astype(jnp.bfloat16)
    row = lax.broadcasted_iota(jnp.int32, rounded.shape, 0) % GROUP
    return jnp.concatenate(
        [jnp.where(row == m, rounded, jnp.zeros_like(rounded)) for m in range(GROUP)], axis=1
    )


def own_halves(out):
    return jnp.concatenate([out[:GROUP, :LANES], out[GROUP:, LANES:]], axis=0)


def apply_stored(vectors, blocks):
    halves = [jnp.concatenate(blocks[half * GROUP : (half + 1) * GROUP], axis=1) for half in range(2)]
    out = lax.dot_general(
        spread_rows(vectors),
        jnp.concatenate(halves, axis=0),
        (((1,), (1,)), ((), ())),
        preferred_element_type=jnp.float32,
    )
    return own_halves(out)


def apply_turned(field_ref, turned_ref, out_ref, firsts):
    for first in firsts:
        halves = [
            jnp.concatenate([turned_ref[first + half * GROUP + m] for m in range(GROUP)], axis=0) for half in range(2)
        ]
        out = jnp.dot(
            spread_rows(field_ref[pl.ds(first, 2 * GROUP), :]),
            jnp.concatenate(halves, axis=1),
            preferred_element_type=jnp.float32,
        )
        out_ref[pl.ds(first, 2 * GROUP), :] = own_halves(out)


def pack_faces(d_ref, outs, flags_ref, ph, th):
    rows = d_ref.shape[0]
    slab = rows // th
    odd_ph, odd_row, odd_th = [flags_ref[i : i + 1, :] > 0.5 for i in range(3)]
    low = d_ref[pl.ds(0, rows // ph, stride=ph), :]
    high = d_ref[pl.ds(ph - 1, rows // ph, stride=ph), :]
    outs["ph_high"][...] = jnp.where(odd_ph, high, low)
    outs["ph_low"][...] = jnp.where(odd_ph, low, high)
    if "row_high" in outs:
        for t in range(th):
            low, high = radial_edges(d_ref, t, slab, ph)
            outs["row_high"][t * ph : (t + 1) * ph, :] = jnp.where(odd_row, high, low)
    low, high = d_ref[:slab, :], d_ref[rows - slab :, :]
    outs["th_low"][...] = jnp.where(odd_th, low, high)
    if "th_high" in outs:
        outs["th_high"][...] = jnp.where(odd_th, high, low)


def radial_edges(d_ref, t, slab, ph):
    return d_ref[t * slab : t * slab + ph, :], d_ref[(t + 1) * slab - ph : (t + 1) * slab, :]


def near_kernel(ph, th, flags_ref, d_ref, out_ref):
    slab = d_ref.shape[0] // th
    half = out_ref.shape[0]
    low, high = [jnp.concatenate(side, axis=0) for side in zip(*[radial_edges(d_ref, t, slab, ph) for t in range(th)])]
    cell = lax.broadcasted_iota(jnp.int32, (half, LANES), 1) % BLK
    low = jnp.where(cell == BLK - 1, pltpu.roll(low[:half], BLK - 1, 1), 0.0) + jnp.where(
        cell == 0, pltpu.roll(low[half:], BLK, 1), 0.0
    )
    high = jnp.where(cell == 0, pltpu.roll(high[:half], LANES - BLK + 1, 1), 0.0) + jnp.where(
        cell == 1, pltpu.roll(high[half:], LANES - BLK + 2, 1), 0.0
    )
    out_ref[...] = jnp.where(flags_ref[1:2, :] > 0.5, low, high)


def radial_kernel(ph, th, names, flags_ref, local_ref, conduct_ref, *rest):
    taken, out_ref = dict(zip(names, rest)), rest[-1]
    slab = out_ref.shape[0] // th
    odd, has_low, has_high = [flags_ref[i : i + 1, :] > 0.5 for i in (1, 3, 4)]
    near = taken["row_low"][...]
    edge = lax.broadcasted_iota(jnp.int32, near.shape, 1) % BLK == jnp.where(odd, 0, BLK - 1)
    near = jnp.concatenate([jnp.where(edge, part, 0.0) for part in (near, pltpu.roll(near, LANES - 1, 1))], axis=0)
    below = above = jnp.zeros_like(near)
    if "row_high" in taken:
        face = taken["row_high"][...]
        cell = lax.broadcasted_iota(jnp.int32, face.shape, 1) % BLK
        below = jnp.where(cell == 0, pltpu.roll(face, LANES - BLK + 1, 1), 0.0)
        above = jnp.where(cell == BLK - 1, pltpu.roll(face, BLK - 1, 1), 0.0)
    low = jnp.where(has_low, jnp.where(odd, near, below), 0.0)
    high = jnp.where(has_high, jnp.where(odd, above, near), 0.0)
    out_ref[...] = local_ref[...]
    for t in range(th):
        for first, side in ((t * slab, low), ((t + 1) * slab - ph, high)):
            at = pl.ds(first, ph)
            out_ref[at, :] = local_ref[at, :] - conduct_ref[at, :] * side[t * ph : (t + 1) * ph]


def local_part(field, krylov, conduct, diagonal, mixing_ref, ph, th):
    rows = field.shape[0]
    slab = rows // th
    nb = slab // ph
    lane = lax.broadcasted_iota(jnp.int32, (rows, LANES), 1)
    row = lax.broadcasted_iota(jnp.int32, (rows, LANES), 0)
    cell = lane % BLK
    azimuth = row % ph
    block = (row // ph) % nb
    mixed = field * mixing_ref[0:1, :]
    for m in range(1, VARS):
        mixed += pltpu.roll(field, LANES - BLK * m, 1) * mixing_ref[m : m + 1, :]
    from_low = pltpu.roll(pltpu.roll(field, LANES - BLK + 1, 1), ph, 0)
    from_high = pltpu.roll(pltpu.roll(field, BLK - 1, 1), rows - ph, 0)
    total = jnp.where(cell == 0, jnp.where(block == 0, 0.0, from_low), pltpu.roll(field, 1, 1))
    total += jnp.where(
        cell == BLK - 1, jnp.where(block == nb - 1, 0.0, from_high), pltpu.roll(field, LANES - 1, 1)
    )
    total += jnp.where(azimuth == 0, 0.0, pltpu.roll(field, 1, 0))
    total += jnp.where(azimuth == ph - 1, 0.0, pltpu.roll(field, rows - 1, 0))
    zero = jnp.zeros((slab, LANES), jnp.float32)
    total += jnp.concatenate([zero, field[: rows - slab]], axis=0)
    total += jnp.concatenate([field[slab:], zero], axis=0)
    return field + mixed + conduct * (diagonal * field - total) - krylov


def sides(axis, taken, flags_ref):
    parity, has_low, has_high = {"ph": (0, None, None), "th": (2, 5, 6)}[axis]
    odd = flags_ref[parity : parity + 1, :] > 0.5
    first = taken[axis + "_low"][...]
    second = taken[axis + "_high"][...] if axis + "_high" in taken else jnp.zeros_like(first)
    low, high = jnp.where(odd, first, second), jnp.where(odd, second, first)
    if has_low is None:
        return low, high
    low = jnp.where(flags_ref[has_low : has_low + 1, :] > 0.5, low, 0.0)
    return low, jnp.where(flags_ref[has_high : has_high + 1, :] > 0.5, high, 0.0)


def take_azimuthal(out_ref, local_ref, conduct_ref, taken, flags_ref, ph):
    rows = out_ref.shape[0]
    low, high = sides("ph", taken, flags_ref)
    out_ref[...] = local_ref[...]
    for first, side in ((0, low), (ph - 1, high)):
        at = pl.ds(first, rows // ph, stride=ph)
        out_ref[at, :] = local_ref[at, :] - conduct_ref[at, :] * side


def split_slabs(th, th_n):
    if th_n > 2:
        return list(range(1, th - 1)), [0, th - 1]
    at = lax.axis_index("th")
    return [i + at for i in range(th - 1)], [(th - 1) * (1 - at)]


def groups_of(slabs, slab):
    return [
        pl.multiple_of(s * slab + i, 2 * GROUP) if not isinstance(s, int) else s * slab + i
        for s in slabs
        for i in range(0, slab, 2 * GROUP)
    ]


def first_kernel(ph, th, names, sizes, right_ref, conduct_ref, coupling_ref, codes_ref, inverse_ref, *rest):
    flags_ref, krylov_ref, conducts_ref, diagonal_ref, mixing_ref, held_ref, right, d_ref, *sent = rest[: 8 + len(names)]
    conduct, coupling, codes, turn, sems = rest[8 + len(names) :]
    rows = d_ref.shape[0]
    slab = rows // th
    pairs = [(right_ref, right), (coupling_ref, coupling), (codes_ref, codes), (conduct_ref, conduct)]
    parts = [pl.ds(t, th // 2) for t in range(0, th, th // 2)]
    pairs += [(inverse_ref.at[:, part], held_ref.at[:, part]) for part in parts]
    copies = [pltpu.make_async_copy(a, b, sems.at[i]) for i, (a, b) in enumerate(pairs)]
    for copy in copies:
        copy.start()

    def mix():
        copies[1].wait()
        lane = lax.broadcasted_iota(jnp.int32, (1, LANES), 1)
        for m in range(VARS):
            line = jnp.zeros((1, LANES), jnp.float32)
            for k in range(VARS):
                line = jnp.where(lane // BLK == k, coupling[k, (k + m) % VARS], line)
            mixing_ref[m : m + 1, :] = line

    def ghosts():
        copies[2].wait()
        cell = lax.broadcasted_iota(jnp.int32, (slab, LANES), 1) % BLK
        row = lax.broadcasted_iota(jnp.int32, (slab, LANES), 0)
        for t in range(th):
            diagonal = jnp.full((slab, LANES), 6.0, jnp.float32)
            for side, (edge, first, has) in enumerate(((0, 0, 3), (BLK - 1, slab - ph, 4))):
                factor = jnp.zeros((slab, LANES), jnp.float32)
                for p in range(ph):
                    code = codes[side, p, t]
                    value = jnp.where(code == 1, 1.0, jnp.where(code == 2, -1.0, 0.0))
                    factor = jnp.where(row == first + p, value, factor)
                diagonal -= jnp.where((cell == edge) & (flags_ref[has : has + 1, :] < 0.5), factor, 0.0)
            diagonal_ref[t * slab : (t + 1) * slab, :] = diagonal

    def lay_out():
        copies[3].wait()
        conducts_ref[...] = to_rows(conduct, turn)

    (row_at, row_n), (th_at, th_n), (ph_at, ph_n) = [(lax.axis_index(axis), n) for axis, n in sizes]
    values = [ph_at % 2, row_at % 2, th_at % 2, row_at > 0, row_at < row_n - 1, th_at > 0, th_at < th_n - 1]
    for i, value in enumerate(values):
        flags_ref[i : i + 1, :] = jnp.full((1, LANES), value.astype(jnp.float32))
    copies[0].wait()
    krylov_ref[...] = to_rows(right, turn)
    mix()
    ghosts()
    lay_out()
    for i, copy in enumerate(copies[4:]):
        copy.wait()
        for first in range(i * rows // 2, (i + 1) * rows // 2, 2 * GROUP):
            blocks = [held_ref[k % ph, k // slab, k % slab // ph] for k in range(first, first + 2 * GROUP)]
            d_ref[first : first + 2 * GROUP, :] = apply_stored(krylov_ref[first : first + 2 * GROUP, :], blocks)
    pack_faces(d_ref, dict(zip(names, sent)), flags_ref, ph, th)


def turn_kernel(held_ref, turned_ref):
    ph, th, nb = held_ref.shape[:3]
    for i in range(turned_ref.shape[0]):
        turned_ref[i] = held_ref[i % ph, i // (nb * ph), i % (nb * ph) // ph].T


def local_kernel(ph, th, count, krylov_ref, last_ref, conduct_ref, diagonal_ref, mixing_ref, *rest):
    fields, (out_ref, *natives), turns = rest[:count], rest[count : 2 * count + 1], rest[2 * count + 1 :]
    out_ref[...] = local_part(
        last_ref[...], krylov_ref[...], conduct_ref[...], diagonal_ref[...], mixing_ref, ph, th
    )
    for field_ref, native_ref, turn_ref in zip(fields, natives, turns):
        from_rows(field_ref[...], native_ref, turn_ref)


def gram_rows(left, right):
    lines = [jnp.sum(a * b, axis=0, keepdims=True) for a, b in zip(left, right)]
    return lines + [jnp.zeros_like(lines[0])] * (-len(lines) % 8)


def gram_kernel(*refs):
    basis = [ref[...] for ref in refs[:-1]]
    left = [basis[i] for i in range(S) for _ in range(i + 1)]
    right = [basis[j] for i in range(S) for j in range(i + 1)]
    refs[-1][...] = jnp.concatenate(gram_rows(left, right), axis=0)


def early_kernel(ph, th, th_n, names, flags_ref, local_ref, conduct_ref, turned_ref, *rest):
    next_ref, d_ref = rest[len(names) :]
    take_azimuthal(next_ref, local_ref, conduct_ref, dict(zip(names, rest)), flags_ref, ph)
    early, late = split_slabs(th, th_n)
    slab = d_ref.shape[0] // th
    apply_turned(next_ref, turned_ref, d_ref, groups_of(early, slab))
    for first in groups_of(late, slab):
        d_ref[pl.ds(first, 2 * GROUP), :] = jnp.zeros((2 * GROUP, LANES), jnp.float32)


def late_kernel(ph, th, th_n, names, late_names, flags_ref, early_ref, part_ref, conduct_ref, turned_ref, *rest):
    n = len(late_names)
    next_ref, d_ref, *sent = rest[n:]
    next_ref[...] = early_ref[...]
    d_ref[...] = part_ref[...]
    rows = d_ref.shape[0]
    slab = rows // th
    low, high = sides("th", dict(zip(late_names, rest)), flags_ref)
    _, late = split_slabs(th, th_n)
    faces = [low, high] if th_n > 2 else [low + high]
    for s, face in zip(late, faces):
        at = pl.ds(pl.multiple_of(s * slab, 2 * GROUP) if not isinstance(s, int) else s * slab, slab)
        next_ref[at, :] = early_ref[at, :] - conduct_ref[at, :] * face
    apply_turned(next_ref, turned_ref, d_ref, groups_of(late, slab))
    pack_faces(d_ref, dict(zip(names, sent)), flags_ref, ph, th)


def last_kernel(ph, th, names, flags_ref, local_ref, conduct_ref, partial_ref, *rest):
    older, taken, (next_ref, gram_ref) = rest[:S], rest[S : S + len(names)], rest[S + len(names) :]
    taken = dict(zip(names, taken))
    take_azimuthal(next_ref, local_ref, conduct_ref, taken, flags_ref, ph)
    low, high = sides("th", taken, flags_ref)
    rows = next_ref.shape[0]
    slab = rows // th
    for at, side in ((pl.ds(0, slab), low), (pl.ds(rows - slab, slab), high)):
        next_ref[at, :] = next_ref[at, :] - conduct_ref[at, :] * side
    final = next_ref[...]
    basis = [ref[...] for ref in older] + [final]
    stacked = jnp.concatenate([partial_ref[...]] + gram_rows([final] * (S + 1), basis), axis=0)
    each = jnp.sum(stacked, axis=1, keepdims=True)
    lane = lax.broadcasted_iota(jnp.int32, stacked.shape, 1)
    row = lax.broadcasted_iota(jnp.int32, stacked.shape, 0)
    line = jnp.sum(jnp.where(lane == row, each, 0.0), axis=0, keepdims=True)
    gram_ref[...] = jnp.broadcast_to(line, gram_ref.shape)


def small_solve(products):
    def entry(i, j):
        return products[max(i, j)][min(i, j)]

    def normal(j, k):
        return (entry(j, k) + entry(j + 1, k + 1)) + (entry(j + 1, k) + entry(j, k + 1))

    matrix = [[normal(j, k) for k in range(j + 1)] for j in range(S)]
    moment = [entry(j, 0) + entry(j + 1, 0) for j in range(S)]
    inverse = []
    for j in range(S):
        inverse.append(1.0 / matrix[j][j])
        scaled = {i: matrix[i][j] * inverse[j] for i in range(j + 1, S)}
        for i in range(j + 1, S):
            for k in range(j + 1, i + 1):
                matrix[i][k] = matrix[i][k] - scaled[i] * matrix[k][j]
            moment[i] = moment[i] - scaled[i] * moment[j]
    weights = [None] * S
    for i in reversed(range(S)):
        summed = moment[i]
        for k in range(i + 1, S):
            summed = summed - matrix[k][i] * weights[k]
        weights[i] = summed * inverse[i]
    return weights


def combine_kernel(partial_rows, gram_ref, final_ref, *refs):
    krylov, directions, rest = refs[:S], refs[S : 2 * S], refs[2 * S :]
    correction_ref, residual_ref, correction, residual, newest, turn, sems = rest
    from_rows(final_ref[...], newest, turn)
    krylov = [*krylov, newest]
    line = jnp.sum(gram_ref[...], axis=0, keepdims=True)
    products, place = [], 0
    for i in range(S + 1):
        products.append([])
        place = partial_rows if i == S else place
        for j in range(i + 1):
            products[i].append(jnp.broadcast_to(line[:, place : place + 1], line.shape))
            place += 1
    weights = small_solve(products)
    weights = [weight[:, : correction.shape[-1]] for weight in weights]
    for v in range(correction.shape[0]):
        total = weights[0] * directions[0][v]
        left = krylov[0][v]
        for j in range(S):
            if j:
                total = total + weights[j] * directions[j][v]
            left = left - weights[j] * (krylov[j + 1][v] + krylov[j][v])
        correction[v] = total
        residual[v] = left
    copies = [
        pltpu.make_async_copy(correction, correction_ref, sems.at[0]),
        pltpu.make_async_copy(residual, residual_ref, sems.at[1]),
    ]
    for copy in copies:
        copy.start()
    for copy in copies:
        copy.wait()


def call(kernel, outs, scratch, *args, stay=()):
    def spec(a):
        return pl.BlockSpec(memory_space=pltpu.HBM if any(a is b for b in stay) else pltpu.VMEM)

    placed = [pltpu.with_memory_space_constraint(a, pltpu.HBM) if any(a is b for b in stay) else a for a in args]
    return pl.pallas_call(
        kernel,
        out_shape=outs,
        in_specs=[spec(a) for a in args],
        out_specs=[spec(a) for a in outs],
        scratch_shapes=scratch,
        compiler_params=pltpu.CompilerParams(vmem_limit_bytes=VMEM_LIMIT),
    )(*placed)


def local(right_side, conduct, coupling, inverse, face_codes):
    _, ph, th, radial = right_side.shape
    nb = radial // BLK
    per = ph * th
    rows = per * nb
    at = {axis: (lax.axis_index(axis), lax.axis_size(axis)) for axis in ("row", "th", "ph")}
    (row_at, row_n), (th_at, th_n), (ph_at, ph_n) = at["row"], at["th"], at["ph"]
    face_rows = {"ph_high": nb * th, "row_high": per, "ph_low": nb * th, "row_low": per // 2, "th_high": rows // th, "th_low": rows // th}
    if row_n == 2:
        face_rows.pop("row_high")
    if th_n == 2:
        face_rows.pop("th_high")
    names = tuple(face_rows)
    late_names = tuple(name for name in names if name[:2] == "th")
    packed = tuple(name for name in names if name != "row_low")
    early_names = tuple(name for name in names if name[:2] == "ph")
    radial_names = tuple(name for name in names if name[:3] == "row")
    def shape(n):
        return jax.ShapeDtypeStruct((n, LANES), jnp.float32)

    faces = [shape(face_rows[name]) for name in packed]
    whole = shape(rows)

    plans = {"low": pairs_low, "high": pairs_high}

    def exchange(sent, direction):
        (near,) = call(functools.partial(near_kernel, ph, th), [shape(face_rows["row_low"])], [], flags, direction)
        sent = dict(zip(packed, sent), row_low=near)
        taken = []
        for name in names:
            axis, side = name.split("_")
            taken.append(lax.ppermute(sent[name], axis, plans[side](lax.axis_size(axis))))
        return taken

    field = pltpu.VMEM(right_side.shape, jnp.float32)
    native = jax.ShapeDtypeStruct(right_side.shape, jnp.float32)
    turn = pltpu.VMEM((rows, LANES), jnp.float32)
    flags, start, conducts, diagonal, mixing, held, right_native, direction, *sent = call(
        functools.partial(first_kernel, ph, th, packed, (("row", row_n), ("th", th_n), ("ph", ph_n))),
        [shape(VARS), whole, whole, whole, shape(VARS), jax.ShapeDtypeStruct(inverse.shape, jnp.bfloat16), native, whole] + faces,
        [
            field,
            pltpu.SMEM(coupling.shape, jnp.float32),
            pltpu.SMEM(face_codes.shape, jnp.int32),
            turn,
            pltpu.SemaphoreType.DMA((6,)),
        ],
        right_side, conduct, coupling, face_codes, inverse,
        stay=(right_side, conduct, coupling, face_codes, inverse),
    )
    (turned,) = call(turn_kernel, [jax.ShapeDtypeStruct((rows, LANES, LANES), jnp.bfloat16)], [], held)
    krylov, directions = [start], [direction]
    krylov_native, direction_native = [right_native], []
    for step in range(S):
        taken = exchange(sent, directions[-1])
        ready = [] if step == 0 else [krylov[-1], directions[-1]] + directions[:1] * (step == 1)
        beside, *laid = call(
            functools.partial(local_kernel, ph, th, len(ready)),
            [whole] + [native] * len(ready),
            [turn] * len(ready),
            krylov[-1], directions[-1], conducts, diagonal, mixing, *ready,
        )
        if laid:
            krylov_native.append(laid[0])
            direction_native += laid[:0:-1]
        taken = dict(zip(names, taken))

        def of(some):
            return [taken[name] for name in some]

        (beside,) = call(
            functools.partial(radial_kernel, ph, th, radial_names), [whole], [], flags, beside, conducts, *of(radial_names)
        )
        if step < S - 1:
            early, part = call(
                functools.partial(early_kernel, ph, th, th_n, early_names),
                [whole, whole],
                [],
                flags, beside, conducts, turned, *of(early_names),
            )
            following, direction, *sent = call(
                functools.partial(late_kernel, ph, th, th_n, packed, late_names),
                [whole, whole] + faces,
                [],
                flags, early, part, conducts, turned, *of(late_names),
            )
            krylov.append(following)
            directions.append(direction)
    partial_rows = S * (S + 1) // 2
    partial_rows += -partial_rows % 8
    (partial,) = call(gram_kernel, [shape(partial_rows)], [], *krylov)
    following, gram = call(
        functools.partial(last_kernel, ph, th, early_names + late_names),
        [whole, shape(row_n * th_n * ph_n)],
        [],
        flags, beside, conducts, partial, *krylov, *of(early_names + late_names),
    )
    krylov.append(following)
    gram = lax.all_to_all(gram, ("row", "th", "ph"), 0, 0, tiled=True)
    results = [native, jax.ShapeDtypeStruct(right_side.shape, jnp.float32)]
    return tuple(
        call(
            functools.partial(combine_kernel, partial_rows),
            results,
            [field, field, field, turn, pltpu.SemaphoreType.DMA((2,))],
            gram, following, *krylov_native, *direction_native,
            stay=results,
        )
    )


def solution(mesh):
    placed = (
        P(None, "ph", "th", "row"),
        P(None, "ph", "th", "row"),
        P(),
        P("ph", "th", "row", None, None),
        P(None, "ph", "th"),
    )
    return jax.shard_map(
        local,
        mesh=mesh,
        in_specs=placed,
        out_specs=(P(None, "ph", "th", "row"), P(None, "ph", "th", "row")),
        check_vma=False,
    )
```

```python
import functools

import jax
import jax.numpy as jnp
from jax import lax
from jax.experimental import pallas as pl
from jax.experimental.pallas import tpu as pltpu
from jax.sharding import PartitionSpec as P

VARS = 8
BLK = 16
S = 4
LANES = VARS * BLK
GROUP = 8
VMEM_LIMIT = 24 * 1024 * 1024


def pairs_low(count):
    return [(i, i ^ 1) for i in range(count)]


def pairs_high(count):
    return [(i, (i + 1) % count if i % 2 else (i - 1) % count) for i in range(count)]


def to_rows(native_ref, turn_ref):
    var, ph, th, radial = native_ref.shape
    planes = [jnp.concatenate([native_ref[v, p] for p in range(ph)], axis=0) for v in range(var)]
    for b in range(radial // BLK):
        turn_ref[b * ph * th : (b + 1) * ph * th, :] = jnp.concatenate(
            [plane[:, b * BLK : (b + 1) * BLK] for plane in planes], axis=1
        )
    slab = turn_ref.shape[0] // th
    return jnp.concatenate([turn_ref[pl.ds(t, slab, stride=th), :] for t in range(th)], axis=0)


def from_rows(rows, native_ref, turn_ref):
    var, ph, th, radial = native_ref.shape
    slab = rows.shape[0] // th
    for t in range(th):
        turn_ref[pl.ds(t, slab, stride=th), :] = rows[t * slab : (t + 1) * slab]
    turned = turn_ref[...]
    per = ph * th
    for v in range(var):
        plane = jnp.concatenate(
            [turned[b * per : (b + 1) * per, v * BLK : (v + 1) * BLK] for b in range(radial // BLK)], axis=1
        )
        for p in range(ph):
            native_ref[v, p] = plane[p * th : (p + 1) * th]


def spread_rows(vectors):
    rounded = vectors.astype(jnp.bfloat16)
    row = lax.broadcasted_iota(jnp.int32, rounded.shape, 0) % GROUP
    return jnp.concatenate(
        [jnp.where(row == m, rounded, jnp.zeros_like(rounded)) for m in range(GROUP)], axis=1
    )


def own_halves(out):
    return jnp.concatenate([out[:GROUP, :LANES], out[GROUP:, LANES:]], axis=0)


def apply_stored(vectors, blocks):
    halves = [jnp.concatenate(blocks[half * GROUP : (half + 1) * GROUP], axis=1) for half in range(2)]
    out = lax.dot_general(
        spread_rows(vectors),
        jnp.concatenate(halves, axis=0),
        (((1,), (1,)), ((), ())),
        preferred_element_type=jnp.float32,
    )
    return own_halves(out)


def apply_turned(field_ref, turned_ref, out_ref, firsts):
    for first in firsts:
        halves = [
            jnp.concatenate([turned_ref[first + half * GROUP + m] for m in range(GROUP)], axis=0) for half in range(2)
        ]
        out = jnp.dot(
            spread_rows(field_ref[pl.ds(first, 2 * GROUP), :]),
            jnp.concatenate(halves, axis=1),
            preferred_element_type=jnp.float32,
        )
        out_ref[pl.ds(first, 2 * GROUP), :] = own_halves(out)


def pack_faces(d_ref, outs, flags_ref, ph, th):
    rows = d_ref.shape[0]
    slab = rows // th
    odd_ph, odd_row, odd_th = [flags_ref[i : i + 1, :] > 0.5 for i in range(3)]
    low = d_ref[pl.ds(0, rows // ph, stride=ph), :]
    high = d_ref[pl.ds(ph - 1, rows // ph, stride=ph), :]
    outs["ph_high"][...] = jnp.where(odd_ph, high, low)
    outs["ph_low"][...] = jnp.where(odd_ph, low, high)
    if "row_high" in outs:
        for t in range(th):
            low, high = radial_edges(d_ref, t, slab, ph)
            outs["row_high"][t * ph : (t + 1) * ph, :] = jnp.where(odd_row, high, low)
    low, high = d_ref[:slab, :], d_ref[rows - slab :, :]
    outs["th_low"][...] = jnp.where(odd_th, low, high)
    if "th_high" in outs:
        outs["th_high"][...] = jnp.where(odd_th, high, low)


def radial_edges(d_ref, t, slab, ph):
    return d_ref[t * slab : t * slab + ph, :], d_ref[(t + 1) * slab - ph : (t + 1) * slab, :]


def near_kernel(ph, th, flags_ref, d_ref, out_ref):
    slab = d_ref.shape[0] // th
    half = out_ref.shape[0]
    low, high = [jnp.concatenate(side, axis=0) for side in zip(*[radial_edges(d_ref, t, slab, ph) for t in range(th)])]
    cell = lax.broadcasted_iota(jnp.int32, (half, LANES), 1) % BLK
    low = jnp.where(cell == BLK - 1, pltpu.roll(low[:half], BLK - 1, 1), 0.0) + jnp.where(
        cell == 0, pltpu.roll(low[half:], BLK, 1), 0.0
    )
    high = jnp.where(cell == 0, pltpu.roll(high[:half], LANES - BLK + 1, 1), 0.0) + jnp.where(
        cell == 1, pltpu.roll(high[half:], LANES - BLK + 2, 1), 0.0
    )
    out_ref[...] = jnp.where(flags_ref[1:2, :] > 0.5, low, high)


def radial_kernel(ph, th, names, flags_ref, local_ref, conduct_ref, *rest):
    taken, out_ref = dict(zip(names, rest)), rest[-1]
    slab = out_ref.shape[0] // th
    odd, has_low, has_high = [flags_ref[i : i + 1, :] > 0.5 for i in (1, 3, 4)]
    near = taken["row_low"][...]
    edge = lax.broadcasted_iota(jnp.int32, near.shape, 1) % BLK == jnp.where(odd, 0, BLK - 1)
    near = jnp.concatenate([jnp.where(edge, part, 0.0) for part in (near, pltpu.roll(near, LANES - 1, 1))], axis=0)
    below = above = jnp.zeros_like(near)
    if "row_high" in taken:
        face = taken["row_high"][...]
        cell = lax.broadcasted_iota(jnp.int32, face.shape, 1) % BLK
        below = jnp.where(cell == 0, pltpu.roll(face, LANES - BLK + 1, 1), 0.0)
        above = jnp.where(cell == BLK - 1, pltpu.roll(face, BLK - 1, 1), 0.0)
    low = jnp.where(has_low, jnp.where(odd, near, below), 0.0)
    high = jnp.where(has_high, jnp.where(odd, above, near), 0.0)
    out_ref[...] = local_ref[...]
    for t in range(th):
        for first, side in ((t * slab, low), ((t + 1) * slab - ph, high)):
            at = pl.ds(first, ph)
            out_ref[at, :] = local_ref[at, :] - conduct_ref[at, :] * side[t * ph : (t + 1) * ph]


def local_part(field, krylov, conduct, diagonal, mixing_ref, ph, th):
    rows = field.shape[0]
    slab = rows // th
    nb = slab // ph
    lane = lax.broadcasted_iota(jnp.int32, (rows, LANES), 1)
    row = lax.broadcasted_iota(jnp.int32, (rows, LANES), 0)
    cell = lane % BLK
    azimuth = row % ph
    block = (row // ph) % nb
    mixed = field * mixing_ref[0:1, :]
    for m in range(1, VARS):
        mixed += pltpu.roll(field, LANES - BLK * m, 1) * mixing_ref[m : m + 1, :]
    from_low = pltpu.roll(pltpu.roll(field, LANES - BLK + 1, 1), ph, 0)
    from_high = pltpu.roll(pltpu.roll(field, BLK - 1, 1), rows - ph, 0)
    total = jnp.where(cell == 0, jnp.where(block == 0, 0.0, from_low), pltpu.roll(field, 1, 1))
    total += jnp.where(
        cell == BLK - 1, jnp.where(block == nb - 1, 0.0, from_high), pltpu.roll(field, LANES - 1, 1)
    )
    total += jnp.where(azimuth == 0, 0.0, pltpu.roll(field, 1, 0))
    total += jnp.where(azimuth == ph - 1, 0.0, pltpu.roll(field, rows - 1, 0))
    zero = jnp.zeros((slab, LANES), jnp.float32)
    total += jnp.concatenate([zero, field[: rows - slab]], axis=0)
    total += jnp.concatenate([field[slab:], zero], axis=0)
    return field + mixed + conduct * (diagonal * field - total) - krylov


def sides(axis, taken, flags_ref):
    parity, has_low, has_high = {"ph": (0, None, None), "th": (2, 5, 6)}[axis]
    odd = flags_ref[parity : parity + 1, :] > 0.5
    first = taken[axis + "_low"][...]
    second = taken[axis + "_high"][...] if axis + "_high" in taken else jnp.zeros_like(first)
    low, high = jnp.where(odd, first, second), jnp.where(odd, second, first)
    if has_low is None:
        return low, high
    low = jnp.where(flags_ref[has_low : has_low + 1, :] > 0.5, low, 0.0)
    return low, jnp.where(flags_ref[has_high : has_high + 1, :] > 0.5, high, 0.0)


def take_azimuthal(out_ref, local_ref, conduct_ref, taken, flags_ref, ph):
    rows = out_ref.shape[0]
    low, high = sides("ph", taken, flags_ref)
    out_ref[...] = local_ref[...]
    for first, side in ((0, low), (ph - 1, high)):
        at = pl.ds(first, rows // ph, stride=ph)
        out_ref[at, :] = local_ref[at, :] - conduct_ref[at, :] * side


def split_slabs(th, th_n):
    if th_n > 2:
        return list(range(1, th - 1)), [0, th - 1]
    at = lax.axis_index("th")
    return [i + at for i in range(th - 1)], [(th - 1) * (1 - at)]


def groups_of(slabs, slab):
    return [
        pl.multiple_of(s * slab + i, 2 * GROUP) if not isinstance(s, int) else s * slab + i
        for s in slabs
        for i in range(0, slab, 2 * GROUP)
    ]


def first_kernel(ph, th, names, sizes, right_ref, conduct_ref, coupling_ref, codes_ref, inverse_ref, *rest):
    flags_ref, krylov_ref, conducts_ref, diagonal_ref, mixing_ref, held_ref, right, d_ref, *sent = rest[: 8 + len(names)]
    conduct, coupling, codes, turn, sems = rest[8 + len(names) :]
    rows = d_ref.shape[0]
    slab = rows // th
    pairs = [(right_ref, right), (coupling_ref, coupling), (codes_ref, codes), (conduct_ref, conduct)]
    parts = [pl.ds(t, th // 2) for t in range(0, th, th // 2)]
    pairs += [(inverse_ref.at[:, part], held_ref.at[:, part]) for part in parts]
    copies = [pltpu.make_async_copy(a, b, sems.at[i]) for i, (a, b) in enumerate(pairs)]
    for copy in copies:
        copy.start()

    def mix():
        copies[1].wait()
        lane = lax.broadcasted_iota(jnp.int32, (1, LANES), 1)
        for m in range(VARS):
            line = jnp.zeros((1, LANES), jnp.float32)
            for k in range(VARS):
                line = jnp.where(lane // BLK == k, coupling[k, (k + m) % VARS], line)
            mixing_ref[m : m + 1, :] = line

    def ghosts():
        copies[2].wait()
        cell = lax.broadcasted_iota(jnp.int32, (slab, LANES), 1) % BLK
        row = lax.broadcasted_iota(jnp.int32, (slab, LANES), 0)
        for t in range(th):
            diagonal = jnp.full((slab, LANES), 6.0, jnp.float32)
            for side, (edge, first, has) in enumerate(((0, 0, 3), (BLK - 1, slab - ph, 4))):
                factor = jnp.zeros((slab, LANES), jnp.float32)
                for p in range(ph):
                    code = codes[side, p, t]
                    value = jnp.where(code == 1, 1.0, jnp.where(code == 2, -1.0, 0.0))
                    factor = jnp.where(row == first + p, value, factor)
                diagonal -= jnp.where((cell == edge) & (flags_ref[has : has + 1, :] < 0.5), factor, 0.0)
            diagonal_ref[t * slab : (t + 1) * slab, :] = diagonal

    def lay_out():
        copies[3].wait()
        conducts_ref[...] = to_rows(conduct, turn)

    (row_at, row_n), (th_at, th_n), (ph_at, ph_n) = [(lax.axis_index(axis), n) for axis, n in sizes]
    values = [ph_at % 2, row_at % 2, th_at % 2, row_at > 0, row_at < row_n - 1, th_at > 0, th_at < th_n - 1]
    for i, value in enumerate(values):
        flags_ref[i : i + 1, :] = jnp.full((1, LANES), value.astype(jnp.float32))
    copies[0].wait()
    krylov_ref[...] = to_rows(right, turn)
    mix()
    ghosts()
    lay_out()
    for i, copy in enumerate(copies[4:]):
        copy.wait()
        for first in range(i * rows // 2, (i + 1) * rows // 2, 2 * GROUP):
            blocks = [held_ref[k % ph, k // slab, k % slab // ph] for k in range(first, first + 2 * GROUP)]
            d_ref[first : first + 2 * GROUP, :] = apply_stored(krylov_ref[first : first + 2 * GROUP, :], blocks)
    pack_faces(d_ref, dict(zip(names, sent)), flags_ref, ph, th)


def turn_kernel(held_ref, turned_ref):
    ph, th, nb = held_ref.shape[:3]
    for i in range(turned_ref.shape[0]):
        turned_ref[i] = held_ref[i % ph, i // (nb * ph), i % (nb * ph) // ph].T


def local_kernel(ph, th, count, krylov_ref, last_ref, conduct_ref, diagonal_ref, mixing_ref, *rest):
    fields, (out_ref, *natives), turns = rest[:count], rest[count : 2 * count + 1], rest[2 * count + 1 :]
    out_ref[...] = local_part(
        last_ref[...], krylov_ref[...], conduct_ref[...], diagonal_ref[...], mixing_ref, ph, th
    )
    for field_ref, native_ref, turn_ref in zip(fields, natives, turns):
        from_rows(field_ref[...], native_ref, turn_ref)


def gram_rows(left, right):
    lines = [jnp.sum(a * b, axis=0, keepdims=True) for a, b in zip(left, right)]
    return lines + [jnp.zeros_like(lines[0])] * (-len(lines) % 8)


def gram_kernel(*refs):
    basis = [ref[...] for ref in refs[:-1]]
    left = [basis[i] for i in range(S) for _ in range(i + 1)]
    right = [basis[j] for i in range(S) for j in range(i + 1)]
    refs[-1][...] = jnp.broadcast_to(in_lanes(gram_rows(left, right), 0), refs[-1].shape)


def in_lanes(lines, first):
    stacked = jnp.concatenate(lines, axis=0)
    each = jnp.sum(stacked, axis=1, keepdims=True)
    lane = lax.broadcasted_iota(jnp.int32, stacked.shape, 1)
    row = lax.broadcasted_iota(jnp.int32, stacked.shape, 0)
    return jnp.sum(jnp.where(lane == row + first, each, 0.0), axis=0, keepdims=True)


def early_kernel(ph, th, th_n, names, flags_ref, local_ref, conduct_ref, turned_ref, *rest):
    next_ref, d_ref = rest[len(names) :]
    take_azimuthal(next_ref, local_ref, conduct_ref, dict(zip(names, rest)), flags_ref, ph)
    early, late = split_slabs(th, th_n)
    slab = d_ref.shape[0] // th
    apply_turned(next_ref, turned_ref, d_ref, groups_of(early, slab))
    for first in groups_of(late, slab):
        d_ref[pl.ds(first, 2 * GROUP), :] = jnp.zeros((2 * GROUP, LANES), jnp.float32)


def late_kernel(ph, th, th_n, names, late_names, flags_ref, early_ref, part_ref, conduct_ref, turned_ref, *rest):
    n = len(late_names)
    next_ref, d_ref, *sent = rest[n:]
    next_ref[...] = early_ref[...]
    d_ref[...] = part_ref[...]
    rows = d_ref.shape[0]
    slab = rows // th
    low, high = sides("th", dict(zip(late_names, rest)), flags_ref)
    _, late = split_slabs(th, th_n)
    faces = [low, high] if th_n > 2 else [low + high]
    for s, face in zip(late, faces):
        at = pl.ds(pl.multiple_of(s * slab, 2 * GROUP) if not isinstance(s, int) else s * slab, slab)
        next_ref[at, :] = early_ref[at, :] - conduct_ref[at, :] * face
    apply_turned(next_ref, turned_ref, d_ref, groups_of(late, slab))
    pack_faces(d_ref, dict(zip(names, sent)), flags_ref, ph, th)


def last_kernel(ph, th, names, first, flags_ref, local_ref, conduct_ref, partial_ref, *rest):
    older, taken, (next_ref, gram_ref) = rest[:S], rest[S : S + len(names)], rest[S + len(names) :]
    taken = dict(zip(names, taken))
    take_azimuthal(next_ref, local_ref, conduct_ref, taken, flags_ref, ph)
    low, high = sides("th", taken, flags_ref)
    rows = next_ref.shape[0]
    slab = rows // th
    for at, side in ((pl.ds(0, slab), low), (pl.ds(rows - slab, slab), high)):
        next_ref[at, :] = next_ref[at, :] - conduct_ref[at, :] * side
    final = next_ref[...]
    basis = [ref[...] for ref in older] + [final]
    line = partial_ref[0:1, :] + in_lanes(gram_rows([final] * (S + 1), basis), first)
    gram_ref[...] = jnp.broadcast_to(line, gram_ref.shape)


def small_solve(products):
    def entry(i, j):
        return products[max(i, j)][min(i, j)]

    def normal(j, k):
        return (entry(j, k) + entry(j + 1, k + 1)) + (entry(j + 1, k) + entry(j, k + 1))

    matrix = [[normal(j, k) for k in range(j + 1)] for j in range(S)]
    moment = [entry(j, 0) + entry(j + 1, 0) for j in range(S)]
    inverse = []
    for j in range(S):
        inverse.append(1.0 / matrix[j][j])
        scaled = {i: matrix[i][j] * inverse[j] for i in range(j + 1, S)}
        for i in range(j + 1, S):
            for k in range(j + 1, i + 1):
                matrix[i][k] = matrix[i][k] - scaled[i] * matrix[k][j]
            moment[i] = moment[i] - scaled[i] * moment[j]
    weights = [None] * S
    for i in reversed(range(S)):
        summed = moment[i]
        for k in range(i + 1, S):
            summed = summed - matrix[k][i] * weights[k]
        weights[i] = summed * inverse[i]
    return weights


def combine_kernel(partial_rows, gram_ref, final_ref, *refs):
    krylov, directions, rest = refs[:S], refs[S : 2 * S], refs[2 * S :]
    correction_ref, residual_ref, correction, residual, newest, turn, sems = rest
    from_rows(final_ref[...], newest, turn)
    krylov = [*krylov, newest]
    line = jnp.sum(gram_ref[...], axis=0, keepdims=True)
    products, place = [], 0
    for i in range(S + 1):
        products.append([])
        place = partial_rows if i == S else place
        for j in range(i + 1):
            products[i].append(jnp.broadcast_to(line[:, place : place + 1], line.shape))
            place += 1
    weights = small_solve(products)
    weights = [weight[:, : correction.shape[-1]] for weight in weights]
    for v in range(correction.shape[0]):
        total = weights[0] * directions[0][v]
        left = krylov[0][v]
        for j in range(S):
            if j:
                total = total + weights[j] * directions[j][v]
            left = left - weights[j] * (krylov[j + 1][v] + krylov[j][v])
        correction[v] = total
        residual[v] = left
    copies = [
        pltpu.make_async_copy(correction, correction_ref, sems.at[0]),
        pltpu.make_async_copy(residual, residual_ref, sems.at[1]),
    ]
    for copy in copies:
        copy.start()
    for copy in copies:
        copy.wait()


def call(kernel, outs, scratch, *args, stay=()):
    def spec(a):
        return pl.BlockSpec(memory_space=pltpu.HBM if any(a is b for b in stay) else pltpu.VMEM)

    placed = [pltpu.with_memory_space_constraint(a, pltpu.HBM) if any(a is b for b in stay) else a for a in args]
    return pl.pallas_call(
        kernel,
        out_shape=outs,
        in_specs=[spec(a) for a in args],
        out_specs=[spec(a) for a in outs],
        scratch_shapes=scratch,
        compiler_params=pltpu.CompilerParams(vmem_limit_bytes=VMEM_LIMIT),
    )(*placed)


def local(right_side, conduct, coupling, inverse, face_codes):
    _, ph, th, radial = right_side.shape
    nb = radial // BLK
    per = ph * th
    rows = per * nb
    at = {axis: (lax.axis_index(axis), lax.axis_size(axis)) for axis in ("row", "th", "ph")}
    (row_at, row_n), (th_at, th_n), (ph_at, ph_n) = at["row"], at["th"], at["ph"]
    face_rows = {"ph_high": nb * th, "row_high": per, "ph_low": nb * th, "row_low": per // 2, "th_high": rows // th, "th_low": rows // th}
    if row_n == 2:
        face_rows.pop("row_high")
    if th_n == 2:
        face_rows.pop("th_high")
    names = tuple(face_rows)
    late_names = tuple(name for name in names if name[:2] == "th")
    packed = tuple(name for name in names if name != "row_low")
    early_names = tuple(name for name in names if name[:2] == "ph")
    radial_names = tuple(name for name in names if name[:3] == "row")
    def shape(n):
        return jax.ShapeDtypeStruct((n, LANES), jnp.float32)

    faces = [shape(face_rows[name]) for name in packed]
    whole = shape(rows)

    plans = {"low": pairs_low, "high": pairs_high}

    def exchange(sent, direction):
        (near,) = call(functools.partial(near_kernel, ph, th), [shape(face_rows["row_low"])], [], flags, direction)
        sent = dict(zip(packed, sent), row_low=near)
        taken = []
        for name in names:
            axis, side = name.split("_")
            taken.append(lax.ppermute(sent[name], axis, plans[side](lax.axis_size(axis))))
        return taken

    field = pltpu.VMEM(right_side.shape, jnp.float32)
    native = jax.ShapeDtypeStruct(right_side.shape, jnp.float32)
    turn = pltpu.VMEM((rows, LANES), jnp.float32)
    flags, start, conducts, diagonal, mixing, held, right_native, direction, *sent = call(
        functools.partial(first_kernel, ph, th, packed, (("row", row_n), ("th", th_n), ("ph", ph_n))),
        [shape(VARS), whole, whole, whole, shape(VARS), jax.ShapeDtypeStruct(inverse.shape, jnp.bfloat16), native, whole] + faces,
        [
            field,
            pltpu.SMEM(coupling.shape, jnp.float32),
            pltpu.SMEM(face_codes.shape, jnp.int32),
            turn,
            pltpu.SemaphoreType.DMA((6,)),
        ],
        right_side, conduct, coupling, face_codes, inverse,
        stay=(right_side, conduct, coupling, face_codes, inverse),
    )
    (turned,) = call(turn_kernel, [jax.ShapeDtypeStruct((rows, LANES, LANES), jnp.bfloat16)], [], held)
    krylov, directions = [start], [direction]
    krylov_native, direction_native = [right_native], []
    for step in range(S):
        taken = exchange(sent, directions[-1])
        ready = [] if step == 0 else [krylov[-1], directions[-1]] + directions[:1] * (step == 1)
        beside, *laid = call(
            functools.partial(local_kernel, ph, th, len(ready)),
            [whole] + [native] * len(ready),
            [turn] * len(ready),
            krylov[-1], directions[-1], conducts, diagonal, mixing, *ready,
        )
        if laid:
            krylov_native.append(laid[0])
            direction_native += laid[:0:-1]
        taken = dict(zip(names, taken))

        def of(some):
            return [taken[name] for name in some]

        (beside,) = call(
            functools.partial(radial_kernel, ph, th, radial_names), [whole], [], flags, beside, conducts, *of(radial_names)
        )
        if step < S - 1:
            early, part = call(
                functools.partial(early_kernel, ph, th, th_n, early_names),
                [whole, whole],
                [],
                flags, beside, conducts, turned, *of(early_names),
            )
            following, direction, *sent = call(
                functools.partial(late_kernel, ph, th, th_n, packed, late_names),
                [whole, whole] + faces,
                [],
                flags, early, part, conducts, turned, *of(late_names),
            )
            krylov.append(following)
            directions.append(direction)
    partial_rows = S * (S + 1) // 2
    partial_rows += -partial_rows % 8
    (partial,) = call(gram_kernel, [shape(GROUP)], [], *krylov)
    following, gram = call(
        functools.partial(last_kernel, ph, th, early_names + late_names, partial_rows),
        [whole, shape(row_n * th_n * ph_n)],
        [],
        flags, beside, conducts, partial, *krylov, *of(early_names + late_names),
    )
    krylov.append(following)
    gram = lax.all_to_all(gram, ("row", "th", "ph"), 0, 0, tiled=True)
    results = [native, jax.ShapeDtypeStruct(right_side.shape, jnp.float32)]
    return tuple(
        call(
            functools.partial(combine_kernel, partial_rows),
            results,
            [field, field, field, turn, pltpu.SemaphoreType.DMA((2,))],
            gram, following, *krylov_native, *direction_native,
            stay=results,
        )
    )


def solution(mesh):
    placed = (
        P(None, "ph", "th", "row"),
        P(None, "ph", "th", "row"),
        P(),
        P("ph", "th", "row", None, None),
        P(None, "ph", "th"),
    )
    return jax.shard_map(
        local,
        mesh=mesh,
        in_specs=placed,
        out_specs=(P(None, "ph", "th", "row"), P(None, "ph", "th", "row")),
        check_vma=False,
    )
```

```python
import functools

import jax
import jax.numpy as jnp
from jax import lax
from jax.experimental import pallas as pl
from jax.experimental.pallas import tpu as pltpu
from jax.sharding import PartitionSpec as P

VARS = 8
BLK = 16
S = 4
LANES = VARS * BLK
GROUP = 8
VMEM_LIMIT = 24 * 1024 * 1024


def pairs_low(count):
    return [(i, i ^ 1) for i in range(count)]


def pairs_high(count):
    return [(i, (i + 1) % count if i % 2 else (i - 1) % count) for i in range(count)]


def to_rows(native_ref, turn_ref):
    var, ph, th, radial = native_ref.shape
    planes = [jnp.concatenate([native_ref[v, p] for p in range(ph)], axis=0) for v in range(var)]
    for b in range(radial // BLK):
        turn_ref[b * ph * th : (b + 1) * ph * th, :] = jnp.concatenate(
            [plane[:, b * BLK : (b + 1) * BLK] for plane in planes], axis=1
        )
    slab = turn_ref.shape[0] // th
    return jnp.concatenate([turn_ref[pl.ds(t, slab, stride=th), :] for t in range(th)], axis=0)


def from_rows(rows, native_ref, turn_ref):
    var, ph, th, radial = native_ref.shape
    slab = rows.shape[0] // th
    for t in range(th):
        turn_ref[pl.ds(t, slab, stride=th), :] = rows[t * slab : (t + 1) * slab]
    turned = turn_ref[...]
    per = ph * th
    for v in range(var):
        plane = jnp.concatenate(
            [turned[b * per : (b + 1) * per, v * BLK : (v + 1) * BLK] for b in range(radial // BLK)], axis=1
        )
        for p in range(ph):
            native_ref[v, p] = plane[p * th : (p + 1) * th]


def spread_rows(vectors):
    rounded = vectors.astype(jnp.bfloat16)
    row = lax.broadcasted_iota(jnp.int32, rounded.shape, 0) % GROUP
    return jnp.concatenate(
        [jnp.where(row == m, rounded, jnp.zeros_like(rounded)) for m in range(GROUP)], axis=1
    )


def own_halves(out):
    return jnp.concatenate([out[:GROUP, :LANES], out[GROUP:, LANES:]], axis=0)


def apply_stored(vectors, blocks):
    halves = [jnp.concatenate(blocks[half * GROUP : (half + 1) * GROUP], axis=1) for half in range(2)]
    out = lax.dot_general(
        spread_rows(vectors),
        jnp.concatenate(halves, axis=0),
        (((1,), (1,)), ((), ())),
        preferred_element_type=jnp.float32,
    )
    return own_halves(out)


def apply_turned(field_ref, turned_ref, out_ref, firsts):
    for first in firsts:
        halves = [
            jnp.concatenate([turned_ref[first + half * GROUP + m] for m in range(GROUP)], axis=0) for half in range(2)
        ]
        out = jnp.dot(
            spread_rows(field_ref[pl.ds(first, 2 * GROUP), :]),
            jnp.concatenate(halves, axis=1),
            preferred_element_type=jnp.float32,
        )
        out_ref[pl.ds(first, 2 * GROUP), :] = own_halves(out)


def pack_faces(d_ref, outs, flags_ref, ph, th):
    rows = d_ref.shape[0]
    slab = rows // th
    odd_ph, odd_row, odd_th = [flags_ref[i : i + 1, :] > 0.5 for i in range(3)]
    low = d_ref[pl.ds(0, rows // ph, stride=ph), :]
    high = d_ref[pl.ds(ph - 1, rows // ph, stride=ph), :]
    outs["ph_high"][...] = jnp.where(odd_ph, high, low)
    outs["ph_low"][...] = jnp.where(odd_ph, low, high)
    if "row_high" in outs:
        for t in range(th):
            low, high = radial_edges(d_ref, t, slab, ph)
            outs["row_high"][t * ph : (t + 1) * ph, :] = jnp.where(odd_row, high, low)
    low, high = d_ref[:slab, :], d_ref[rows - slab :, :]
    outs["th_low"][...] = jnp.where(odd_th, low, high)
    if "th_high" in outs:
        outs["th_high"][...] = jnp.where(odd_th, high, low)


def radial_edges(d_ref, t, slab, ph):
    return d_ref[t * slab : t * slab + ph, :], d_ref[(t + 1) * slab - ph : (t + 1) * slab, :]


def near_kernel(ph, th, flags_ref, d_ref, out_ref):
    slab = d_ref.shape[0] // th
    half = out_ref.shape[0]
    low, high = [jnp.concatenate(side, axis=0) for side in zip(*[radial_edges(d_ref, t, slab, ph) for t in range(th)])]
    cell = lax.broadcasted_iota(jnp.int32, (half, LANES), 1) % BLK
    low = jnp.where(cell == BLK - 1, pltpu.roll(low[:half], BLK - 1, 1), 0.0) + jnp.where(
        cell == 0, pltpu.roll(low[half:], BLK, 1), 0.0
    )
    high = jnp.where(cell == 0, pltpu.roll(high[:half], LANES - BLK + 1, 1), 0.0) + jnp.where(
        cell == 1, pltpu.roll(high[half:], LANES - BLK + 2, 1), 0.0
    )
    out_ref[...] = jnp.where(flags_ref[1:2, :] > 0.5, low, high)


def radial_kernel(ph, th, names, flags_ref, local_ref, conduct_ref, *rest):
    taken, out_ref = dict(zip(names, rest)), rest[-1]
    slab = out_ref.shape[0] // th
    odd, has_low, has_high = [flags_ref[i : i + 1, :] > 0.5 for i in (1, 3, 4)]
    near = taken["row_low"][...]
    edge = lax.broadcasted_iota(jnp.int32, near.shape, 1) % BLK == jnp.where(odd, 0, BLK - 1)
    near = jnp.concatenate([jnp.where(edge, part, 0.0) for part in (near, pltpu.roll(near, LANES - 1, 1))], axis=0)
    below = above = jnp.zeros_like(near)
    if "row_high" in taken:
        face = taken["row_high"][...]
        cell = lax.broadcasted_iota(jnp.int32, face.shape, 1) % BLK
        below = jnp.where(cell == 0, pltpu.roll(face, LANES - BLK + 1, 1), 0.0)
        above = jnp.where(cell == BLK - 1, pltpu.roll(face, BLK - 1, 1), 0.0)
    low = jnp.where(has_low, jnp.where(odd, near, below), 0.0)
    high = jnp.where(has_high, jnp.where(odd, above, near), 0.0)
    out_ref[...] = local_ref[...]
    for t in range(th):
        for first, side in ((t * slab, low), ((t + 1) * slab - ph, high)):
            at = pl.ds(first, ph)
            out_ref[at, :] = local_ref[at, :] - conduct_ref[at, :] * side[t * ph : (t + 1) * ph]


def local_part(field, krylov, conduct, diagonal, mixing_ref, ph, th):
    rows = field.shape[0]
    slab = rows // th
    nb = slab // ph
    lane = lax.broadcasted_iota(jnp.int32, (rows, LANES), 1)
    row = lax.broadcasted_iota(jnp.int32, (rows, LANES), 0)
    cell = lane % BLK
    azimuth = row % ph
    block = (row // ph) % nb
    mixed = field * mixing_ref[0:1, :]
    for m in range(1, VARS):
        mixed += pltpu.roll(field, LANES - BLK * m, 1) * mixing_ref[m : m + 1, :]
    from_low = pltpu.roll(pltpu.roll(field, LANES - BLK + 1, 1), ph, 0)
    from_high = pltpu.roll(pltpu.roll(field, BLK - 1, 1), rows - ph, 0)
    total = jnp.where(cell == 0, jnp.where(block == 0, 0.0, from_low), pltpu.roll(field, 1, 1))
    total += jnp.where(
        cell == BLK - 1, jnp.where(block == nb - 1, 0.0, from_high), pltpu.roll(field, LANES - 1, 1)
    )
    total += jnp.where(azimuth == 0, 0.0, pltpu.roll(field, 1, 0))
    total += jnp.where(azimuth == ph - 1, 0.0, pltpu.roll(field, rows - 1, 0))
    zero = jnp.zeros((slab, LANES), jnp.float32)
    total += jnp.concatenate([zero, field[: rows - slab]], axis=0)
    total += jnp.concatenate([field[slab:], zero], axis=0)
    return field + mixed + conduct * (diagonal * field - total) - krylov


def sides(axis, taken, flags_ref):
    parity, has_low, has_high = {"ph": (0, None, None), "th": (2, 5, 6)}[axis]
    odd = flags_ref[parity : parity + 1, :] > 0.5
    first = taken[axis + "_low"][...]
    second = taken[axis + "_high"][...] if axis + "_high" in taken else jnp.zeros_like(first)
    low, high = jnp.where(odd, first, second), jnp.where(odd, second, first)
    if has_low is None:
        return low, high
    low = jnp.where(flags_ref[has_low : has_low + 1, :] > 0.5, low, 0.0)
    return low, jnp.where(flags_ref[has_high : has_high + 1, :] > 0.5, high, 0.0)


def take_azimuthal(out_ref, local_ref, conduct_ref, taken, flags_ref, ph):
    rows = out_ref.shape[0]
    low, high = sides("ph", taken, flags_ref)
    out_ref[...] = local_ref[...]
    for first, side in ((0, low), (ph - 1, high)):
        at = pl.ds(first, rows // ph, stride=ph)
        out_ref[at, :] = local_ref[at, :] - conduct_ref[at, :] * side


def split_slabs(th, th_n):
    if th_n > 2:
        return list(range(1, th - 1)), [0, th - 1]
    at = lax.axis_index("th")
    return [i + at for i in range(th - 1)], [(th - 1) * (1 - at)]


def groups_of(slabs, slab):
    return [
        pl.multiple_of(s * slab + i, 2 * GROUP) if not isinstance(s, int) else s * slab + i
        for s in slabs
        for i in range(0, slab, 2 * GROUP)
    ]


def first_kernel(ph, th, names, sizes, right_ref, conduct_ref, coupling_ref, codes_ref, inverse_ref, *rest):
    flags_ref, krylov_ref, conducts_ref, diagonal_ref, mixing_ref, held_ref, right, d_ref, *sent = rest[: 8 + len(names)]
    conduct, coupling, codes, turn, sems = rest[8 + len(names) :]
    rows = d_ref.shape[0]
    slab = rows // th
    pairs = [(right_ref, right), (coupling_ref, coupling), (codes_ref, codes), (conduct_ref, conduct)]
    parts = [pl.ds(t, th // 2) for t in range(0, th, th // 2)]
    pairs += [(inverse_ref.at[:, part], held_ref.at[:, part]) for part in parts]
    copies = [pltpu.make_async_copy(a, b, sems.at[i]) for i, (a, b) in enumerate(pairs)]
    for copy in copies:
        copy.start()

    def mix():
        copies[1].wait()
        lane = lax.broadcasted_iota(jnp.int32, (1, LANES), 1)
        for m in range(VARS):
            line = jnp.zeros((1, LANES), jnp.float32)
            for k in range(VARS):
                line = jnp.where(lane // BLK == k, coupling[k, (k + m) % VARS], line)
            mixing_ref[m : m + 1, :] = line

    def ghosts():
        copies[2].wait()
        cell = lax.broadcasted_iota(jnp.int32, (slab, LANES), 1) % BLK
        row = lax.broadcasted_iota(jnp.int32, (slab, LANES), 0)
        for t in range(th):
            diagonal = jnp.full((slab, LANES), 6.0, jnp.float32)
            for side, (edge, first, has) in enumerate(((0, 0, 3), (BLK - 1, slab - ph, 4))):
                factor = jnp.zeros((slab, LANES), jnp.float32)
                for p in range(ph):
                    code = codes[side, p, t]
                    value = jnp.where(code == 1, 1.0, jnp.where(code == 2, -1.0, 0.0))
                    factor = jnp.where(row == first + p, value, factor)
                diagonal -= jnp.where((cell == edge) & (flags_ref[has : has + 1, :] < 0.5), factor, 0.0)
            diagonal_ref[t * slab : (t + 1) * slab, :] = diagonal

    def lay_out():
        copies[3].wait()
        conducts_ref[...] = to_rows(conduct, turn)

    (row_at, row_n), (th_at, th_n), (ph_at, ph_n) = [(lax.axis_index(axis), n) for axis, n in sizes]
    values = [ph_at % 2, row_at % 2, th_at % 2, row_at > 0, row_at < row_n - 1, th_at > 0, th_at < th_n - 1]
    for i, value in enumerate(values):
        flags_ref[i : i + 1, :] = jnp.full((1, LANES), value.astype(jnp.float32))
    copies[0].wait()
    krylov_ref[...] = to_rows(right, turn)
    mix()
    ghosts()
    lay_out()
    for i, copy in enumerate(copies[4:]):
        copy.wait()
        for first in range(i * rows // 2, (i + 1) * rows // 2, 2 * GROUP):
            blocks = [held_ref[k % ph, k // slab, k % slab // ph] for k in range(first, first + 2 * GROUP)]
            d_ref[first : first + 2 * GROUP, :] = apply_stored(krylov_ref[first : first + 2 * GROUP, :], blocks)
    pack_faces(d_ref, dict(zip(names, sent)), flags_ref, ph, th)


def turn_kernel(held_ref, turned_ref):
    ph, th, nb = held_ref.shape[:3]
    for i in range(turned_ref.shape[0]):
        turned_ref[i] = held_ref[i % ph, i // (nb * ph), i % (nb * ph) // ph].T


def local_kernel(ph, th, count, krylov_ref, last_ref, conduct_ref, diagonal_ref, mixing_ref, *rest):
    fields, (out_ref, *natives), turns = rest[:count], rest[count : 2 * count + 1], rest[2 * count + 1 :]
    out_ref[...] = local_part(
        last_ref[...], krylov_ref[...], conduct_ref[...], diagonal_ref[...], mixing_ref, ph, th
    )
    for field_ref, native_ref, turn_ref in zip(fields, natives, turns):
        from_rows(field_ref[...], native_ref, turn_ref)


def gram_rows(left, right):
    lines = [jnp.sum(a * b, axis=0, keepdims=True) for a, b in zip(left, right)]
    return lines + [jnp.zeros_like(lines[0])] * (-len(lines) % 8)


def gram_kernel(*refs):
    basis = [ref[...] for ref in refs[:-1]]
    left = [basis[i] for i in range(S) for _ in range(i + 1)]
    right = [basis[j] for i in range(S) for j in range(i + 1)]
    refs[-1][...] = jnp.broadcast_to(in_lanes(gram_rows(left, right), 0), refs[-1].shape)


def in_lanes(lines, first):
    stacked = jnp.concatenate(lines, axis=0)
    each = jnp.sum(stacked, axis=1, keepdims=True)
    lane = lax.broadcasted_iota(jnp.int32, stacked.shape, 1)
    row = lax.broadcasted_iota(jnp.int32, stacked.shape, 0)
    return jnp.sum(jnp.where(lane == row + first, each, 0.0), axis=0, keepdims=True)


def early_kernel(ph, th, th_n, names, flags_ref, local_ref, conduct_ref, turned_ref, *rest):
    next_ref, d_ref = rest[len(names) :]
    take_azimuthal(next_ref, local_ref, conduct_ref, dict(zip(names, rest)), flags_ref, ph)
    early, late = split_slabs(th, th_n)
    slab = d_ref.shape[0] // th
    apply_turned(next_ref, turned_ref, d_ref, groups_of(early, slab))
    for first in groups_of(late, slab):
        d_ref[pl.ds(first, 2 * GROUP), :] = jnp.zeros((2 * GROUP, LANES), jnp.float32)


def late_kernel(ph, th, th_n, names, late_names, flags_ref, early_ref, part_ref, conduct_ref, turned_ref, *rest):
    n = len(late_names)
    next_ref, d_ref, *sent = rest[n:]
    next_ref[...] = early_ref[...]
    d_ref[...] = part_ref[...]
    rows = d_ref.shape[0]
    slab = rows // th
    low, high = sides("th", dict(zip(late_names, rest)), flags_ref)
    _, late = split_slabs(th, th_n)
    faces = [low, high] if th_n > 2 else [low + high]
    for s, face in zip(late, faces):
        at = pl.ds(pl.multiple_of(s * slab, 2 * GROUP) if not isinstance(s, int) else s * slab, slab)
        next_ref[at, :] = early_ref[at, :] - conduct_ref[at, :] * face
    apply_turned(next_ref, turned_ref, d_ref, groups_of(late, slab))
    pack_faces(d_ref, dict(zip(names, sent)), flags_ref, ph, th)


def last_kernel(ph, th, names, first, flags_ref, local_ref, conduct_ref, partial_ref, *rest):
    older, taken, (next_ref, gram_ref) = rest[:S], rest[S : S + len(names)], rest[S + len(names) :]
    taken = dict(zip(names, taken))
    take_azimuthal(next_ref, local_ref, conduct_ref, taken, flags_ref, ph)
    low, high = sides("th", taken, flags_ref)
    rows = next_ref.shape[0]
    slab = rows // th
    for at, side in ((pl.ds(0, slab), low), (pl.ds(rows - slab, slab), high)):
        next_ref[at, :] = next_ref[at, :] - conduct_ref[at, :] * side
    final = next_ref[...]
    basis = [ref[...] for ref in older] + [final]
    line = partial_ref[0:1, :] + in_lanes(gram_rows([final] * (S + 1), basis), first)
    gram_ref[...] = jnp.broadcast_to(line, gram_ref.shape)


def small_solve(products):
    def entry(i, j):
        return products[max(i, j)][min(i, j)]

    def normal(j, k):
        return (entry(j, k) + entry(j + 1, k + 1)) + (entry(j + 1, k) + entry(j, k + 1))

    matrix = [[normal(j, k) for k in range(j + 1)] for j in range(S)]
    moment = [entry(j, 0) + entry(j + 1, 0) for j in range(S)]
    inverse = []
    for j in range(S):
        inverse.append(1.0 / matrix[j][j])
        scaled = {i: matrix[i][j] * inverse[j] for i in range(j + 1, S)}
        for i in range(j + 1, S):
            for k in range(j + 1, i + 1):
                matrix[i][k] = matrix[i][k] - scaled[i] * matrix[k][j]
            moment[i] = moment[i] - scaled[i] * moment[j]
    weights = [None] * S
    for i in reversed(range(S)):
        summed = moment[i]
        for k in range(i + 1, S):
            summed = summed - matrix[k][i] * weights[k]
        weights[i] = summed * inverse[i]
    return weights


def combine_kernel(partial_rows, gram_ref, final_ref, *refs):
    krylov, directions, rest = refs[:S], refs[S : 2 * S], refs[2 * S :]
    correction_ref, residual_ref, correction, residual, newest, turn, sems = rest
    from_rows(final_ref[...], newest, turn)
    krylov = [*krylov, newest]
    line = jnp.sum(gram_ref[...], axis=0, keepdims=True)
    products, place = [], 0
    for i in range(S + 1):
        products.append([])
        place = partial_rows if i == S else place
        for j in range(i + 1):
            products[i].append(jnp.broadcast_to(line[:, place : place + 1], line.shape))
            place += 1
    weights = small_solve(products)
    weights = [weight[:, : correction.shape[-1]] for weight in weights]
    for v in range(correction.shape[0]):
        total = weights[0] * directions[0][v]
        left = krylov[0][v]
        for j in range(S):
            if j:
                total = total + weights[j] * directions[j][v]
            left = left - weights[j] * (krylov[j + 1][v] + krylov[j][v])
        correction[v] = total
        residual[v] = left
    copies = [
        pltpu.make_async_copy(correction, correction_ref, sems.at[0]),
        pltpu.make_async_copy(residual, residual_ref, sems.at[1]),
    ]
    for copy in copies:
        copy.start()
    for copy in copies:
        copy.wait()


def call(kernel, outs, scratch, *args, stay=()):
    def spec(a):
        return pl.BlockSpec(memory_space=pltpu.HBM if any(a is b for b in stay) else pltpu.VMEM)

    placed = [pltpu.with_memory_space_constraint(a, pltpu.HBM) if any(a is b for b in stay) else a for a in args]
    return pl.pallas_call(
        kernel,
        out_shape=outs,
        in_specs=[spec(a) for a in args],
        out_specs=[spec(a) for a in outs],
        scratch_shapes=scratch,
        compiler_params=pltpu.CompilerParams(vmem_limit_bytes=VMEM_LIMIT),
    )(*placed)


def local(right_side, conduct, coupling, inverse, face_codes):
    _, ph, th, radial = right_side.shape
    nb = radial // BLK
    per = ph * th
    rows = per * nb
    at = {axis: (lax.axis_index(axis), lax.axis_size(axis)) for axis in ("row", "th", "ph")}
    (row_at, row_n), (th_at, th_n), (ph_at, ph_n) = at["row"], at["th"], at["ph"]
    face_rows = {"ph_low": nb * th, "row_high": per, "ph_high": nb * th, "row_low": per // 2, "th_high": rows // th, "th_low": rows // th}
    if row_n == 2:
        face_rows.pop("row_high")
    if th_n == 2:
        face_rows.pop("th_high")
    names = tuple(face_rows)
    late_names = tuple(name for name in names if name[:2] == "th")
    packed = tuple(name for name in names if name != "row_low")
    early_names = tuple(name for name in names if name[:2] == "ph")
    radial_names = tuple(name for name in names if name[:3] == "row")
    def shape(n):
        return jax.ShapeDtypeStruct((n, LANES), jnp.float32)

    faces = [shape(face_rows[name]) for name in packed]
    whole = shape(rows)

    plans = {"low": pairs_low, "high": pairs_high}

    def exchange(sent, direction):
        (near,) = call(functools.partial(near_kernel, ph, th), [shape(face_rows["row_low"])], [], flags, direction)
        sent = dict(zip(packed, sent), row_low=near)
        taken = []
        for name in names:
            axis, side = name.split("_")
            taken.append(lax.ppermute(sent[name], axis, plans[side](lax.axis_size(axis))))
        return taken

    field = pltpu.VMEM(right_side.shape, jnp.float32)
    native = jax.ShapeDtypeStruct(right_side.shape, jnp.float32)
    turn = pltpu.VMEM((rows, LANES), jnp.float32)
    flags, start, conducts, diagonal, mixing, held, right_native, direction, *sent = call(
        functools.partial(first_kernel, ph, th, packed, (("row", row_n), ("th", th_n), ("ph", ph_n))),
        [shape(VARS), whole, whole, whole, shape(VARS), jax.ShapeDtypeStruct(inverse.shape, jnp.bfloat16), native, whole] + faces,
        [
            field,
            pltpu.SMEM(coupling.shape, jnp.float32),
            pltpu.SMEM(face_codes.shape, jnp.int32),
            turn,
            pltpu.SemaphoreType.DMA((6,)),
        ],
        right_side, conduct, coupling, face_codes, inverse,
        stay=(right_side, conduct, coupling, face_codes, inverse),
    )
    (turned,) = call(turn_kernel, [jax.ShapeDtypeStruct((rows, LANES, LANES), jnp.bfloat16)], [], held)
    krylov, directions = [start], [direction]
    krylov_native, direction_native = [right_native], []
    for step in range(S):
        taken = exchange(sent, directions[-1])
        ready = [] if step == 0 else [krylov[-1], directions[-1]] + directions[:1] * (step == 1)
        beside, *laid = call(
            functools.partial(local_kernel, ph, th, len(ready)),
            [whole] + [native] * len(ready),
            [turn] * len(ready),
            krylov[-1], directions[-1], conducts, diagonal, mixing, *ready,
        )
        if laid:
            krylov_native.append(laid[0])
            direction_native += laid[:0:-1]
        taken = dict(zip(names, taken))

        def of(some):
            return [taken[name] for name in some]

        (beside,) = call(
            functools.partial(radial_kernel, ph, th, radial_names), [whole], [], flags, beside, conducts, *of(radial_names)
        )
        if step < S - 1:
            early, part = call(
                functools.partial(early_kernel, ph, th, th_n, early_names),
                [whole, whole],
                [],
                flags, beside, conducts, turned, *of(early_names),
            )
            following, direction, *sent = call(
                functools.partial(late_kernel, ph, th, th_n, packed, late_names),
                [whole, whole] + faces,
                [],
                flags, early, part, conducts, turned, *of(late_names),
            )
            krylov.append(following)
            directions.append(direction)
    partial_rows = S * (S + 1) // 2
    partial_rows += -partial_rows % 8
    (partial,) = call(gram_kernel, [shape(GROUP)], [], *krylov)
    following, gram = call(
        functools.partial(last_kernel, ph, th, early_names + late_names, partial_rows),
        [whole, shape(row_n * th_n * ph_n)],
        [],
        flags, beside, conducts, partial, *krylov, *of(early_names + late_names),
    )
    krylov.append(following)
    gram = lax.all_to_all(gram, ("row", "th", "ph"), 0, 0, tiled=True)
    results = [native, jax.ShapeDtypeStruct(right_side.shape, jnp.float32)]
    return tuple(
        call(
            functools.partial(combine_kernel, partial_rows),
            results,
            [field, field, field, turn, pltpu.SemaphoreType.DMA((2,))],
            gram, following, *krylov_native, *direction_native,
            stay=results,
        )
    )


def solution(mesh):
    placed = (
        P(None, "ph", "th", "row"),
        P(None, "ph", "th", "row"),
        P(),
        P("ph", "th", "row", None, None),
        P(None, "ph", "th"),
    )
    return jax.shard_map(
        local,
        mesh=mesh,
        in_specs=placed,
        out_specs=(P(None, "ph", "th", "row"), P(None, "ph", "th", "row")),
        check_vma=False,
    )
```
